128 devices in a mesh: ctx: 8 (over z_lo, x), fsdp: 16 (over y, z_hi, core).
Axes of the slice: x: 4, y: 4, z: 4 (z_hi: 2, z_lo: 2; z = z_hi * 2 + z_lo), core: 2. Of those that a mesh axis runs over, the one named last changes fastest.
Arguments:
- inputs: bfloat16 [16, 1024, 1152], P('fsdp', 'ctx'), may hold values from -6 to 6
- pair_order: int32 [16, 8], P('fsdp'), may hold values from 0 to 7, each once within a row
- attn_gain: bfloat16 [1152], P(('ctx', 'fsdp')), may hold values from 0.099609375 to 1.8984375
- query_gain: bfloat16 [256], P(('ctx', 'fsdp')), may hold values from 0.099609375 to 1.8984375
- key_gain: bfloat16 [256], P(('ctx', 'fsdp')), may hold values from 0.099609375 to 1.8984375
- mixer_gain: bfloat16 [1152], P(('ctx', 'fsdp')), may hold values from 0.099609375 to 1.8984375
- ffn_gain: bfloat16 [1152], P(('ctx', 'fsdp')), may hold values from 0.099609375 to 1.8984375
- branch_gain: bfloat16 [1152], P(('ctx', 'fsdp')), may hold values from 0.099609375 to 1.8984375
- query_weight: bfloat16 [1152, 1024], P(('ctx', 'fsdp')), may hold values from -0.1875 to 0.1875
- key_weight: bfloat16 [1152, 256], P(('ctx', 'fsdp')), may hold values from -0.1875 to 0.1875
- value_weight: bfloat16 [1152, 256], P(('ctx', 'fsdp')), may hold values from -0.1875 to 0.1875
- output_weight: bfloat16 [1024, 1152], P(('ctx', 'fsdp')), may hold values from -0.1875 to 0.1875
- gate_weight: bfloat16 [1152, 6912], P('ctx', 'fsdp'), may hold values from -0.1875 to 0.1875
- up_weight: bfloat16 [1152, 6912], P('ctx', 'fsdp'), may hold values from -0.1875 to 0.1875
- down_weight: bfloat16 [6912, 1152], P('fsdp', 'ctx'), may hold values from -0.078125 to 0.078125
- cotangent: bfloat16 [16, 1024, 1152], P('fsdp', 'ctx'), may hold values from -6 to 6
Outputs:
- outputs: float32 [16, 1024, 1152], P('fsdp', 'ctx')
- inputs_grad: float32 [16, 1024, 1152], P('fsdp', 'ctx')
- attn_gain_grad: float32 [1152], P(('ctx', 'fsdp'))
- query_gain_grad: float32 [256], P(('ctx', 'fsdp'))
- key_gain_grad: float32 [256], P(('ctx', 'fsdp'))
- mixer_gain_grad: float32 [1152], P(('ctx', 'fsdp'))
- ffn_gain_grad: float32 [1152], P(('ctx', 'fsdp'))
- branch_gain_grad: float32 [1152], P(('ctx', 'fsdp'))
- query_weight_grad: float32 [1152, 1024], P(('ctx', 'fsdp'))
- key_weight_grad: float32 [1152, 256], P(('ctx', 'fsdp'))
- value_weight_grad: float32 [1152, 256], P(('ctx', 'fsdp'))
- output_weight_grad: float32 [1024, 1152], P(('ctx', 'fsdp'))
- gate_weight_grad: float32 [1152, 6912], P('ctx', 'fsdp')
- up_weight_grad: float32 [1152, 6912], P('ctx', 'fsdp')
- down_weight_grad: float32 [6912, 1152], P('fsdp', 'ctx')
The draws below stay inside these ranges and needn't reach their ends.
Inputs may be any that keep to these rules, and one draw needn't show every extreme that they name: Each row of pair_order names every number of 0 to 7 once.
All inputs are finite; a program needn't handle non-finite values.
Results may differ from the reference program's by a relative error of at most 0.04.
Values may be sent and summed in bfloat16 or wider, within the bound.
A program may use at most 128 MiB of HBM per device.

```python
import jax
import jax.numpy as jnp
from jax import lax

D = 1152
HEADS = 4
HEAD_DIM = 256
FF = 6912
LENGTH = 1024
SEQS = 16
N_CTX = 8


def shard_levels(own_key, shape, pieces, least, largest):
    factor_of, own = 1.0, jax.random.fold_in(own_key, 6)
    for position, blocks in pieces:
        draws = jnp.exp(jax.random.uniform(jax.random.fold_in(own, position), (blocks,), jnp.float32, least / len(pieces), largest / len(pieces)))
        factor_of = factor_of * jnp.repeat(draws, shape[position] // blocks).reshape([-1 if axis == position else 1 for axis in range(len(shape))])
    return factor_of


def centred(rng, shape, scale, bound, split=(), kind=jnp.bfloat16):
    loudness = shard_levels(rng, shape, split, -0.22, 0.18) if split else 1.0
    drawn = jax.random.normal(rng, shape, jnp.float32) * scale * loudness
    return jnp.minimum(jnp.maximum(drawn, -bound), bound).astype(kind)


def setup_inputs(seed: int = 0) -> dict:
    key_of = jax.random.split(jax.random.key(seed), 17)
    inputs = centred(key_of[0], (SEQS, LENGTH, D), 1.0, 6.0, ((0, 16), (1, 8)))
    pair_order = jax.vmap(lambda own: jax.random.permutation(own, N_CTX))(jax.random.split(key_of[1], SEQS)).reshape((SEQS, N_CTX)).astype(jnp.int32)
    attn_gain = jnp.clip(1.0 + 0.18 * jax.random.normal(key_of[2], (D,), jnp.float32), 0.099609375, 1.8984375).astype(jnp.bfloat16)
    query_gain = jnp.clip(1.0 + 0.18 * jax.random.normal(key_of[3], (HEAD_DIM,), jnp.float32), 0.099609375, 1.8984375).astype(jnp.bfloat16)
    key_gain = jnp.clip(1.0 + 0.18 * jax.random.normal(key_of[4], (HEAD_DIM,), jnp.float32), 0.099609375, 1.8984375).astype(jnp.bfloat16)
    mixer_gain = jnp.clip(1.0 + 0.18 * jax.random.normal(key_of[5], (D,), jnp.float32), 0.099609375, 1.8984375).astype(jnp.bfloat16)
    ffn_gain = jnp.clip(1.0 + 0.18 * jax.random.normal(key_of[6], (D,), jnp.float32), 0.099609375, 1.8984375).astype(jnp.bfloat16)
    branch_gain = jnp.clip(1.0 + 0.18 * jax.random.normal(key_of[7], (D,), jnp.float32), 0.099609375, 1.8984375).astype(jnp.bfloat16)
    query_weight = centred(key_of[8], (D, HEADS * HEAD_DIM), D ** -0.5, 0.1875, ((0, 128),))
    key_weight = centred(key_of[9], (D, HEAD_DIM), D ** -0.5, 0.1875, ((0, 128),))
    value_weight = centred(key_of[10], (D, HEAD_DIM), D ** -0.5, 0.1875, ((0, 128),))
    output_weight = centred(key_of[11], (HEADS * HEAD_DIM, D), (HEADS * HEAD_DIM) ** -0.5, 0.1875, ((0, 128),))
    gate_weight = centred(key_of[12], (D, FF), D ** -0.5, 0.1875, ((0, 8), (1, 16)))
    up_weight = centred(key_of[13], (D, FF), D ** -0.5, 0.1875, ((0, 8), (1, 16)))
    down_weight = centred(key_of[14], (FF, D), FF ** -0.5, 0.078125, ((0, 16), (1, 8)))
    cotangent = centred(key_of[15], (SEQS, LENGTH, D), 1.0, 6.0, ((0, 16), (1, 8)))
    return {"inputs": inputs, "pair_order": pair_order, "attn_gain": attn_gain, "query_gain": query_gain, "key_gain": key_gain, "mixer_gain": mixer_gain, "ffn_gain": ffn_gain, "branch_gain": branch_gain, "query_weight": query_weight, "key_weight": key_weight, "value_weight": value_weight, "output_weight": output_weight, "gate_weight": gate_weight, "up_weight": up_weight, "down_weight": down_weight, "cotangent": cotangent}


EPS = 1e-06
SCALE = 0.0625
BASE = 1000000.0
MASKED = -1e+30
HIGH = lax.Precision.HIGHEST

@jax.custom_vjp
def low(v):
    return lax.optimization_barrier(v.astype(jnp.bfloat16)).astype(jnp.float32)

@jax.custom_vjp
def low_back(v):
    return v

def low_keep(v):
    return (low(v), None)

def low_pass(kept, grad):
    return (grad,)

def back_keep(v):
    return (v, None)

def back_low(kept, grad):
    return (low(grad),)
low.defvjp(low_keep, low_pass)
low_back.defvjp(back_keep, back_low)

def rms_norm(values, gain):
    return values * lax.rsqrt(lax.optimization_barrier(jnp.mean(values * values, axis=-1, keepdims=True)) + EPS) * gain

def rotary(values, cosines, sines):
    half = values.shape[-1] // 2
    first = values[..., :half]
    second = values[..., half:]
    return jnp.concatenate([first * cosines - second * sines, second * cosines + first * sines], axis=-1)

def angles(positions, width):
    half = width // 2
    freqs = BASE ** (-jnp.arange(half, dtype=jnp.float32) / half)
    return positions.astype(jnp.float32)[:, None] * freqs[None, :]

def token_positions(pairs, tok_rows):
    half = tok_rows // 2
    index = jnp.arange(tok_rows, dtype=jnp.int32)
    count = 2 * pairs.shape[0]
    blocks = jnp.where(index[None, :] < half, pairs[:, None], count - 1 - pairs[:, None])
    return (blocks * half + index[None, :] % half).astype(jnp.int32)

def mat_high(left, right):
    return jnp.dot(left, right, precision=HIGH)

def layer(params, hidden_in, positions):
    attn_gain, query_gain, key_gain, mixer_gain, ffn_gain, branch_gain, query_weight, key_weight, value_weight, output_weight, gate_weight, up_weight, down_weight = params
    length = hidden_in.shape[0]
    head_dim = key_weight.shape[1]
    heads = query_weight.shape[1] // head_dim
    angle = angles(positions, head_dim)
    cosines = jnp.cos(angle)
    sines = jnp.sin(angle)
    attn_in = low(rms_norm(hidden_in, attn_gain))
    queries_raw = low_back(mat_high(attn_in, query_weight)).reshape(length, heads, head_dim)
    keys_raw = low_back(mat_high(attn_in, key_weight))
    values = low(low_back(mat_high(attn_in, value_weight)))
    query_rot = low(rotary(rms_norm(queries_raw, query_gain), cosines[:, None, :], sines[:, None, :]))
    key_rot = low(rotary(rms_norm(keys_raw, key_gain), cosines, sines))
    scores = low_back(jnp.einsum('thd,kd->htk', query_rot, key_rot, precision=HIGH) * SCALE)
    causal = positions[None, :] <= positions[:, None]
    scores = jnp.where(causal[None], scores, MASKED)
    peak = lax.optimization_barrier(jnp.max(scores, axis=-1, keepdims=True))
    expo = jnp.exp(scores - peak)
    probs = low(expo / lax.optimization_barrier(jnp.sum(expo, axis=-1, keepdims=True)))
    mixed = low(low_back(jnp.einsum('htk,kd->thd', probs, values, precision=HIGH).reshape(length, heads * head_dim)))
    attn_out = low_back(mat_high(mixed, output_weight))
    resid = hidden_in + rms_norm(attn_out, mixer_gain)
    ffn_in = low(rms_norm(resid, ffn_gain))
    gate = low_back(mat_high(ffn_in, gate_weight))
    upper = low_back(mat_high(ffn_in, up_weight))
    hidden = low(jax.nn.gelu(gate, approximate=True) * upper)
    branch = low_back(mat_high(hidden, down_weight))
    return resid + rms_norm(branch, branch_gain)

def reference(inputs, pair_order, attn_gain, query_gain, key_gain, mixer_gain, ffn_gain, branch_gain, query_weight, key_weight, value_weight, output_weight, gate_weight, up_weight, down_weight, cotangent):
    params = (attn_gain.astype(jnp.float32), query_gain.astype(jnp.float32), key_gain.astype(jnp.float32), mixer_gain.astype(jnp.float32), ffn_gain.astype(jnp.float32), branch_gain.astype(jnp.float32), query_weight.astype(jnp.float32), key_weight.astype(jnp.float32), value_weight.astype(jnp.float32), output_weight.astype(jnp.float32), gate_weight.astype(jnp.float32), up_weight.astype(jnp.float32), down_weight.astype(jnp.float32))
    hidden_all = inputs.astype(jnp.float32)
    upstream = cotangent.astype(jnp.float32)
    tok_rows = LENGTH // N_CTX
    positions = jax.vmap(lambda row: token_positions(row, tok_rows).reshape(-1))(pair_order)

    def forward(weights, hidden_seqs):

        def one_seq(pair):
            return layer(weights, pair[0], pair[1])
        return lax.map(jax.checkpoint(one_seq), (hidden_seqs, positions))
    result, backward = jax.vjp(forward, params, hidden_all)
    grads, inputs_grad = backward(upstream)
    return (result, inputs_grad, grads[0], grads[1], grads[2], grads[3], grads[4], grads[5], grads[6], grads[7], grads[8], grads[9], grads[10], grads[11], grads[12])
```

```python
from functools import partial

import jax
import jax.numpy as jnp
from jax import lax
from jax.experimental import pallas as pl
from jax.experimental.pallas import tpu as pltpu
from jax.sharding import PartitionSpec as P

EPS = 1e-06
SCALE = 0.0625
BASE = 1000000.0
MASKED = -1e30
BF16 = jnp.bfloat16
F32 = jnp.float32
VMEM_BYTES = 56 * 1024 * 1024


def rms_norm(values, gain):
    return values * lax.rsqrt(jnp.mean(values * values, axis=-1, keepdims=True) + EPS) * gain


def rotary(values, cosines, sines):
    half = values.shape[-1] // 2
    first = values[..., :half]
    second = values[..., half:]
    return jnp.concatenate(
        [first * cosines - second * sines, second * cosines + first * sines], axis=-1
    )


def angles(positions, width):
    half = width // 2
    freqs = BASE ** (-jnp.arange(half, dtype=jnp.float32) / half)
    return positions.astype(jnp.float32)[:, None] * freqs[None, :]


def token_positions(pairs, tok_rows):
    half = tok_rows // 2
    index = jnp.arange(tok_rows, dtype=jnp.int32)
    count = 2 * pairs.shape[0]
    blocks = jnp.where(index[None, :] < half, pairs[:, None], count - 1 - pairs[:, None])
    return blocks * half + index[None, :] % half


def matmul(left, right):
    return jnp.dot(left, right, preferred_element_type=jnp.float32)


def matmul_tn(left, right):
    return lax.dot_general(
        left, right, (((0,), (0,)), ((), ())), preferred_element_type=jnp.float32
    )


def matmul_nt(left, right):
    return lax.dot_general(
        left, right, (((1,), (1,)), ((), ())), preferred_element_type=jnp.float32
    )


def score_block(query_low, key_all, causal):
    scores = (
        jnp.einsum("thd,kd->htk", query_low, key_all, preferred_element_type=jnp.float32) * SCALE
    )
    return jnp.where(causal[None], scores, MASKED)


def here():
    ctx = lax.axis_index("ctx")
    fsdp = lax.axis_index("fsdp")
    return {
        "x": lax.rem(ctx, 4),
        "y": lax.div(fsdp, 4),
        "z": lax.rem(lax.div(fsdp, 2), 2) * 2 + lax.div(ctx, 4),
        "core": lax.rem(fsdp, 2),
    }


class Net:
    def __init__(self, send_sems, recv_sems):
        self.me = here()
        self.send_sems, self.recv_sems = send_sems, recv_sems
        self.used = 0
        self.sent = []

    def device(self, **moved):
        at = {**self.me, **moved}
        return (
            lax.rem(at["z"], 2) * 4 + at["x"],
            at["y"] * 4 + lax.div(at["z"], 2) * 2 + at["core"],
        )

    def step(self, axis, by):
        return lax.rem(self.me[axis] + by, 4)

    def neighbour(self, axis, by):
        return self.device(**{axis: self.step(axis, by)})

    def sibling(self):
        return self.device(core=1 - self.me["core"])

    def mirror(self):
        z = self.me["z"]
        return self.device(z=z + 1 - 2 * lax.rem(z, 2))

    def barrier(self, peers):
        sem = pltpu.get_barrier_semaphore()
        for peer in peers:
            pl.semaphore_signal(sem, inc=1, device_id=peer, device_id_type=pl.DeviceIdType.MESH)
        pl.semaphore_wait(sem, len(peers))

    def send(self, src, dst, peer):
        n = self.used
        self.used += 1
        copy = pltpu.make_async_remote_copy(
            src_ref=src,
            dst_ref=dst,
            send_sem=self.send_sems.at[n],
            recv_sem=self.recv_sems.at[n],
            device_id=peer,
            device_id_type=pl.DeviceIdType.MESH,
        )
        copy.start()
        self.sent.append(copy)
        return copy

    def send_done(self):
        for copy in self.sent:
            copy.wait_send()


def interleave(*tasks):
    tasks = list(tasks)
    while tasks:
        for task in list(tasks):
            try:
                next(task)
            except StopIteration:
                tasks.remove(task)


def gather_ring(net, axis, own, place, arrived=None):
    mine = net.me[axis]
    left, right, far = net.step(axis, 3), net.step(axis, 1), net.step(axis, 2)
    to_left, to_right = net.neighbour(axis, 3), net.neighbour(axis, 1)
    r0 = net.send(own(0), place(mine, 0), to_right)
    l1 = net.send(own(1), place(mine, 1), to_left)
    r1 = net.send(own(1), place(mine, 1), to_right)
    l0 = net.send(own(0), place(mine, 0), to_left)
    yield
    r0.wait_recv()
    f0 = net.send(place(left, 0), place(left, 0), to_right)
    yield
    l1.wait_recv()
    f1 = net.send(place(right, 1), place(right, 1), to_left)
    yield
    r1.wait_recv()
    if arrived:
        arrived(left)
    yield
    l0.wait_recv()
    if arrived:
        arrived(right)
    yield
    f0.wait_recv()
    f1.wait_recv()
    if arrived:
        arrived(far)


def scatter_ring(net, axis, part, bufs, total):
    mine = net.me[axis]
    left, right, far = net.step(axis, 3), net.step(axis, 1), net.step(axis, 2)
    to_left, to_right = net.neighbour(axis, 3), net.neighbour(axis, 1)
    from_left, from_right, hold, stage = bufs
    a0 = net.send(part(far, 0), hold.at[0], to_right)
    a1 = net.send(part(far, 1), hold.at[1], to_left)
    r1 = net.send(part(right, 1), from_left.at[1], to_right)
    l0 = net.send(part(left, 0), from_right.at[0], to_left)
    yield
    a0.wait_recv()
    stage[0] = (part(right, 0)[...].astype(F32) + hold[0].astype(F32)).astype(BF16)
    r0 = net.send(stage.at[0], from_left.at[0], to_right)
    yield
    a1.wait_recv()
    stage[1] = (part(left, 1)[...].astype(F32) + hold[1].astype(F32)).astype(BF16)
    l1 = net.send(stage.at[1], from_right.at[1], to_left)
    yield
    l0.wait_recv()
    r0.wait_recv()
    total(0, (part(mine, 0), from_left.at[0], from_right.at[0]))
    yield
    r1.wait_recv()
    l1.wait_recv()
    total(1, (part(mine, 1), from_left.at[1], from_right.at[1]))


def add_up(terms):
    out = terms[0][...].astype(F32)
    for term in terms[1:]:
        out = out + term[...].astype(F32)
    return out


def sems(count):
    return [pltpu.SemaphoreType.DMA((count,)), pltpu.SemaphoreType.DMA((count,))]


def call(kernel, name, out_shape, in_spaces, out_spaces, scratch, number):
    return pl.pallas_call(
        kernel,
        name=name,
        out_shape=out_shape,
        in_specs=[pl.BlockSpec(memory_space=space) for space in in_spaces],
        out_specs=[pl.BlockSpec(memory_space=space) for space in out_spaces],
        scratch_shapes=scratch,
        compiler_params=pltpu.CompilerParams(
            collective_id=number, has_side_effects=True, vmem_limit_bytes=VMEM_BYTES
        ),
    )


ORDERS = ("xyz", "yzx", "zxy")
BLOB = 192
PART = BLOB // 3
HALF = PART // 2
FFN_ROWS = (((0, 48), (48, 32)), ((80, 32), (112, 32)))


def grid_at(ref, have, sel, tail):
    index = []
    every = slice(None)
    if "z" in have:
        index.append(lax.rem(sel["z"], 2) if "z" in sel else every)
    for axis in "xy":
        if axis in have:
            index.append(sel.get(axis, every))
    if "z" in have:
        index.append(lax.div(sel["z"], 2) if "z" in sel else every)
    return ref.at[tuple(index) + tail]


def weights_kernel(blob, ffn, all_blobs, all_ffn, send_sems, recv_sems, local_sems):
    net = Net(send_sems, recv_sems)
    me = net.me
    sibling = net.sibling()
    net.barrier([net.neighbour(axis, by) for axis in "xyz" for by in (1, 3)] + [sibling])
    core = me["core"]
    own_blob = pltpu.make_async_copy(
        blob, grid_at(all_blobs, "xyz", me, (core,)), local_sems.at[0]
    )
    own_blob.start()
    own_ffn = pltpu.make_async_copy(ffn, all_ffn.at[:, me["z"], me["x"]], local_sems.at[1])
    own_ffn.start()
    forwards = []

    def blob_task(order, start):
        def rows(h):
            return pl.ds(start + h * HALF, HALF)

        both = pl.ds(start, PART)
        known = dict(me)
        for count, axis in enumerate(order):
            fixed = {k: me[k] for k in order[count + 1 :]}

            def place(k, h):
                return grid_at(all_blobs, "xyz", {**fixed, axis: k}, (core, rows(h)))

            def own(h):
                if count == 0:
                    return blob.at[rows(h)]
                return place(me[axis], h)

            def forward(k):
                ref = grid_at(all_blobs, "xyz", {**fixed, axis: k}, (core, both))
                forwards.append(net.send(ref, ref, sibling))

            if count == 2:
                forward(me[axis])
            yield from gather_ring(net, axis, own, place, forward if count == 2 else None)
            if count == 0 and start == 0:
                own_blob.wait()
            yield

    def ffn_task(order, rows):
        first, second = order
        fixed = me[second]

        def spot(i, j, h):
            ix, iz = (i, j) if first == "x" else (j, i)
            return all_ffn.at[:, iz, ix, pl.ds(*rows[h])]

        yield from gather_ring(
            net, first, lambda h: ffn.at[:, pl.ds(*rows[h])], lambda k, h: spot(k, fixed, h)
        )
        if first == "x":
            own_ffn.wait()
        yield
        yield from gather_ring(
            net,
            second,
            lambda h: spot(slice(None), fixed, h),
            lambda k, h: spot(slice(None), k, h),
        )

    interleave(*(blob_task(order, i * PART) for i, order in enumerate(ORDERS)))
    interleave(ffn_task("xz", FFN_ROWS[0]), ffn_task("zx", FFN_ROWS[1]))
    for copy in forwards:
        copy.wait_recv()
    net.send_done()


def gather_weights(blob, ffn):
    any_ = pl.ANY
    return call(
        weights_kernel,
        "gather_weights",
        [
            jax.ShapeDtypeStruct((2, 4, 4, 2, 2, BLOB, 128), BF16),
            jax.ShapeDtypeStruct((3, 4, 4) + ffn.shape[1:], BF16),
        ],
        [any_, any_],
        [any_, any_],
        sems(3 * (18 + 4) + 24) + [pltpu.SemaphoreType.DMA((2,))],
        1,
    )(blob, ffn)


def grads_kernel(blob, ffn, blob_out, ffn_out, send_sems, recv_sems, *bufs):
    net = Net(send_sems, recv_sems)
    me = net.me
    bufs = list(bufs)
    sibling = net.sibling()
    net.barrier([net.neighbour(axis, by) for axis in "xyz" for by in (1, 3)] + [sibling])
    core = me["core"]
    every = slice(None)
    paired = bufs.pop(0)
    copies = []
    for i in range(3):
        rows = pl.ds(i * PART, PART)
        copies.append(
            net.send(
                blob.at[every, every, every, every, 1 - core, rows],
                paired.at[every, every, every, every, rows],
                sibling,
            )
        )

    def blob_task(order, start, copy, own_bufs):
        own_bufs = list(own_bufs)
        yield
        copy.wait_recv()
        rows = pl.ds(start, PART)
        for a in range(2):
            for b in range(4):
                paired[a, b, :, :, rows] = (
                    paired[a, b, :, :, rows].astype(F32) + blob[a, b, :, :, core, rows].astype(F32)
                ).astype(BF16)
        source, offset = paired, start
        for count, axis in enumerate(order):
            have = order[count:]
            result = own_bufs[4] if count < 2 else None

            def part(k, h, source=source, offset=offset, have=have, axis=axis):
                return grid_at(source, have, {axis: k}, (pl.ds(offset + h * HALF, HALF),))

            def total(h, terms, result=result, count=count, have=have):
                if count < 2:
                    grid_at(result, have[1:], {}, (pl.ds(h * HALF, HALF),))[...] = add_up(
                        terms
                    ).astype(BF16)
                else:
                    blob_out[pl.ds(start + h * HALF, HALF)] = add_up(terms)

            yield from scatter_ring(net, axis, part, own_bufs[:4], total)
            yield
            source, offset = result, 0
            own_bufs = own_bufs[5:]

    def ffn_task(order, rows, own_bufs):
        first, second = order
        fl, fr, hold, stage, result, fl2, fr2, hold2, stage2 = own_bufs

        def cut(bufs, h):
            return tuple(buf.at[:, :, :, pl.ds(0, rows[h][1])] for buf in bufs)

        low = rows[0][0]

        def part(k, h):
            if first == "x":
                return ffn.at[:, :, k, pl.ds(*rows[h])]
            return ffn.at[:, k, :, pl.ds(*rows[h])]

        def total(h, terms):
            result[:, :, pl.ds(rows[h][0] - low, rows[h][1])] = add_up(terms).astype(BF16)

        def part2(k, h):
            return result.at[:, k, pl.ds(rows[h][0] - low, rows[h][1])]

        def total2(h, terms):
            ffn_out[:, pl.ds(*rows[h])] = add_up(terms)

        yield from scatter_uneven(net, first, part, (fl, fr, hold, stage), rows, total)
        yield
        yield from scatter_uneven(net, second, part2, (fl2, fr2, hold2, stage2), rows, total2)

    tasks = []
    for i, order in enumerate(ORDERS):
        tasks.append(blob_task(order, i * PART, copies[i], bufs[:14]))
        bufs = bufs[14:]
    interleave(
        ffn_task("xz", FFN_ROWS[0], bufs[:9]), ffn_task("zx", FFN_ROWS[1], bufs[9:]), *tasks
    )
    net.send_done()


class Cut:
    def __init__(self, ref, rows):
        self.ref, self.rows = ref, rows

    @property
    def at(self):
        return self

    def __getitem__(self, h):
        ref = self.ref.at[h]
        lead = (slice(None),) * (len(ref.shape) - 2)
        return ref.at[lead + (pl.ds(0, self.rows[h][1]),)]


def scatter_uneven(net, axis, part, bufs, rows, total):
    mine = net.me[axis]
    left, right, far = net.step(axis, 3), net.step(axis, 1), net.step(axis, 2)
    to_left, to_right = net.neighbour(axis, 3), net.neighbour(axis, 1)
    from_left, from_right, hold, stage = (Cut(buf, rows) for buf in bufs)
    a0 = net.send(part(far, 0), hold[0], to_right)
    a1 = net.send(part(far, 1), hold[1], to_left)
    r1 = net.send(part(right, 1), from_left[1], to_right)
    l0 = net.send(part(left, 0), from_right[0], to_left)
    yield
    a0.wait_recv()
    stage[0][...] = (part(right, 0)[...].astype(F32) + hold[0][...].astype(F32)).astype(BF16)
    r0 = net.send(stage[0], from_left[0], to_right)
    yield
    a1.wait_recv()
    stage[1][...] = (part(left, 1)[...].astype(F32) + hold[1][...].astype(F32)).astype(BF16)
    l1 = net.send(stage[1], from_right[1], to_left)
    yield
    l0.wait_recv()
    r0.wait_recv()
    total(0, (part(mine, 0), from_left[0], from_right[0]))
    yield
    r1.wait_recv()
    l1.wait_recv()
    total(1, (part(mine, 1), from_left[1], from_right[1]))


def lead_dims(have):
    dims = []
    if "z" in have:
        dims.append(2)
    dims += [4 for axis in "xy" if axis in have]
    if "z" in have:
        dims.append(2)
    return tuple(dims)


def scatter_grads(blob, ffn):
    wide = ffn.shape[-1]
    scratch = sems(3 * 19 + 24) + [pltpu.VMEM((2, 4, 4, 2, BLOB, 128), BF16)]
    for order in ORDERS:
        for count in range(3):
            left = lead_dims(order[count + 1 :])
            scratch += [pltpu.VMEM((2,) + left + (HALF, 128), BF16)] * 4
            if count < 2:
                scratch.append(pltpu.VMEM(left + (PART, 128), BF16))
    for rows in FFN_ROWS:
        most = max(rows[0][1], rows[1][1])
        every = rows[0][1] + rows[1][1]
        scratch += [pltpu.VMEM((2, 3, 4, most, wide), BF16)] * 4
        scratch.append(pltpu.VMEM((3, 4, every, wide), BF16))
        scratch += [pltpu.VMEM((2, 3, most, wide), BF16)] * 4
    vmem = pltpu.VMEM
    return call(
        grads_kernel,
        "scatter_grads",
        [
            jax.ShapeDtypeStruct((BLOB, 128), F32),
            jax.ShapeDtypeStruct((3,) + ffn.shape[3:], F32),
        ],
        [vmem, vmem],
        [vmem, vmem],
        scratch,
        2,
    )(blob, ffn)


def keys_kernel(key, value, keys, values, send_sems, recv_sems, local_sems):
    net = Net(send_sems, recv_sems)
    me = net.me
    mirror = net.mirror()
    net.barrier([net.neighbour("x", 1), net.neighbour("x", 3), mirror])
    low, x = lax.rem(me["z"], 2), me["x"]
    own_key = pltpu.make_async_copy(key, keys.at[low, x], local_sems.at[0])
    own_value = pltpu.make_async_copy(value, values.at[low, x], local_sems.at[1])
    own_key.start()
    own_value.start()
    half = key.shape[0] // 2

    def rows(h):
        return pl.ds(h * half, half)

    def key_task():
        swap = net.send(key, keys.at[low, x], mirror)
        yield
        own_key.wait()
        swap.wait_recv()
        yield from gather_ring(
            net, "x", lambda h: keys.at[:, x, rows(h)], lambda k, h: keys.at[:, k, rows(h)]
        )

    def value_task():
        yield from gather_ring(
            net, "x", lambda h: value.at[rows(h)], lambda k, h: values.at[low, k, rows(h)]
        )
        own_value.wait()
        swap = net.send(values.at[low], values.at[low], mirror)
        yield
        swap.wait_recv()

    interleave(key_task(), value_task())
    net.send_done()


def gather_keys(key, value):
    any_ = pl.ANY
    return call(
        keys_kernel,
        "gather_keys",
        [jax.ShapeDtypeStruct((2, 4) + key.shape, BF16)] * 2,
        [any_, any_],
        [any_, any_],
        sems(14) + [pltpu.SemaphoreType.DMA((2,))],
        3,
    )(key, value)


def key_grads_kernel(keys, values, key, value, send_sems, recv_sems, *bufs):
    net = Net(send_sems, recv_sems)
    me = net.me
    mirror = net.mirror()
    net.barrier([net.neighbour("x", 1), net.neighbour("x", 3), mirror])
    low = lax.rem(me["z"], 2)
    half = key.shape[0] // 2
    key_bufs, value_bufs = bufs[:4], bufs[4:8]
    key_pair, key_sent, value_pair = bufs[8:]

    def rows(h):
        return pl.ds(h * half, half)

    def key_task():
        def total(h, terms):
            key_sent[:, rows(h)] = add_up(terms).astype(BF16)

        yield from scatter_ring(
            net, "x", lambda k, h: keys.at[:, k, rows(h)], key_bufs, total
        )
        swap = net.send(key_sent.at[1 - low], key_pair, mirror)
        yield
        swap.wait_recv()
        key[...] = add_up((key_sent.at[low], key_pair))

    def value_task():
        swap = net.send(values.at[1 - low], value_pair, mirror)
        yield
        swap.wait_recv()
        value_pair[...] = add_up((value_pair, values.at[low])).astype(BF16)

        def total(h, terms):
            value[rows(h)] = add_up(terms)

        yield from scatter_ring(
            net, "x", lambda k, h: value_pair.at[k, rows(h)], value_bufs, total
        )

    interleave(key_task(), value_task())
    net.send_done()


def scatter_key_grads(keys, values):
    rows, width = keys.shape[2:]
    vmem = pltpu.VMEM
    return call(
        key_grads_kernel,
        "scatter_key_grads",
        [jax.ShapeDtypeStruct((rows, width), F32)] * 2,
        [vmem, vmem],
        [vmem, vmem],
        sems(14)
        + [pltpu.VMEM((2, 2, rows // 2, width), BF16)] * 4
        + [pltpu.VMEM((2, rows // 2, width), BF16)] * 4
        + [
            pltpu.VMEM((rows, width), BF16),
            pltpu.VMEM((2, rows, width), BF16),
            pltpu.VMEM((4, rows, width), BF16),
        ],
        4,
    )(keys, values)


def tokens_kernel(own, out, send_sems, recv_sems, local_sems):
    net = Net(send_sems, recv_sems)
    me = net.me
    sibling = net.sibling()
    net.barrier([net.neighbour("y", 1), net.neighbour("y", 3), sibling])
    core, y = me["core"], me["y"]
    local = pltpu.make_async_copy(own, out.at[y, core], local_sems.at[0])
    local.start()
    half = own.shape[0] // 2
    forwards = [net.send(own, out.at[y, core], sibling)]

    def forward(k):
        forwards.append(net.send(out.at[k, core], out.at[k, core], sibling))

    def rows(h):
        return pl.ds(h * half, half)

    interleave(
        gather_ring(
            net,
            "y",
            lambda h: own.at[rows(h)],
            lambda k, h: out.at[k, core, rows(h)],
            forward,
        )
    )
    for copy in forwards:
        copy.wait_recv()
    local.wait()
    net.send_done()


def gather_tokens(own, number):
    any_ = pl.ANY
    return call(
        tokens_kernel,
        f"gather_tokens_{number}",
        [jax.ShapeDtypeStruct((4, 2) + own.shape, BF16)],
        [any_],
        [any_],
        sems(10) + [pltpu.SemaphoreType.DMA((1,))],
        number,
    )(own)[0]


def sums_kernel(parts, out, send_sems, recv_sems, paired, *bufs):
    net = Net(send_sems, recv_sems)
    me = net.me
    sibling = net.sibling()
    net.barrier([net.neighbour("y", 1), net.neighbour("y", 3), sibling])
    core = me["core"]
    half = out.shape[0] // 2
    order = [net.step("y", by) for by in (2, 1, 3)] + [me["y"]]
    copies = [net.send(parts.at[k, 1 - core], paired.at[k], sibling) for k in order]
    for k, copy in zip(order, copies):
        copy.wait_recv()
        paired[k] = (paired[k].astype(F32) + parts[k, core].astype(F32)).astype(BF16)

    def rows(h):
        return pl.ds(h * half, half)

    def total(h, terms):
        out[rows(h)] = add_up(terms)

    interleave(scatter_ring(net, "y", lambda k, h: paired.at[k, rows(h)], bufs, total))
    net.send_done()


def scatter_sums(parts, number):
    rows, width = parts.shape[2:]
    vmem = pltpu.VMEM
    return call(
        sums_kernel,
        f"scatter_sums_{number}",
        [jax.ShapeDtypeStruct((rows, width), F32)],
        [vmem],
        [vmem],
        sems(10)
        + [pltpu.VMEM((4, rows, width), BF16)]
        + [pltpu.VMEM((2, rows // 2, width), BF16)] * 4,
        number,
    )(parts)[0]


def body(
    inputs,
    pair_order,
    attn_gain,
    query_gain,
    key_gain,
    mixer_gain,
    ffn_gain,
    branch_gain,
    query_weight,
    key_weight,
    value_weight,
    output_weight,
    gate_weight,
    up_weight,
    down_weight,
    cotangent,
):
    gains = (attn_gain, query_gain, key_gain, mixer_gain, ffn_gain, branch_gain)
    n_dev = 128
    width = inputs.shape[2]
    rows = inputs.shape[1]
    head_dim = key_weight.shape[1]
    qw = query_weight.shape[1]
    heads = qw // head_dim
    d_own = query_weight.shape[0]
    o_own = output_weight.shape[0]
    qkv_w = qw + 2 * head_dim
    qkv_rows = d_own * qkv_w // 128
    out_rows = o_own * width // 128
    qkv_pad = 112

    gain_row = jnp.concatenate(gains)
    n_gain = gain_row.shape[0]
    gain_row = jnp.pad(gain_row, (0, (qkv_pad - qkv_rows) * 128 - n_gain))
    blob = jnp.concatenate(
        [
            jnp.concatenate([query_weight, key_weight, value_weight], axis=1).reshape(
                qkv_rows, 128
            ),
            gain_row.reshape(qkv_pad - qkv_rows, 128),
            output_weight.reshape(out_rows, 128),
            jnp.zeros((BLOB - qkv_pad - out_rows, 128), BF16),
        ]
    )
    ffn_own = jnp.stack([gate_weight, up_weight, down_weight.T])
    all_blobs, all_ffn = gather_weights(blob, ffn_own)
    all_blobs = all_blobs.reshape(n_dev, BLOB, 128)
    qkv_all = all_blobs[:, :qkv_rows].reshape(n_dev * d_own, qkv_w)
    output_all_w = all_blobs[:, qkv_pad : qkv_pad + out_rows].reshape(n_dev * o_own, width)
    gain_all = all_blobs[:, qkv_rows, :n_gain].astype(F32)
    full_gains = []
    at = 0
    for gain in gains:
        full_gains.append(gain_all[:, at : at + gain.shape[0]].reshape(-1))
        at += gain.shape[0]
    gain_in, gain_query, gain_key, gain_mixed, gain_ffn, gain_branch = full_gains
    ff_own = gate_weight.shape[1]
    all_ffn = all_ffn.reshape(3, 2, width, ff_own)

    slot = lax.axis_index("ctx")
    all_positions = token_positions(pair_order[0], rows).reshape(-1)
    own_positions = lax.dynamic_slice_in_dim(all_positions, slot * rows, rows)
    angle = angles(own_positions, head_dim)
    cosines = jnp.cos(angle)
    sines = jnp.sin(angle)
    causal = all_positions[None, :] <= own_positions[:, None]
    hidden_in = inputs[0].astype(jnp.float32)
    normed_in, norm_in_back = jax.vjp(rms_norm, hidden_in, gain_in)
    attn_input = normed_in.astype(jnp.bfloat16)
    qkv_raw = matmul(attn_input, qkv_all)
    queries_raw = qkv_raw[:, :qw]
    keys_raw = qkv_raw[:, qw : qw + head_dim]
    values_raw = qkv_raw[:, qw + head_dim :]

    def query_shape(raw, gain):
        return rotary(
            rms_norm(raw.reshape(rows, heads, head_dim), gain),
            cosines[:, None, :],
            sines[:, None, :],
        )

    def key_shape(raw, gain):
        return rotary(rms_norm(raw, gain), cosines, sines)

    queries_rot, query_back = jax.vjp(query_shape, queries_raw, gain_query)
    keys_rot, key_back = jax.vjp(key_shape, keys_raw, gain_key)
    query_low = queries_rot.astype(jnp.bfloat16)
    key_low = keys_rot.astype(jnp.bfloat16)
    value_low = values_raw.astype(jnp.bfloat16)
    key_all, value_all = gather_keys(key_low, value_low)
    key_all = key_all.reshape(-1, head_dim)
    value_all = value_all.reshape(-1, head_dim)
    scores = score_block(query_low, key_all, causal)
    peak = jnp.max(scores, axis=-1, keepdims=True)
    expo = jnp.exp(scores - peak)
    total = jnp.sum(expo, axis=-1, keepdims=True)
    probs = expo / total
    probs_low = probs.astype(jnp.bfloat16)
    mixed = jnp.einsum("htk,kd->thd", probs_low, value_all, preferred_element_type=jnp.float32)
    mixed_low = mixed.reshape(rows, heads * head_dim).astype(jnp.bfloat16)
    attn_out = matmul(mixed_low, output_all_w)
    post_attn, post_attn_back = jax.vjp(rms_norm, attn_out, gain_mixed)
    resid = hidden_in + post_attn
    normed_mid, mid_back = jax.vjp(rms_norm, resid, gain_ffn)
    ffn_input = normed_mid.astype(jnp.bfloat16)
    tokens_all = gather_tokens(ffn_input, 5).reshape(-1, width)

    fronts = []
    partial_out = 0.0
    for j in range(2):
        gate_pre = matmul(tokens_all, all_ffn[0, j])
        up_pre = matmul(tokens_all, all_ffn[1, j])
        activated, gelu_back = jax.vjp(partial(jax.nn.gelu, approximate=True), gate_pre)
        hidden_low = (activated * up_pre).astype(jnp.bfloat16)
        fronts.append((up_pre, activated, gelu_back, hidden_low))
        partial_out = partial_out + matmul_nt(hidden_low, all_ffn[2, j])
    branch_raw = scatter_sums(partial_out.astype(BF16).reshape(4, 2, rows, width), 6)
    post_ffn, post_ffn_back = jax.vjp(rms_norm, branch_raw, gain_branch)
    outputs = (resid + post_ffn)[None]
    upstream = cotangent[0].astype(jnp.float32)
    grad_branch, grad_gain_branch = post_ffn_back(upstream)
    branch_low = grad_branch.astype(jnp.bfloat16)
    branch_all = gather_tokens(branch_low, 7).reshape(-1, width)
    grad_tokens_all = 0.0
    ffn_grads = [[], [], []]
    for j in range(2):
        up_pre, activated, gelu_back, hidden_low = fronts[j]
        grad_hidden = matmul(branch_all, all_ffn[2, j])
        ffn_grads[2].append(matmul_tn(branch_all, hidden_low))
        gate_low = gelu_back(grad_hidden * up_pre)[0].astype(jnp.bfloat16)
        up_low = (grad_hidden * activated).astype(jnp.bfloat16)
        grad_tokens_all = (
            grad_tokens_all
            + matmul_nt(gate_low, all_ffn[0, j])
            + matmul_nt(up_low, all_ffn[1, j])
        )
        ffn_grads[0].append(matmul_tn(tokens_all, gate_low))
        ffn_grads[1].append(matmul_tn(tokens_all, up_low))
    ffn_grads = jnp.stack([jnp.stack([g.astype(BF16) for g in pair]) for pair in ffn_grads])
    ffn_grads = ffn_grads.reshape(3, 4, 4, width // 8, ff_own)
    grad_ffn_input = scatter_sums(grad_tokens_all.astype(BF16).reshape(4, 2, rows, width), 8)
    grad_resid_mid, grad_gain_ffn = mid_back(grad_ffn_input)
    grad_resid = upstream + grad_resid_mid
    grad_attn_out, grad_gain_mixed = post_attn_back(grad_resid)
    attn_low = grad_attn_out.astype(jnp.bfloat16)
    grad_mixed = matmul_nt(attn_low, output_all_w)
    grad_output_w = matmul_tn(mixed_low, attn_low)
    mixed_grad_low = grad_mixed.astype(jnp.bfloat16).reshape(rows, heads, head_dim)
    grad_value_all = jnp.einsum(
        "htk,thd->kd", probs_low, mixed_grad_low, preferred_element_type=jnp.float32
    )
    grad_probs = jnp.einsum(
        "thd,kd->htk", mixed_grad_low, value_all, preferred_element_type=jnp.float32
    )
    delta = jnp.sum(grad_probs * probs, axis=-1, keepdims=True)
    grad_scores_low = (probs * (grad_probs - delta)).astype(jnp.bfloat16)
    grad_query_rot = (
        jnp.einsum("htk,kd->thd", grad_scores_low, key_all, preferred_element_type=jnp.float32)
        * SCALE
    )
    grad_key_all = (
        jnp.einsum("htk,thd->kd", grad_scores_low, query_low, preferred_element_type=jnp.float32)
        * SCALE
    )
    grad_key_rot, grad_value = scatter_key_grads(
        grad_key_all.astype(BF16).reshape(2, 4, rows, head_dim),
        grad_value_all.astype(BF16).reshape(2, 4, rows, head_dim),
    )
    grad_query_raw, grad_gain_query = query_back(grad_query_rot)
    grad_key_raw, grad_gain_key = key_back(grad_key_rot)
    glow = jnp.concatenate([grad_query_raw, grad_key_raw, grad_value], axis=1).astype(BF16)
    grad_attn_input = matmul_nt(glow, qkv_all)
    grad_qkv_w = matmul_tn(attn_input, glow)
    grad_hidden_in, grad_gain_in = norm_in_back(grad_attn_input)
    inputs_grad = (grad_resid + grad_hidden_in)[None]
    gain_grads = (
        grad_gain_in,
        grad_gain_query,
        grad_gain_key,
        grad_gain_mixed,
        grad_gain_ffn,
        grad_gain_branch,
    )
    gain_rows = jnp.concatenate([g.astype(BF16).reshape(n_dev, -1) for g in gain_grads], axis=1)
    gain_rows = jnp.pad(gain_rows, ((0, 0), (0, (qkv_pad - qkv_rows) * 128 - n_gain)))
    grad_blobs = jnp.concatenate(
        [
            grad_qkv_w.astype(BF16).reshape(n_dev, qkv_rows, 128),
            gain_rows.reshape(n_dev, qkv_pad - qkv_rows, 128),
            grad_output_w.astype(BF16).reshape(n_dev, out_rows, 128),
            jnp.zeros((n_dev, BLOB - qkv_pad - out_rows, 128), BF16),
        ],
        axis=1,
    ).reshape(2, 4, 4, 2, 2, BLOB, 128)
    blob_sum, ffn_sum = scatter_grads(grad_blobs, ffn_grads)
    qkv_sum = blob_sum[:qkv_rows].reshape(d_own, qkv_w)
    out_sum = blob_sum[qkv_pad : qkv_pad + out_rows].reshape(o_own, width)
    gain_sums = []
    at = 0
    for gain in gains:
        gain_sums.append(blob_sum[qkv_rows, at : at + gain.shape[0]])
        at += gain.shape[0]
    return (
        outputs,
        inputs_grad,
        *gain_sums,
        qkv_sum[:, :qw],
        qkv_sum[:, qw : qw + head_dim],
        qkv_sum[:, qw + head_dim :],
        out_sum,
        ffn_sum[0],
        ffn_sum[1],
        ffn_sum[2].T,
    )


def solution(mesh):
    placed = (
        P("fsdp", "ctx", None),
        P("fsdp", None),
        P(("ctx", "fsdp")),
        P(("ctx", "fsdp")),
        P(("ctx", "fsdp")),
        P(("ctx", "fsdp")),
        P(("ctx", "fsdp")),
        P(("ctx", "fsdp")),
        P(("ctx", "fsdp"), None),
        P(("ctx", "fsdp"), None),
        P(("ctx", "fsdp"), None),
        P(("ctx", "fsdp"), None),
        P("ctx", "fsdp"),
        P("ctx", "fsdp"),
        P("fsdp", "ctx"),
        P("fsdp", "ctx", None),
    )
    return jax.shard_map(
        body,
        mesh=mesh,
        in_specs=placed,
        out_specs=(
            P("fsdp", "ctx", None),
            P("fsdp", "ctx", None),
            P(("ctx", "fsdp")),
            P(("ctx", "fsdp")),
            P(("ctx", "fsdp")),
            P(("ctx", "fsdp")),
            P(("ctx", "fsdp")),
            P(("ctx", "fsdp")),
            P(("ctx", "fsdp"), None),
            P(("ctx", "fsdp"), None),
            P(("ctx", "fsdp"), None),
            P(("ctx", "fsdp"), None),
            P("ctx", "fsdp"),
            P("ctx", "fsdp"),
            P("fsdp", "ctx"),
        ),
        check_vma=False,
    )
```

```python
import jax
import jax.numpy as jnp
from jax import lax
from jax.experimental import pallas as pl
from jax.experimental.pallas import tpu as pltpu
from jax.sharding import PartitionSpec as P

EPS = 1e-06
SCALE = 0.0625
BASE = 1000000.0
MASKED = -1e30
BF16 = jnp.bfloat16
F32 = jnp.float32
VMEM_BYTES = 56 * 1024 * 1024


def rms_norm(values, gain):
    return values * lax.rsqrt(jnp.mean(values * values, axis=-1, keepdims=True) + EPS) * gain


def rotary(values, cosines, sines):
    half = values.shape[-1] // 2
    first = values[..., :half]
    second = values[..., half:]
    return jnp.concatenate(
        [first * cosines - second * sines, second * cosines + first * sines], axis=-1
    )


def angles(positions, width):
    half = width // 2
    freqs = BASE ** (-jnp.arange(half, dtype=jnp.float32) / half)
    return positions.astype(jnp.float32)[:, None] * freqs[None, :]


def token_positions(pairs, tok_rows):
    half = tok_rows // 2
    index = jnp.arange(tok_rows, dtype=jnp.int32)
    count = 2 * pairs.shape[0]
    blocks = jnp.where(index[None, :] < half, pairs[:, None], count - 1 - pairs[:, None])
    return blocks * half + index[None, :] % half


def matmul(left, right):
    return jnp.dot(left, right, preferred_element_type=jnp.float32)


def matmul_tn(left, right):
    return lax.dot_general(
        left, right, (((0,), (0,)), ((), ())), preferred_element_type=jnp.float32
    )


def matmul_nt(left, right):
    return lax.dot_general(
        left, right, (((1,), (1,)), ((), ())), preferred_element_type=jnp.float32
    )


def score_block(query_low, key_all, causal):
    scores = (
        jnp.einsum("thd,kd->htk", query_low, key_all, preferred_element_type=jnp.float32) * SCALE
    )
    return jnp.where(causal[None], scores, MASKED)


def here():
    ctx = lax.axis_index("ctx")
    fsdp = lax.axis_index("fsdp")
    return {
        "x": lax.rem(ctx, 4),
        "y": lax.div(fsdp, 4),
        "z": lax.rem(lax.div(fsdp, 2), 2) * 2 + lax.div(ctx, 4),
        "core": lax.rem(fsdp, 2),
    }


class Net:
    def __init__(self, send_sems, recv_sems):
        self.me = here()
        self.send_sems, self.recv_sems = send_sems, recv_sems
        self.used = 0
        self.sent = []

    def device(self, **moved):
        at = {**self.me, **moved}
        return (
            lax.rem(at["z"], 2) * 4 + at["x"],
            at["y"] * 4 + lax.div(at["z"], 2) * 2 + at["core"],
        )

    def step(self, axis, by):
        return lax.rem(self.me[axis] + by, 4)

    def neighbour(self, axis, by):
        return self.device(**{axis: self.step(axis, by)})

    def sibling(self):
        return self.device(core=1 - self.me["core"])

    def mirror(self):
        z = self.me["z"]
        return self.device(z=z + 1 - 2 * lax.rem(z, 2))

    def barrier(self, peers):
        sem = pltpu.get_barrier_semaphore()
        for peer in peers:
            pl.semaphore_signal(sem, inc=1, device_id=peer, device_id_type=pl.DeviceIdType.MESH)
        pl.semaphore_wait(sem, len(peers))

    def send(self, src, dst, peer):
        n = self.used
        self.used += 1
        copy = pltpu.make_async_remote_copy(
            src_ref=src,
            dst_ref=dst,
            send_sem=self.send_sems.at[n],
            recv_sem=self.recv_sems.at[n],
            device_id=peer,
            device_id_type=pl.DeviceIdType.MESH,
        )
        copy.start()
        self.sent.append(copy)
        return copy

    def send_done(self):
        for copy in self.sent:
            copy.wait_send()


def interleave(*tasks):
    tasks = list(tasks)
    while tasks:
        for task in list(tasks):
            try:
                next(task)
            except StopIteration:
                tasks.remove(task)


def gather_ring(net, axis, own, place, arrived=None):
    mine = net.me[axis]
    left, right, far = net.step(axis, 3), net.step(axis, 1), net.step(axis, 2)
    to_left, to_right = net.neighbour(axis, 3), net.neighbour(axis, 1)
    r0 = net.send(own(0), place(mine, 0), to_right)
    l1 = net.send(own(1), place(mine, 1), to_left)
    r1 = net.send(own(1), place(mine, 1), to_right)
    l0 = net.send(own(0), place(mine, 0), to_left)
    yield
    r0.wait_recv()
    f0 = net.send(place(left, 0), place(left, 0), to_right)
    yield
    l1.wait_recv()
    f1 = net.send(place(right, 1), place(right, 1), to_left)
    yield
    r1.wait_recv()
    if arrived:
        arrived(left)
    yield
    l0.wait_recv()
    if arrived:
        arrived(right)
    yield
    f0.wait_recv()
    f1.wait_recv()
    if arrived:
        arrived(far)


def scatter_ring(net, axis, part, bufs, total):
    mine = net.me[axis]
    left, right, far = net.step(axis, 3), net.step(axis, 1), net.step(axis, 2)
    to_left, to_right = net.neighbour(axis, 3), net.neighbour(axis, 1)
    from_left, from_right, hold, stage = bufs
    a0 = net.send(part(far, 0), hold.at[0], to_right)
    a1 = net.send(part(far, 1), hold.at[1], to_left)
    r1 = net.send(part(right, 1), from_left.at[1], to_right)
    l0 = net.send(part(left, 0), from_right.at[0], to_left)
    yield
    a0.wait_recv()
    stage[0] = (part(right, 0)[...].astype(F32) + hold[0].astype(F32)).astype(BF16)
    r0 = net.send(stage.at[0], from_left.at[0], to_right)
    yield
    a1.wait_recv()
    stage[1] = (part(left, 1)[...].astype(F32) + hold[1].astype(F32)).astype(BF16)
    l1 = net.send(stage.at[1], from_right.at[1], to_left)
    yield
    l0.wait_recv()
    r0.wait_recv()
    total(0, (part(mine, 0), from_left.at[0], from_right.at[0]))
    yield
    r1.wait_recv()
    l1.wait_recv()
    total(1, (part(mine, 1), from_left.at[1], from_right.at[1]))


def add_up(terms):
    out = terms[0][...].astype(F32)
    for term in terms[1:]:
        out = out + term[...].astype(F32)
    return out


def sems(count):
    return [pltpu.SemaphoreType.DMA((count,)), pltpu.SemaphoreType.DMA((count,))]


def call(kernel, name, out_shape, in_spaces, out_spaces, scratch, number):
    return pl.pallas_call(
        kernel,
        name=name,
        out_shape=out_shape,
        in_specs=[pl.BlockSpec(memory_space=space) for space in in_spaces],
        out_specs=[pl.BlockSpec(memory_space=space) for space in out_spaces],
        scratch_shapes=scratch,
        compiler_params=pltpu.CompilerParams(
            collective_id=number, has_side_effects=True, vmem_limit_bytes=VMEM_BYTES
        ),
    )


ORDERS = ("xyz", "yzx", "zxy")
BLOB = 192
PART = BLOB // 3
HALF = PART // 2
FFN_ROWS = (((0, 48), (48, 32)), ((80, 32), (112, 32)))


def grid_at(ref, have, sel, tail):
    index = []
    every = slice(None)
    if "z" in have:
        index.append(lax.rem(sel["z"], 2) if "z" in sel else every)
    for axis in "xy":
        if axis in have:
            index.append(sel.get(axis, every))
    if "z" in have:
        index.append(lax.div(sel["z"], 2) if "z" in sel else every)
    return ref.at[tuple(index) + tail]


def weights_kernel(blob, ffn, all_blobs, all_ffn, send_sems, recv_sems, local_sems):
    net = Net(send_sems, recv_sems)
    me = net.me
    sibling = net.sibling()
    net.barrier([net.neighbour(axis, by) for axis in "xyz" for by in (1, 3)] + [sibling])
    core = me["core"]
    own_blob = pltpu.make_async_copy(
        blob, grid_at(all_blobs, "xyz", me, (core,)), local_sems.at[0]
    )
    own_blob.start()
    own_ffn = pltpu.make_async_copy(ffn, all_ffn.at[:, me["z"], me["x"]], local_sems.at[1])
    own_ffn.start()
    forwards = []

    def blob_task(order, start):
        def rows(h):
            return pl.ds(start + h * HALF, HALF)

        both = pl.ds(start, PART)
        known = dict(me)
        for count, axis in enumerate(order):
            fixed = {k: me[k] for k in order[count + 1 :]}

            def place(k, h):
                return grid_at(all_blobs, "xyz", {**fixed, axis: k}, (core, rows(h)))

            def own(h):
                if count == 0:
                    return blob.at[rows(h)]
                return place(me[axis], h)

            def forward(k):
                ref = grid_at(all_blobs, "xyz", {**fixed, axis: k}, (core, both))
                forwards.append(net.send(ref, ref, sibling))

            if count == 2:
                forward(me[axis])
            yield from gather_ring(net, axis, own, place, forward if count == 2 else None)
            if count == 0 and start == 0:
                own_blob.wait()
            yield

    def ffn_task(order, rows):
        first, second = order
        fixed = me[second]

        def spot(i, j, h):
            ix, iz = (i, j) if first == "x" else (j, i)
            return all_ffn.at[:, iz, ix, pl.ds(*rows[h])]

        yield from gather_ring(
            net, first, lambda h: ffn.at[:, pl.ds(*rows[h])], lambda k, h: spot(k, fixed, h)
        )
        if first == "x":
            own_ffn.wait()
        yield
        yield from gather_ring(
            net,
            second,
            lambda h: spot(slice(None), fixed, h),
            lambda k, h: spot(slice(None), k, h),
        )

    interleave(*(blob_task(order, i * PART) for i, order in enumerate(ORDERS)))
    interleave(ffn_task("xz", FFN_ROWS[0]), ffn_task("zx", FFN_ROWS[1]))
    for copy in forwards:
        copy.wait_recv()
    net.send_done()


def gather_weights(blob, ffn):
    any_ = pl.ANY
    return call(
        weights_kernel,
        "gather_weights",
        [
            jax.ShapeDtypeStruct((2, 4, 4, 2, 2, BLOB, 128), BF16),
            jax.ShapeDtypeStruct((3, 4, 4) + ffn.shape[1:], BF16),
        ],
        [any_, any_],
        [any_, any_],
        sems(3 * (18 + 4) + 24) + [pltpu.SemaphoreType.DMA((2,))],
        1,
    )(blob, ffn)


def grads_kernel(blob, ffn, blob_out, ffn_out, send_sems, recv_sems, *bufs):
    net = Net(send_sems, recv_sems)
    me = net.me
    bufs = list(bufs)
    sibling = net.sibling()
    net.barrier([net.neighbour(axis, by) for axis in "xyz" for by in (1, 3)] + [sibling])
    core = me["core"]
    every = slice(None)
    paired = bufs.pop(0)
    copies = []
    for i in range(3):
        rows = pl.ds(i * PART, PART)
        copies.append(
            net.send(
                blob.at[every, every, every, every, 1 - core, rows],
                paired.at[every, every, every, every, rows],
                sibling,
            )
        )

    def blob_task(order, start, copy, own_bufs):
        own_bufs = list(own_bufs)
        yield
        copy.wait_recv()
        rows = pl.ds(start, PART)
        for a in range(2):
            for b in range(4):
                paired[a, b, :, :, rows] = (
                    paired[a, b, :, :, rows].astype(F32) + blob[a, b, :, :, core, rows].astype(F32)
                ).astype(BF16)
        source, offset = paired, start
        for count, axis in enumerate(order):
            have = order[count:]
            result = own_bufs[4] if count < 2 else None

            def part(k, h, source=source, offset=offset, have=have, axis=axis):
                return grid_at(source, have, {axis: k}, (pl.ds(offset + h * HALF, HALF),))

            def total(h, terms, result=result, count=count, have=have):
                if count < 2:
                    grid_at(result, have[1:], {}, (pl.ds(h * HALF, HALF),))[...] = add_up(
                        terms
                    ).astype(BF16)
                else:
                    blob_out[pl.ds(start + h * HALF, HALF)] = add_up(terms)

            yield from scatter_ring(net, axis, part, own_bufs[:4], total)
            yield
            source, offset = result, 0
            own_bufs = own_bufs[5:]

    def ffn_task(order, rows, own_bufs):
        first, second = order
        fl, fr, hold, stage, result, fl2, fr2, hold2, stage2 = own_bufs

        def cut(bufs, h):
            return tuple(buf.at[:, :, :, pl.ds(0, rows[h][1])] for buf in bufs)

        low = rows[0][0]

        def part(k, h):
            if first == "x":
                return ffn.at[:, :, k, pl.ds(*rows[h])]
            return ffn.at[:, k, :, pl.ds(*rows[h])]

        def total(h, terms):
            result[:, :, pl.ds(rows[h][0] - low, rows[h][1])] = add_up(terms).astype(BF16)

        def part2(k, h):
            return result.at[:, k, pl.ds(rows[h][0] - low, rows[h][1])]

        def total2(h, terms):
            ffn_out[:, pl.ds(*rows[h])] = add_up(terms)

        yield from scatter_uneven(net, first, part, (fl, fr, hold, stage), rows, total)
        yield
        yield from scatter_uneven(net, second, part2, (fl2, fr2, hold2, stage2), rows, total2)

    tasks = []
    for i, order in enumerate(ORDERS):
        tasks.append(blob_task(order, i * PART, copies[i], bufs[:14]))
        bufs = bufs[14:]
    interleave(
        ffn_task("xz", FFN_ROWS[0], bufs[:9]), ffn_task("zx", FFN_ROWS[1], bufs[9:]), *tasks
    )
    net.send_done()


class Cut:
    def __init__(self, ref, rows):
        self.ref, self.rows = ref, rows

    @property
    def at(self):
        return self

    def __getitem__(self, h):
        ref = self.ref.at[h]
        lead = (slice(None),) * (len(ref.shape) - 2)
        return ref.at[lead + (pl.ds(0, self.rows[h][1]),)]


def scatter_uneven(net, axis, part, bufs, rows, total):
    mine = net.me[axis]
    left, right, far = net.step(axis, 3), net.step(axis, 1), net.step(axis, 2)
    to_left, to_right = net.neighbour(axis, 3), net.neighbour(axis, 1)
    from_left, from_right, hold, stage = (Cut(buf, rows) for buf in bufs)
    a0 = net.send(part(far, 0), hold[0], to_right)
    a1 = net.send(part(far, 1), hold[1], to_left)
    r1 = net.send(part(right, 1), from_left[1], to_right)
    l0 = net.send(part(left, 0), from_right[0], to_left)
    yield
    a0.wait_recv()
    stage[0][...] = (part(right, 0)[...].astype(F32) + hold[0][...].astype(F32)).astype(BF16)
    r0 = net.send(stage[0], from_left[0], to_right)
    yield
    a1.wait_recv()
    stage[1][...] = (part(left, 1)[...].astype(F32) + hold[1][...].astype(F32)).astype(BF16)
    l1 = net.send(stage[1], from_right[1], to_left)
    yield
    l0.wait_recv()
    r0.wait_recv()
    total(0, (part(mine, 0), from_left[0], from_right[0]))
    yield
    r1.wait_recv()
    l1.wait_recv()
    total(1, (part(mine, 1), from_left[1], from_right[1]))


def lead_dims(have):
    dims = []
    if "z" in have:
        dims.append(2)
    dims += [4 for axis in "xy" if axis in have]
    if "z" in have:
        dims.append(2)
    return tuple(dims)


def scatter_grads(blob, ffn):
    wide = ffn.shape[-1]
    scratch = sems(3 * 19 + 24) + [pltpu.VMEM((2, 4, 4, 2, BLOB, 128), BF16)]
    for order in ORDERS:
        for count in range(3):
            left = lead_dims(order[count + 1 :])
            scratch += [pltpu.VMEM((2,) + left + (HALF, 128), BF16)] * 4
            if count < 2:
                scratch.append(pltpu.VMEM(left + (PART, 128), BF16))
    for rows in FFN_ROWS:
        most = max(rows[0][1], rows[1][1])
        every = rows[0][1] + rows[1][1]
        scratch += [pltpu.VMEM((2, 3, 4, most, wide), BF16)] * 4
        scratch.append(pltpu.VMEM((3, 4, every, wide), BF16))
        scratch += [pltpu.VMEM((2, 3, most, wide), BF16)] * 4
    vmem = pltpu.VMEM
    return call(
        grads_kernel,
        "scatter_grads",
        [
            jax.ShapeDtypeStruct((BLOB, 128), F32),
            jax.ShapeDtypeStruct((3,) + ffn.shape[3:], F32),
        ],
        [vmem, vmem],
        [vmem, vmem],
        scratch,
        2,
    )(blob, ffn)


def keys_kernel(key, value, keys, values, send_sems, recv_sems, local_sems):
    net = Net(send_sems, recv_sems)
    me = net.me
    mirror = net.mirror()
    net.barrier([net.neighbour("x", 1), net.neighbour("x", 3), mirror])
    low, x = lax.rem(me["z"], 2), me["x"]
    own_key = pltpu.make_async_copy(key, keys.at[low, x], local_sems.at[0])
    own_value = pltpu.make_async_copy(value, values.at[low, x], local_sems.at[1])
    own_key.start()
    own_value.start()
    half = key.shape[0] // 2

    def rows(h):
        return pl.ds(h * half, half)

    def key_task():
        swap = net.send(key, keys.at[low, x], mirror)
        yield
        own_key.wait()
        swap.wait_recv()
        yield from gather_ring(
            net, "x", lambda h: keys.at[:, x, rows(h)], lambda k, h: keys.at[:, k, rows(h)]
        )

    def value_task():
        yield from gather_ring(
            net, "x", lambda h: value.at[rows(h)], lambda k, h: values.at[low, k, rows(h)]
        )
        own_value.wait()
        swap = net.send(values.at[low], values.at[low], mirror)
        yield
        swap.wait_recv()

    interleave(key_task(), value_task())
    net.send_done()


def gather_keys(key, value):
    any_ = pl.ANY
    return call(
        keys_kernel,
        "gather_keys",
        [jax.ShapeDtypeStruct((2, 4) + key.shape, BF16)] * 2,
        [any_, any_],
        [any_, any_],
        sems(14) + [pltpu.SemaphoreType.DMA((2,))],
        3,
    )(key, value)


def key_grads_kernel(keys, values, key, value, send_sems, recv_sems, *bufs):
    net = Net(send_sems, recv_sems)
    me = net.me
    mirror = net.mirror()
    net.barrier([net.neighbour("x", 1), net.neighbour("x", 3), mirror])
    low = lax.rem(me["z"], 2)
    half = key.shape[0] // 2
    key_bufs, value_bufs = bufs[:4], bufs[4:8]
    key_pair, key_sent, value_pair = bufs[8:]

    def rows(h):
        return pl.ds(h * half, half)

    def key_task():
        def total(h, terms):
            key_sent[:, rows(h)] = add_up(terms).astype(BF16)

        yield from scatter_ring(
            net, "x", lambda k, h: keys.at[:, k, rows(h)], key_bufs, total
        )
        swap = net.send(key_sent.at[1 - low], key_pair, mirror)
        yield
        swap.wait_recv()
        key[...] = add_up((key_sent.at[low], key_pair))

    def value_task():
        swap = net.send(values.at[1 - low], value_pair, mirror)
        yield
        swap.wait_recv()
        value_pair[...] = add_up((value_pair, values.at[low])).astype(BF16)

        def total(h, terms):
            value[rows(h)] = add_up(terms)

        yield from scatter_ring(
            net, "x", lambda k, h: value_pair.at[k, rows(h)], value_bufs, total
        )

    interleave(key_task(), value_task())
    net.send_done()


def scatter_key_grads(keys, values):
    rows, width = keys.shape[2:]
    vmem = pltpu.VMEM
    return call(
        key_grads_kernel,
        "scatter_key_grads",
        [jax.ShapeDtypeStruct((rows, width), F32)] * 2,
        [vmem, vmem],
        [vmem, vmem],
        sems(14)
        + [pltpu.VMEM((2, 2, rows // 2, width), BF16)] * 4
        + [pltpu.VMEM((2, rows // 2, width), BF16)] * 4
        + [
            pltpu.VMEM((rows, width), BF16),
            pltpu.VMEM((2, rows, width), BF16),
            pltpu.VMEM((4, rows, width), BF16),
        ],
        4,
    )(keys, values)


class GatherRing:
    def __init__(self, net, axis, own, place):
        self.net, self.own, self.place = net, own, place
        self.mine = net.me[axis]
        self.left, self.right, self.far = (net.step(axis, by) for by in (3, 1, 2))
        self.to_left, self.to_right = net.neighbour(axis, 3), net.neighbour(axis, 1)

    def start(self):
        send, own, place, mine = self.net.send, self.own, self.place, self.mine
        self.r0 = send(own(0), place(mine, 0), self.to_right)
        self.l1 = send(own(1), place(mine, 1), self.to_left)
        self.r1 = send(own(1), place(mine, 1), self.to_right)
        self.l0 = send(own(0), place(mine, 0), self.to_left)

    def pass_on(self):
        send, place = self.net.send, self.place
        self.r0.wait_recv()
        self.f0 = send(place(self.left, 0), place(self.left, 0), self.to_right)
        self.l1.wait_recv()
        self.f1 = send(place(self.right, 1), place(self.right, 1), self.to_left)

    def wait_far(self):
        self.f0.wait_recv()
        self.f1.wait_recv()


class SumRing:
    def __init__(self, net, axis, part, bufs):
        self.net, self.part = net, part
        self.mine = net.me[axis]
        self.left, self.right, self.far = (net.step(axis, by) for by in (3, 1, 2))
        self.to_left, self.to_right = net.neighbour(axis, 3), net.neighbour(axis, 1)
        self.from_left, self.from_right, self.hold, self.stage = bufs

    def send_far(self):
        self.a0 = self.net.send(self.part(self.far, 0), self.hold.at[0], self.to_right)
        self.a1 = self.net.send(self.part(self.far, 1), self.hold.at[1], self.to_left)

    def send_right(self):
        self.r1 = self.net.send(self.part(self.right, 1), self.from_left.at[1], self.to_right)

    def send_left(self):
        self.l0 = self.net.send(self.part(self.left, 0), self.from_right.at[0], self.to_left)

    def pass_on(self):
        self.a0.wait_recv()
        self.stage[0] = add_up((self.part(self.right, 0), self.hold.at[0])).astype(BF16)
        self.r0 = self.net.send(self.stage.at[0], self.from_left.at[0], self.to_right)
        self.a1.wait_recv()
        self.stage[1] = add_up((self.part(self.left, 1), self.hold.at[1])).astype(BF16)
        self.l1 = self.net.send(self.stage.at[1], self.from_right.at[1], self.to_left)

    def total(self, h):
        if h == 0:
            self.l0.wait_recv()
            self.r0.wait_recv()
        else:
            self.r1.wait_recv()
            self.l1.wait_recv()
        return add_up((self.part(self.mine, h), self.from_left.at[h], self.from_right.at[h]))


def gelu_parts(u):
    root = 0.7978845608028654
    square = u * u
    th = jnp.tanh(root * u * (1.0 + 0.044715 * square))
    half = 0.5 * (1.0 + th)
    slope = half + 0.5 * u * (1.0 - th * th) * (root * (1.0 + 3 * 0.044715 * square))
    return u * half, slope


def ffn_kernel(
    own,
    weights,
    resid,
    cotangent,
    gain,
    outputs,
    back,
    gain_grad,
    weight_grads,
    send_sems,
    recv_sems,
    tokens,
    grads,
    act,
    slope,
    hidden,
    gate_g,
    up_g,
    branch,
    *bufs,
):
    net = Net(send_sems, recv_sems)
    me = net.me
    sibling = net.sibling()
    net.barrier([net.neighbour("y", 1), net.neighbour("y", 3), sibling])
    core, y = me["core"], me["y"]
    rows, width = own.shape
    half = rows // 2

    def cut(h):
        return pl.ds(h * half, half)

    def phase(source, held, run, bufs, meanwhile):
        parts, paired, ring_bufs = bufs[0], bufs[1], bufs[2:]
        gather = GatherRing(
            net, "y", lambda h: source.at[cut(h)], lambda k, h: held.at[k, core, cut(h)]
        )
        gather.start()
        swap = net.send(source, held.at[y, core], sibling)
        held[y, core] = source[...]
        left, right, far = gather.left, gather.right, gather.far

        def across(k):
            return net.send(held.at[k, core], held.at[k, core], sibling)

        def give(k):
            return net.send(parts.at[k, 1 - core], paired.at[k], sibling)

        def pair(k, copy):
            copy.wait_recv()
            paired[k] = add_up((paired.at[k], parts.at[k, core])).astype(BF16)

        sums = SumRing(net, "y", lambda k, h: paired.at[k, cut(h)], ring_bufs)
        swap.wait_recv()
        parts[y] = run(y)
        pair_own = give(y)
        gather.pass_on()
        gather.r1.wait_recv()
        swap_left = across(left)
        gather.l0.wait_recv()
        swap_right = across(right)
        swap_left.wait_recv()
        parts[left] = run(left)
        pair_left = give(left)
        gather.wait_far()
        swap_far = across(far)
        pair(y, pair_own)
        swap_right.wait_recv()
        parts[right] = run(right)
        pair_right = give(right)
        pair(left, pair_left)
        sums.send_left()
        swap_far.wait_recv()
        parts[far] = run(far)
        pair_far = give(far)
        pair(right, pair_right)
        sums.send_right()
        pair(far, pair_far)
        sums.send_far()
        meanwhile(0)
        sums.pass_on()
        meanwhile(1)
        return sums

    def dot(left, right, dims):
        return lax.dot_general(left, right, (dims, ((), ())), preferred_element_type=F32)

    def forward(k):
        rows_k = tokens[k].reshape(2 * rows, width)
        total = None
        for j in range(2):
            gate = dot(rows_k, weights[0, j], ((1,), (0,)))
            upper = dot(rows_k, weights[1, j], ((1,), (0,)))
            value, diff = gelu_parts(gate)
            act[k, j] = value.astype(BF16)
            slope[k, j] = (diff * upper).astype(BF16)
            hidden_low = (value * upper).astype(BF16)
            hidden[k, j] = hidden_low
            out = dot(hidden_low, weights[2, j], ((1,), (1,)))
            total = out if total is None else total + out
        return total.astype(BF16).reshape(2, rows, width)

    def backward(k):
        rows_k = grads[k].reshape(2 * rows, width)
        total = None
        for j in range(2):
            hidden_grad = dot(rows_k, weights[2, j], ((1,), (0,)))
            gate_low = (hidden_grad * slope[k, j].astype(F32)).astype(BF16)
            up_low = (hidden_grad * act[k, j].astype(F32)).astype(BF16)
            gate_g[k, j] = gate_low
            up_g[k, j] = up_low
            out = dot(gate_low, weights[0, j], ((1,), (1,))) + dot(
                up_low, weights[1, j], ((1,), (1,))
            )
            total = out if total is None else total + out
        return total.astype(BF16).reshape(2, rows, width)

    def weight_grad(which, held, factor):
        flat = held[...].reshape(8 * rows, width)
        for j in range(2):
            weight_grads[which, j] = dot(
                flat, factor[:, j].reshape(8 * rows, factor.shape[-1]), ((0,), (0,))
            ).astype(BF16)

    sums = phase(own, tokens, forward, bufs[:6], lambda step: None)
    gain_f = gain[...]
    gain_total = jnp.zeros_like(gain_f)
    for h in range(2):
        raw = sums.total(h)
        upstream = cotangent[cut(h)].astype(F32)
        scale = lax.rsqrt(jnp.mean(raw * raw, axis=-1, keepdims=True) + EPS)
        normed = raw * scale
        outputs[cut(h)] = resid[cut(h)] + normed * gain_f
        scaled = upstream * gain_f
        gain_total = gain_total + jnp.sum(upstream * normed, axis=0, keepdims=True)
        inner = jnp.mean(scaled * normed, axis=-1, keepdims=True)
        branch[cut(h)] = (scale * (scaled - normed * inner)).astype(BF16)
    gain_grad[...] = gain_total

    def meanwhile(step):
        if step == 0:
            weight_grad(2, grads, hidden)
        else:
            weight_grad(0, tokens, gate_g)
            weight_grad(1, tokens, up_g)

    sums = phase(branch, grads, backward, bufs[6:], meanwhile)
    for h in range(2):
        back[cut(h)] = sums.total(h)
    net.send_done()


def feed_forward(own, weights, resid, cotangent, gain):
    rows, width = own.shape
    wide = weights.shape[-1]
    vmem = pltpu.VMEM
    phase_bufs = [
        pltpu.VMEM((4, 2, rows, width), BF16),
        pltpu.VMEM((4, rows, width), BF16),
    ] + [pltpu.VMEM((2, rows // 2, width), BF16)] * 4
    return call(
        ffn_kernel,
        "feed_forward",
        [
            jax.ShapeDtypeStruct((rows, width), F32),
            jax.ShapeDtypeStruct((rows, width), F32),
            jax.ShapeDtypeStruct((1, width), F32),
            jax.ShapeDtypeStruct(weights.shape, BF16),
        ],
        [vmem] * 5,
        [vmem] * 4,
        sems(40)
        + [pltpu.VMEM((4, 2, rows, width), BF16)] * 2
        + [pltpu.VMEM((4, 2, 2 * rows, wide), BF16)] * 5
        + [pltpu.VMEM((rows, width), BF16)]
        + phase_bufs * 2,
        5,
    )(own, weights, resid, cotangent, gain)


def body(
    inputs,
    pair_order,
    attn_gain,
    query_gain,
    key_gain,
    mixer_gain,
    ffn_gain,
    branch_gain,
    query_weight,
    key_weight,
    value_weight,
    output_weight,
    gate_weight,
    up_weight,
    down_weight,
    cotangent,
):
    gains = (attn_gain, query_gain, key_gain, mixer_gain, ffn_gain, branch_gain)
    n_dev = 128
    width = inputs.shape[2]
    rows = inputs.shape[1]
    head_dim = key_weight.shape[1]
    qw = query_weight.shape[1]
    heads = qw // head_dim
    d_own = query_weight.shape[0]
    o_own = output_weight.shape[0]
    qkv_w = qw + 2 * head_dim
    qkv_rows = d_own * qkv_w // 128
    out_rows = o_own * width // 128
    qkv_pad = 112

    gain_row = jnp.concatenate(gains)
    n_gain = gain_row.shape[0]
    gain_row = jnp.pad(gain_row, (0, (qkv_pad - qkv_rows) * 128 - n_gain))
    blob = jnp.concatenate(
        [
            jnp.concatenate([query_weight, key_weight, value_weight], axis=1).reshape(
                qkv_rows, 128
            ),
            gain_row.reshape(qkv_pad - qkv_rows, 128),
            output_weight.reshape(out_rows, 128),
            jnp.zeros((BLOB - qkv_pad - out_rows, 128), BF16),
        ]
    )
    ffn_own = jnp.stack([gate_weight, up_weight, down_weight.T])
    all_blobs, all_ffn = gather_weights(blob, ffn_own)
    all_blobs = all_blobs.reshape(n_dev, BLOB, 128)
    qkv_all = all_blobs[:, :qkv_rows].reshape(n_dev * d_own, qkv_w)
    output_all_w = all_blobs[:, qkv_pad : qkv_pad + out_rows].reshape(n_dev * o_own, width)
    gain_all = all_blobs[:, qkv_rows, :n_gain].astype(F32)
    full_gains = []
    at = 0
    for gain in gains:
        full_gains.append(gain_all[:, at : at + gain.shape[0]].reshape(-1))
        at += gain.shape[0]
    gain_in, gain_query, gain_key, gain_mixed, gain_ffn, gain_branch = full_gains
    ff_own = gate_weight.shape[1]
    all_ffn = all_ffn.reshape(3, 2, width, ff_own)

    slot = lax.axis_index("ctx")
    all_positions = token_positions(pair_order[0], rows).reshape(-1)
    own_positions = lax.dynamic_slice_in_dim(all_positions, slot * rows, rows)
    angle = angles(own_positions, head_dim)
    cosines = jnp.cos(angle)
    sines = jnp.sin(angle)
    causal = all_positions[None, :] <= own_positions[:, None]
    hidden_in = inputs[0].astype(jnp.float32)
    normed_in, norm_in_back = jax.vjp(rms_norm, hidden_in, gain_in)
    attn_input = normed_in.astype(jnp.bfloat16)
    qkv_raw = matmul(attn_input, qkv_all)
    queries_raw = qkv_raw[:, :qw]
    keys_raw = qkv_raw[:, qw : qw + head_dim]
    values_raw = qkv_raw[:, qw + head_dim :]

    def query_shape(raw, gain):
        return rotary(
            rms_norm(raw.reshape(rows, heads, head_dim), gain),
            cosines[:, None, :],
            sines[:, None, :],
        )

    def key_shape(raw, gain):
        return rotary(rms_norm(raw, gain), cosines, sines)

    queries_rot, query_back = jax.vjp(query_shape, queries_raw, gain_query)
    keys_rot, key_back = jax.vjp(key_shape, keys_raw, gain_key)
    query_low = queries_rot.astype(jnp.bfloat16)
    key_low = keys_rot.astype(jnp.bfloat16)
    value_low = values_raw.astype(jnp.bfloat16)
    key_all, value_all = gather_keys(key_low, value_low)
    key_all = key_all.reshape(-1, head_dim)
    value_all = value_all.reshape(-1, head_dim)
    scores = score_block(query_low, key_all, causal)
    peak = jnp.max(scores, axis=-1, keepdims=True)
    expo = jnp.exp(scores - peak)
    total = jnp.sum(expo, axis=-1, keepdims=True)
    probs = expo / total
    probs_low = probs.astype(jnp.bfloat16)
    mixed = jnp.einsum("htk,kd->thd", probs_low, value_all, preferred_element_type=jnp.float32)
    mixed_low = mixed.reshape(rows, heads * head_dim).astype(jnp.bfloat16)
    attn_out = matmul(mixed_low, output_all_w)
    post_attn, post_attn_back = jax.vjp(rms_norm, attn_out, gain_mixed)
    resid = hidden_in + post_attn
    normed_mid, mid_back = jax.vjp(rms_norm, resid, gain_ffn)
    ffn_input = normed_mid.astype(jnp.bfloat16)
    outputs, grad_ffn_input, grad_gain_branch, ffn_grads = feed_forward(
        ffn_input, all_ffn, resid, cotangent[0], gain_branch[None]
    )
    ffn_grads = ffn_grads.reshape(3, 4, 4, width // 8, ff_own)
    upstream = cotangent[0].astype(jnp.float32)
    grad_resid_mid, grad_gain_ffn = mid_back(grad_ffn_input)
    grad_resid = upstream + grad_resid_mid
    grad_attn_out, grad_gain_mixed = post_attn_back(grad_resid)
    attn_low = grad_attn_out.astype(jnp.bfloat16)
    grad_mixed = matmul_nt(attn_low, output_all_w)
    grad_output_w = matmul_tn(mixed_low, attn_low)
    mixed_grad_low = grad_mixed.astype(jnp.bfloat16).reshape(rows, heads, head_dim)
    grad_value_all = jnp.einsum(
        "htk,thd->kd", probs_low, mixed_grad_low, preferred_element_type=jnp.float32
    )
    grad_probs = jnp.einsum(
        "thd,kd->htk", mixed_grad_low, value_all, preferred_element_type=jnp.float32
    )
    delta = jnp.sum(grad_probs * probs, axis=-1, keepdims=True)
    grad_scores_low = (probs * (grad_probs - delta)).astype(jnp.bfloat16)
    grad_query_rot = (
        jnp.einsum("htk,kd->thd", grad_scores_low, key_all, preferred_element_type=jnp.float32)
        * SCALE
    )
    grad_key_all = (
        jnp.einsum("htk,thd->kd", grad_scores_low, query_low, preferred_element_type=jnp.float32)
        * SCALE
    )
    grad_key_rot, grad_value = scatter_key_grads(
        grad_key_all.astype(BF16).reshape(2, 4, rows, head_dim),
        grad_value_all.astype(BF16).reshape(2, 4, rows, head_dim),
    )
    grad_query_raw, grad_gain_query = query_back(grad_query_rot)
    grad_key_raw, grad_gain_key = key_back(grad_key_rot)
    glow = jnp.concatenate([grad_query_raw, grad_key_raw, grad_value], axis=1).astype(BF16)
    grad_attn_input = matmul_nt(glow, qkv_all)
    grad_qkv_w = matmul_tn(attn_input, glow)
    grad_hidden_in, grad_gain_in = norm_in_back(grad_attn_input)
    inputs_grad = (grad_resid + grad_hidden_in)[None]
    gain_grads = (
        grad_gain_in,
        grad_gain_query,
        grad_gain_key,
        grad_gain_mixed,
        grad_gain_ffn,
        grad_gain_branch,
    )
    gain_rows = jnp.concatenate([g.astype(BF16).reshape(n_dev, -1) for g in gain_grads], axis=1)
    gain_rows = jnp.pad(gain_rows, ((0, 0), (0, (qkv_pad - qkv_rows) * 128 - n_gain)))
    grad_blobs = jnp.concatenate(
        [
            grad_qkv_w.astype(BF16).reshape(n_dev, qkv_rows, 128),
            gain_rows.reshape(n_dev, qkv_pad - qkv_rows, 128),
            grad_output_w.astype(BF16).reshape(n_dev, out_rows, 128),
            jnp.zeros((n_dev, BLOB - qkv_pad - out_rows, 128), BF16),
        ],
        axis=1,
    ).reshape(2, 4, 4, 2, 2, BLOB, 128)
    blob_sum, ffn_sum = scatter_grads(grad_blobs, ffn_grads)
    qkv_sum = blob_sum[:qkv_rows].reshape(d_own, qkv_w)
    out_sum = blob_sum[qkv_pad : qkv_pad + out_rows].reshape(o_own, width)
    gain_sums = []
    at = 0
    for gain in gains:
        gain_sums.append(blob_sum[qkv_rows, at : at + gain.shape[0]])
        at += gain.shape[0]
    return (
        outputs[None],
        inputs_grad,
        *gain_sums,
        qkv_sum[:, :qw],
        qkv_sum[:, qw : qw + head_dim],
        qkv_sum[:, qw + head_dim :],
        out_sum,
        ffn_sum[0],
        ffn_sum[1],
        ffn_sum[2].T,
    )


def solution(mesh):
    placed = (
        P("fsdp", "ctx", None),
        P("fsdp", None),
        P(("ctx", "fsdp")),
        P(("ctx", "fsdp")),
        P(("ctx", "fsdp")),
        P(("ctx", "fsdp")),
        P(("ctx", "fsdp")),
        P(("ctx", "fsdp")),
        P(("ctx", "fsdp"), None),
        P(("ctx", "fsdp"), None),
        P(("ctx", "fsdp"), None),
        P(("ctx", "fsdp"), None),
        P("ctx", "fsdp"),
        P("ctx", "fsdp"),
        P("fsdp", "ctx"),
        P("fsdp", "ctx", None),
    )
    return jax.shard_map(
        body,
        mesh=mesh,
        in_specs=placed,
        out_specs=(
            P("fsdp", "ctx", None),
            P("fsdp", "ctx", None),
            P(("ctx", "fsdp")),
            P(("ctx", "fsdp")),
            P(("ctx", "fsdp")),
            P(("ctx", "fsdp")),
            P(("ctx", "fsdp")),
            P(("ctx", "fsdp")),
            P(("ctx", "fsdp"), None),
            P(("ctx", "fsdp"), None),
            P(("ctx", "fsdp"), None),
            P(("ctx", "fsdp"), None),
            P("ctx", "fsdp"),
            P("ctx", "fsdp"),
            P("fsdp", "ctx"),
        ),
        check_vma=False,
    )
```

```python
import jax
import jax.numpy as jnp
import numpy as np
from jax import lax
from jax.experimental import pallas as pl
from jax.experimental.pallas import tpu as pltpu
from jax.sharding import PartitionSpec as P

EPS = 1e-06
SCALE = 0.0625
BASE = 1000000.0
MASKED = -1e30
BF16 = jnp.bfloat16
F32 = jnp.float32
VMEM_BYTES = 56 * 1024 * 1024


def rms_norm(values, gain):
    return values * lax.rsqrt(jnp.mean(values * values, axis=-1, keepdims=True) + EPS) * gain


def rotary(values, cosines, sines):
    half = values.shape[-1] // 2
    first = values[..., :half]
    second = values[..., half:]
    return jnp.concatenate(
        [first * cosines - second * sines, second * cosines + first * sines], axis=-1
    )


def angles(positions, width):
    half = width // 2
    freqs = BASE ** (-jnp.arange(half, dtype=jnp.float32) / half)
    return positions.astype(jnp.float32)[:, None] * freqs[None, :]


def token_positions(pairs, tok_rows):
    half = tok_rows // 2
    index = jnp.arange(tok_rows, dtype=jnp.int32)
    count = 2 * pairs.shape[0]
    blocks = jnp.where(index[None, :] < half, pairs[:, None], count - 1 - pairs[:, None])
    return blocks * half + index[None, :] % half


def matmul(left, right):
    return jnp.dot(left, right, preferred_element_type=jnp.float32)


def matmul_tn(left, right):
    return lax.dot_general(
        left, right, (((0,), (0,)), ((), ())), preferred_element_type=jnp.float32
    )


def matmul_nt(left, right):
    return lax.dot_general(
        left, right, (((1,), (1,)), ((), ())), preferred_element_type=jnp.float32
    )


def score_block(query_low, key_all, causal):
    scores = (
        jnp.einsum("thd,kd->htk", query_low, key_all, preferred_element_type=jnp.float32) * SCALE
    )
    return jnp.where(causal[None], scores, MASKED)


def here():
    ctx = lax.axis_index("ctx")
    fsdp = lax.axis_index("fsdp")
    return {
        "x": lax.rem(ctx, 4),
        "y": lax.div(fsdp, 4),
        "z": lax.rem(lax.div(fsdp, 2), 2) * 2 + lax.div(ctx, 4),
        "core": lax.rem(fsdp, 2),
    }


class Net:
    def __init__(self, send_sems, recv_sems):
        self.me = here()
        self.send_sems, self.recv_sems = send_sems, recv_sems
        self.used = 0
        self.sent = []

    def device(self, **moved):
        at = {**self.me, **moved}
        return (
            lax.rem(at["z"], 2) * 4 + at["x"],
            at["y"] * 4 + lax.div(at["z"], 2) * 2 + at["core"],
        )

    def step(self, axis, by):
        return lax.rem(self.me[axis] + by, 4)

    def neighbour(self, axis, by):
        return self.device(**{axis: self.step(axis, by)})

    def sibling(self):
        return self.device(core=1 - self.me["core"])

    def mirror(self):
        z = self.me["z"]
        return self.device(z=z + 1 - 2 * lax.rem(z, 2))

    def barrier(self, peers):
        sem = pltpu.get_barrier_semaphore()
        for peer in peers:
            pl.semaphore_signal(sem, inc=1, device_id=peer, device_id_type=pl.DeviceIdType.MESH)
        pl.semaphore_wait(sem, len(peers))

    def send(self, src, dst, peer):
        n = self.used
        self.used += 1
        copy = pltpu.make_async_remote_copy(
            src_ref=src,
            dst_ref=dst,
            send_sem=self.send_sems.at[n],
            recv_sem=self.recv_sems.at[n],
            device_id=peer,
            device_id_type=pl.DeviceIdType.MESH,
        )
        copy.start()
        self.sent.append(copy)
        return copy

    def send_done(self):
        for copy in self.sent:
            copy.wait_send()


def interleave(*tasks):
    tasks = list(tasks)
    while tasks:
        for task in list(tasks):
            try:
                next(task)
            except StopIteration:
                tasks.remove(task)


def gather_ring(net, axis, own, place, arrived=None):
    mine = net.me[axis]
    left, right, far = net.step(axis, 3), net.step(axis, 1), net.step(axis, 2)
    to_left, to_right = net.neighbour(axis, 3), net.neighbour(axis, 1)
    r0 = net.send(own(0), place(mine, 0), to_right)
    l1 = net.send(own(1), place(mine, 1), to_left)
    r1 = net.send(own(1), place(mine, 1), to_right)
    l0 = net.send(own(0), place(mine, 0), to_left)
    yield
    r0.wait_recv()
    f0 = net.send(place(left, 0), place(left, 0), to_right)
    yield
    l1.wait_recv()
    f1 = net.send(place(right, 1), place(right, 1), to_left)
    yield
    r1.wait_recv()
    if arrived:
        arrived(left)
    yield
    l0.wait_recv()
    if arrived:
        arrived(right)
    yield
    f0.wait_recv()
    f1.wait_recv()
    if arrived:
        arrived(far)


def scatter_ring(net, axis, part, bufs, total):
    mine = net.me[axis]
    left, right, far = net.step(axis, 3), net.step(axis, 1), net.step(axis, 2)
    to_left, to_right = net.neighbour(axis, 3), net.neighbour(axis, 1)
    from_left, from_right, hold, stage = bufs
    a0 = net.send(part(far, 0), hold.at[0], to_right)
    a1 = net.send(part(far, 1), hold.at[1], to_left)
    r1 = net.send(part(right, 1), from_left.at[1], to_right)
    l0 = net.send(part(left, 0), from_right.at[0], to_left)
    yield
    a0.wait_recv()
    stage[0] = add_up((part(right, 0), hold.at[0])).astype(BF16)
    r0 = net.send(stage.at[0], from_left.at[0], to_right)
    yield
    a1.wait_recv()
    stage[1] = add_up((part(left, 1), hold.at[1])).astype(BF16)
    l1 = net.send(stage.at[1], from_right.at[1], to_left)
    yield
    l0.wait_recv()
    r0.wait_recv()
    total(0, (part(mine, 0), from_left.at[0], from_right.at[0]))
    yield
    r1.wait_recv()
    l1.wait_recv()
    total(1, (part(mine, 1), from_left.at[1], from_right.at[1]))


def add_up(terms):
    out = terms[0][...].astype(F32)
    for term in terms[1:]:
        out = out + term[...].astype(F32)
    return out


def sems(count):
    return [pltpu.SemaphoreType.DMA((count,)), pltpu.SemaphoreType.DMA((count,))]


def call(kernel, name, out_shape, in_spaces, out_spaces, scratch, number):
    return pl.pallas_call(
        kernel,
        name=name,
        out_shape=out_shape,
        in_specs=[pl.BlockSpec(memory_space=space) for space in in_spaces],
        out_specs=[pl.BlockSpec(memory_space=space) for space in out_spaces],
        scratch_shapes=scratch,
        compiler_params=pltpu.CompilerParams(
            collective_id=number, has_side_effects=True, vmem_limit_bytes=VMEM_BYTES
        ),
    )


ORDERS = ("xyz", "yzx", "zxy")
FFN_ROWS = (((0, 48), (48, 32)), ((80, 32), (112, 32)))
HEADS = 4
EXTRA = 16
GAIN_ROW = 12
WIRE = 1536
PIECE = WIRE // 3


def grid_at(ref, have, sel, tail):
    index = []
    every = slice(None)
    if "z" in have:
        index.append(lax.rem(sel["z"], 2) if "z" in sel else every)
    for axis in "xy":
        if axis in have:
            index.append(sel.get(axis, every))
    if "z" in have:
        index.append(lax.div(sel["z"], 2) if "z" in sel else every)
    return ref.at[tuple(index) + tail]


def lead_dims(have):
    dims = []
    if "z" in have:
        dims.append(2)
    dims += [4 for axis in "xy" if axis in have]
    if "z" in have:
        dims.append(2)
    return tuple(dims)


def dot(left, right, dims):
    return lax.dot_general(left, right, (dims, ((), ())), preferred_element_type=F32)


NN = ((1,), (0,))
NT = ((1,), (1,))
TN = ((0,), (0,))


def spread(width, offset, mod):
    lane = lax.broadcasted_iota(jnp.int32, (128, width), 0)
    return jnp.where(lane == offset + mod, 1.0, 0.0).astype(BF16)


def owned(width, div):
    row = lax.broadcasted_iota(jnp.int32, (128, width), 0)
    device = jnp.where(row < 64, 2 * row, 2 * row - 127)
    return device == div


def order_matrix(natural):
    width = natural.shape[1]
    row = lax.broadcasted_iota(jnp.int32, (width, width), 0)
    return jnp.where(row == natural, 1.0, 0.0).astype(BF16)


def norm_parts(v, gain):
    scale = lax.rsqrt(jnp.mean(v * v, axis=-1, keepdims=True) + EPS)
    normed = v * scale
    return normed * gain, normed, scale


def norm_grad(v, gain, dy):
    _, normed, scale = norm_parts(v, gain)
    scaled = dy * gain
    inner = jnp.mean(scaled * normed, axis=-1, keepdims=True)
    return scale * (scaled - normed * inner), jnp.sum(dy * normed, axis=0, keepdims=True)


def turn(v, cosines, sines):
    a, b = v[:, :128], v[:, 128:]
    return jnp.concatenate([a * cosines - b * sines, b * cosines + a * sines], axis=1)


def turn_back(v, cosines, sines):
    a, b = v[:, :128], v[:, 128:]
    return jnp.concatenate([a * cosines + b * sines, b * cosines - a * sines], axis=1)


def attention_kernel(
    own8,
    own_extra,
    ffn,
    inputs,
    own_pos,
    all_pos,
    cosines,
    sines,
    natural,
    mod9,
    div9,
    mod2,
    div2,
    all_ffn,
    weights_out,
    last_rows,
    gains,
    attn_p,
    qkv,
    query_low,
    keys_out,
    values_out,
    probs_out,
    mixed_out,
    attn_out,
    resid_out,
    ffn_in,
    send_sems,
    recv_sems,
    local_sems,
    weights,
    other8,
    other_extra,
    start,
    extras,
    key_own,
    value_own,
    keys,
    values,
):
    net = Net(send_sems, recv_sems)
    me = net.me
    sibling, mirror = net.sibling(), net.mirror()
    net.barrier(
        [net.neighbour(axis, by) for axis in "xyz" for by in (1, 3)] + [sibling]
    )
    core, x_at, low = me["core"], me["x"], lax.rem(me["z"], 2)
    swap8 = net.send(own8, other8, sibling)
    swap_extra = net.send(own_extra, other_extra, sibling)
    own_ffn = pltpu.make_async_copy(ffn, all_ffn.at[:, me["z"], x_at], local_sems.at[0])
    own_ffn.start()
    forwards = []

    def piece(p, h):
        return pl.ds(p * PIECE + h * (PIECE // 2), PIECE // 2)

    every = slice(None)

    def blob_task(order, p):
        both = pl.ds(p * PIECE, PIECE)
        held = weights.at[core]
        for count, axis in enumerate(order):
            fixed = {k: me[k] for k in order[count + 1 :]}

            def place(k, h):
                return grid_at(held, "xyz", {**fixed, axis: k}, (every, piece(p, h)))

            def own(h):
                if count == 0:
                    return start.at[:, piece(p, h)]
                return place(me[axis], h)

            def forward(k):
                ref = grid_at(held, "xyz", {**fixed, axis: k}, (every, both))
                forwards.append(net.send(ref, ref, sibling))

            if count == 2:
                forward(me[axis])
            yield from gather_ring(net, axis, own, place, forward if count == 2 else None)
            yield

    def ffn_first(first, rows):
        fixed = me["z" if first == "x" else "x"]

        def spot(k, h):
            ix, iz = (k, fixed) if first == "x" else (fixed, k)
            return all_ffn.at[:, iz, ix, pl.ds(*rows[h])]

        yield from gather_ring(net, first, lambda h: ffn.at[:, pl.ds(*rows[h])], spot)

    def ffn_second(second, rows):
        def spot(k, h):
            ix, iz = (k, every) if second == "x" else (every, k)
            return all_ffn.at[:, iz, ix, pl.ds(*rows[h])]

        yield from gather_ring(net, second, lambda h: spot(me[second], h), spot)

    swap8.wait_recv()
    swap_extra.wait_recv()
    first = core == 0
    mine8, theirs8 = own8[...], other8[...]
    chip = jnp.concatenate(
        [jnp.where(first, mine8, theirs8), jnp.where(first, theirs8, mine8)], axis=0
    )
    mine_x, theirs_x = own_extra[...].astype(F32), other_extra[...].astype(F32)
    half1 = jnp.concatenate(
        [
            chip[:, WIRE:],
            jnp.where(first, mine_x, theirs_x),
            jnp.where(first, theirs_x, mine_x),
            jnp.zeros((16, 2 * WIRE - chip.shape[1] - 256), F32),
        ],
        axis=1,
    )
    block = jnp.where(first, chip[:, :WIRE], half1).astype(BF16)
    start[...] = block
    weights[core, low, x_at, me["y"], lax.div(me["z"], 2)] = block

    interleave(
        *(blob_task(order, p) for p, order in enumerate(ORDERS)),
        ffn_first("x", FFN_ROWS[0]),
        ffn_first("z", FFN_ROWS[1]),
    )
    own_ffn.wait()
    background = [ffn_second("z", FFN_ROWS[0]), ffn_second("x", FFN_ROWS[1])]

    def progress():
        for task in list(background):
            try:
                next(task)
            except StopIteration:
                background.remove(task)

    progress()
    order = order_matrix(natural[...])
    for copy in forwards:
        copy.wait_recv()
    save = pltpu.make_async_copy(weights, weights_out, local_sems.at[1])
    save.start()
    for c in range(2):
        extras[c * 1024 : (c + 1) * 1024] = (
            weights[1, :, :, :, :, :, 1152 + c * 128 : 1280 + c * 128]
            .reshape(1024, 128)
            .astype(F32)
        )

    def extra_row(j):
        return extras[pl.ds(j, 128, stride=EXTRA), :].astype(BF16)

    for j in range(12):
        last_rows[:, j * 128 : (j + 1) * 128] = extra_row(j)
    packed = extra_row(GAIN_ROW)

    def unpack(offset, mod, div):
        wide = dot(packed, spread(mod.shape[1], offset, mod), NN)
        return jnp.sum(jnp.where(owned(mod.shape[1], div), wide, 0.0), axis=0, keepdims=True)

    gains[...] = jnp.zeros(gains.shape, F32)
    gain_in = unpack(0, mod9[...], div9[...])
    gain_query = unpack(9, mod2[...], div2[...])
    gain_key = unpack(11, mod2[...], div2[...])
    gain_mixed = unpack(13, mod9[...], div9[...])
    gain_ffn = unpack(22, mod9[...], div9[...])
    gain_branch = unpack(31, mod9[...], div9[...])
    gains[0:1, :] = gain_in
    gains[1:2, :] = gain_mixed
    gains[2:3, :] = gain_ffn
    gains[3:4, :] = gain_branch
    gains[4:5, 0:256] = gain_query
    gains[5:6, 0:256] = gain_key

    hidden_in = inputs[...].astype(F32)
    attn_in = norm_parts(hidden_in, gain_in)[0].astype(BF16)
    permuted = dot(attn_in, order, NN).astype(BF16)
    attn_p[...] = permuted
    cos_, sin_ = cosines[...], sines[...]

    def project(low_col, width):
        cols = slice(low_col, low_col + width)
        main = weights[0, :, :, :, :, :, cols].reshape(1024, width)
        out = dot(permuted[:, :1024], main, NN) + dot(permuted[:, 1024:], last_rows[:, cols], NN)
        qkv[:, cols] = out
        return out

    raw = project(1024, 512)
    key_own[...] = turn(norm_parts(raw[:, :256], gain_key)[0], cos_, sin_).astype(BF16)
    value_own[...] = raw[:, 256:].astype(BF16)
    keys[low, x_at] = key_own[...]
    values[low, x_at] = value_own[...]
    half = key_own.shape[0] // 2

    def cut(h):
        return pl.ds(h * half, half)

    def key_task():
        swap = net.send(key_own, keys.at[low, x_at], mirror)
        yield
        swap.wait_recv()
        yield from gather_ring(
            net, "x", lambda h: keys.at[:, x_at, cut(h)], lambda k, h: keys.at[:, k, cut(h)]
        )

    def value_task():
        yield from gather_ring(
            net, "x", lambda h: value_own.at[cut(h)], lambda k, h: values.at[low, k, cut(h)]
        )
        swap = net.send(values.at[low], values.at[low], mirror)
        yield
        swap.wait_recv()

    tasks = [key_task(), value_task()]
    for task in tasks:
        next(task)
    for h in range(HEADS):
        raw = project(h * 256, 256)
        query_low[:, h * 256 : (h + 1) * 256] = turn(
            norm_parts(raw, gain_query)[0], cos_, sin_
        ).astype(BF16)
    interleave(*tasks)
    progress()
    key_all = keys[...].reshape(1024, 256)
    value_all = values[...].reshape(1024, 256)
    keys_out[...] = key_all
    values_out[...] = value_all
    allowed = all_pos[...] <= own_pos[...]
    for h in range(HEADS):
        scores = dot(query_low[:, h * 256 : (h + 1) * 256], key_all, NT) * SCALE
        scores = jnp.where(allowed, scores, MASKED)
        expo = jnp.exp(scores - jnp.max(scores, axis=-1, keepdims=True))
        probs = expo / jnp.sum(expo, axis=-1, keepdims=True)
        probs_out[h] = probs
        mixed_out[:, h * 256 : (h + 1) * 256] = dot(probs.astype(BF16), value_all, NN).astype(BF16)
    progress()
    out_weight = weights[1, :, :, :, :, :, 0:1152].reshape(1024, 1152)
    mixed_by = dot(mixed_out[...], out_weight, NN)
    attn_out[...] = mixed_by
    resid = hidden_in + norm_parts(mixed_by, gain_mixed)[0]
    resid_out[...] = resid
    ffn_in[...] = norm_parts(resid, gain_ffn)[0].astype(BF16)
    while background:
        progress()
    save.wait()
    net.send_done()


def attention(own8, own_extra, ffn, inputs, own_pos, all_pos, cosines, sines, tables):
    rows, width = inputs.shape
    vmem, any_ = pltpu.VMEM, pl.ANY
    shape = jax.ShapeDtypeStruct
    wire = (2, 2, 4, 4, 2, 16, WIRE)
    return call(
        attention_kernel,
        "attention",
        [
            shape((3, 4, 4) + ffn.shape[1:], BF16),
            shape(wire, BF16),
            shape((128, WIRE), BF16),
            shape((8, width), F32),
            shape((rows, width), BF16),
            shape((rows, WIRE), F32),
            shape((rows, 1024), BF16),
            shape((1024, 256), BF16),
            shape((1024, 256), BF16),
            shape((HEADS, rows, 1024), F32),
            shape((rows, 1024), BF16),
            shape((rows, width), F32),
            shape((rows, width), F32),
            shape((rows, width), BF16),
        ],
        [vmem, vmem, any_] + [vmem] * 10,
        [any_, any_] + [vmem] * 12,
        sems(2 + 3 * 22 + 24 + 14)
        + [pltpu.SemaphoreType.DMA((2,))]
        + [
            vmem(wire, BF16),
            vmem(own8.shape, F32),
            vmem(own_extra.shape, BF16),
            vmem((16, WIRE), BF16),
            vmem((2048, 128), F32),
            vmem((rows, 256), BF16),
            vmem((rows, 256), BF16),
            vmem((2, 4, rows, 256), BF16),
            vmem((2, 4, rows, 256), BF16),
        ],
        1,
    )(own8, own_extra, ffn, inputs, own_pos, all_pos, cosines, sines, *tables)


class Cut:
    def __init__(self, ref, rows):
        self.ref, self.rows = ref, rows

    @property
    def at(self):
        return self

    def __getitem__(self, h):
        ref = self.ref.at[h]
        lead = (slice(None),) * (len(ref.shape) - 2)
        return ref.at[lead + (pl.ds(0, self.rows[h][1]),)]

    def __setitem__(self, h, value):
        self[h][...] = value


def backward_kernel(
    ffn_in_grad,
    cotangent,
    inputs,
    resid,
    attn_out,
    gains,
    weights,
    last_rows,
    attn_p,
    qkv,
    query_low,
    keys,
    values,
    probs,
    mixed,
    cosines,
    sines,
    ffn,
    branch_gain_grad,
    natural,
    mod9,
    div9,
    mod2,
    div2,
    inputs_grad,
    main_out,
    extra_out,
    ffn_out,
    send_sems,
    recv_sems,
    wire,
    paired,
    extras,
    final,
    glow,
    key_sum,
    value_sum,
    key_grads,
    value_grads,
    key_sent,
    key_pair,
    value_pair,
    *bufs,
):
    net = Net(send_sems, recv_sems)
    me = net.me
    sibling, mirror = net.sibling(), net.mirror()
    net.barrier(
        [net.neighbour(axis, by) for axis in "xyz" for by in (1, 3)] + [sibling]
    )
    core, low = me["core"], lax.rem(me["z"], 2)
    every = slice(None)
    bufs = list(bufs)

    def take(n):
        got = bufs[:n]
        del bufs[:n]
        return got

    def ffn_task(order, rows):
        first, second = order
        bufs1, result, bufs2 = take(4), take(1)[0], take(4)
        start = rows[0][0]

        def part(k, h):
            if first == "x":
                return ffn.at[:, :, k, pl.ds(*rows[h])]
            return ffn.at[:, k, :, pl.ds(*rows[h])]

        def total(h, terms):
            result[:, :, pl.ds(rows[h][0] - start, rows[h][1])] = add_up(terms).astype(BF16)

        def part2(k, h):
            return result.at[:, k, pl.ds(rows[h][0] - start, rows[h][1])]

        def total2(h, terms):
            ffn_out[:, pl.ds(*rows[h])] = add_up(terms)

        yield from scatter_ring(net, first, part, [Cut(b, rows) for b in bufs1], total)
        yield
        yield from scatter_ring(net, second, part2, [Cut(b, rows) for b in bufs2], total2)

    background = [ffn_task("xz", FFN_ROWS[0]), ffn_task("zx", FFN_ROWS[1])]

    def progress():
        for task in list(background):
            try:
                next(task)
            except StopIteration:
                background.remove(task)

    progress()
    gain_in, gain_mixed, gain_ffn = gains[0:1, :], gains[1:2, :], gains[2:3, :]
    gain_query, gain_key = gains[4:5, 0:256], gains[5:6, 0:256]
    cos_, sin_ = cosines[...], sines[...]

    resid_dv, ffn_gain_grad = norm_grad(resid[...], gain_ffn, ffn_in_grad[...])
    resid_grad = cotangent[...].astype(F32) + resid_dv
    inputs_grad[...] = resid_grad
    attn_dv, mixed_gain_grad = norm_grad(attn_out[...], gain_mixed, resid_grad)
    attn_grad = attn_dv.astype(BF16)
    out_weight = weights[1, :, :, :, :, :, 0:1152].reshape(1024, 1152)
    mixed_grad = dot(attn_grad, out_weight, NT).astype(BF16)
    key_all, value_all = keys[...], values[...]
    query_gain_grad = jnp.zeros((1, 256), F32)
    for h in range(HEADS):
        cols = slice(h * 256, (h + 1) * 256)
        mine = mixed_grad[:, cols]
        prob = probs[h]
        prob_grad = dot(mine, value_all, NT)
        delta = jnp.sum(prob_grad * prob, axis=-1, keepdims=True)
        score_grad = (prob * (prob_grad - delta)).astype(BF16)
        value_part = dot(prob.astype(BF16), mine, TN)
        key_part = dot(score_grad, query_low[:, cols], TN)
        if h == 0:
            value_sum[...] = value_part
            key_sum[...] = key_part
        else:
            value_sum[...] += value_part
            key_sum[...] += key_part
        rot_grad = dot(score_grad, key_all, NN) * SCALE
        raw_grad, gain_part = norm_grad(qkv[:, cols], gain_query, turn_back(rot_grad, cos_, sin_))
        query_gain_grad = query_gain_grad + gain_part
        glow[:, cols] = raw_grad.astype(BF16)
    rows = glow.shape[0]
    key_grads[...] = (key_sum[...] * SCALE).astype(BF16).reshape(2, 4, rows, 256)
    value_grads[...] = value_sum[...].astype(BF16).reshape(2, 4, rows, 256)
    half = rows // 2

    def cut(h):
        return pl.ds(h * half, half)

    done = {}

    def key_task():
        ring = take(4)

        def total(h, terms):
            key_sent[:, cut(h)] = add_up(terms).astype(BF16)

        yield from scatter_ring(net, "x", lambda k, h: key_grads.at[:, k, cut(h)], ring, total)
        swap = net.send(key_sent.at[1 - low], key_pair, mirror)
        yield
        swap.wait_recv()
        done["key"] = add_up((key_sent.at[low], key_pair))

    def value_task():
        ring = take(4)
        swap = net.send(value_grads.at[1 - low], value_pair, mirror)
        yield
        swap.wait_recv()
        value_pair[...] = add_up((value_pair, value_grads.at[low])).astype(BF16)
        sums = [None, None]

        def total(h, terms):
            sums[h] = add_up(terms)

        yield from scatter_ring(net, "x", lambda k, h: value_pair.at[k, cut(h)], ring, total)
        done["value"] = jnp.concatenate(sums, axis=0)

    tasks = [key_task(), value_task()]
    for task in tasks:
        next(task)
    for c in range(3):
        cols = slice(c * 384, (c + 1) * 384)
        wire[1, :, :, :, :, :, cols] = (
            dot(mixed[...], attn_grad[:, cols], TN).astype(BF16).reshape(2, 4, 4, 2, 16, 384)
        )
    interleave(*tasks)

    def weight_grad(low_col, width):
        cols = slice(low_col, low_col + width)
        out = dot(attn_p[...], glow[:, cols], TN)
        wire[0, :, :, :, :, :, cols] = out[:1024].astype(BF16).reshape(2, 4, 4, 2, 16, width)
        for j in range(low_col // 128, (low_col + width) // 128):
            extras[pl.ds(j, 128, stride=EXTRA), :] = out[
                1024:, j * 128 - low_col : (j + 1) * 128 - low_col
            ]

    extras[...] = jnp.zeros(extras.shape, F32)
    weight_grad(0, 512)
    weight_grad(512, 512)
    progress()
    key_raw_grad, key_gain_grad = norm_grad(
        qkv[:, 1024:1280], gain_key, turn_back(done["key"], cos_, sin_)
    )
    glow[:, 1024:1280] = key_raw_grad.astype(BF16)
    glow[:, 1280:1536] = done["value"].astype(BF16)
    weight_grad(1024, 512)
    main = weights[0].reshape(1024, WIRE)
    grad_p = jnp.concatenate(
        [dot(glow[...], main, NT), dot(glow[...], last_rows[...], NT)], axis=1
    )
    order = order_matrix(natural[...])
    high_part = grad_p.astype(BF16)
    low_part = (grad_p - high_part.astype(F32)).astype(BF16)
    attn_in_grad = dot(high_part, order, NT) + dot(low_part, order, NT)
    input_dv, in_gain_grad = norm_grad(inputs[...].astype(F32), gain_in, attn_in_grad)
    inputs_grad[...] += input_dv

    def pack(grad, offset, mod, div):
        width = mod.shape[1]
        placed = jnp.where(owned(width, div), grad, 0.0).astype(BF16)
        return dot(placed, spread(width, offset, mod), NT)

    packed = (
        pack(in_gain_grad, 0, mod9[...], div9[...])
        + pack(query_gain_grad, 9, mod2[...], div2[...])
        + pack(key_gain_grad, 11, mod2[...], div2[...])
        + pack(mixed_gain_grad, 13, mod9[...], div9[...])
        + pack(ffn_gain_grad, 22, mod9[...], div9[...])
        + pack(branch_gain_grad[...], 31, mod9[...], div9[...])
    )
    extras[pl.ds(GAIN_ROW, 128, stride=EXTRA), :] = packed
    for c in range(2):
        wire[1, :, :, :, :, :, 1152 + c * 128 : 1280 + c * 128] = (
            extras[c * 1024 : (c + 1) * 1024].astype(BF16).reshape(2, 4, 4, 2, 16, 128)
        )
    wire[1, :, :, :, :, :, 1408:1536] = jnp.zeros((2, 4, 4, 2, 16, 128), BF16)

    copies = []
    for p in range(3):
        cols = pl.ds(p * PIECE, PIECE)
        copies.append(
            net.send(
                wire.at[1 - core, :, :, :, :, :, cols], paired.at[:, :, :, :, :, cols], sibling
            )
        )

    def blob_task(order, p, copy):
        own_bufs = take(14)
        yield
        copy.wait_recv()
        cols = pl.ds(p * PIECE, PIECE)
        for a in range(2):
            for b in range(4):
                paired[a, b, :, :, :, cols] = add_up(
                    (paired.at[a, b, :, :, :, cols], wire.at[core, a, b, :, :, :, cols])
                ).astype(BF16)
        source, offset = paired, p * PIECE
        for count, axis in enumerate(order):
            have = order[count:]
            result = own_bufs[4] if count < 2 else None

            def part(k, h, source=source, offset=offset, have=have, axis=axis):
                return grid_at(
                    source, have, {axis: k}, (every, pl.ds(offset + h * (PIECE // 2), PIECE // 2))
                )

            def total(h, terms, result=result, count=count, have=have):
                if count < 2:
                    grid_at(
                        result, have[1:], {}, (every, pl.ds(h * (PIECE // 2), PIECE // 2))
                    )[...] = add_up(terms).astype(BF16)
                else:
                    final[core, :, pl.ds(p * PIECE + h * (PIECE // 2), PIECE // 2)] = add_up(terms)

            yield from scatter_ring(net, axis, part, own_bufs[:4], total)
            yield
            source, offset = result, 0
            own_bufs = own_bufs[5:]

    interleave(*(blob_task(order, p, copies[p]) for p, order in enumerate(ORDERS)), *background)
    swap = net.send(final.at[core], final.at[core], sibling)
    swap.wait_recv()
    mine8 = pl.ds(pl.multiple_of(core * 8, 8), 8)
    main_out[:, 0:WIRE] = final[0, mine8, :]
    main_out[:, WIRE:] = final[1, mine8, 0:1152]
    extra_out[...] = jnp.where(core == 0, final[1, :, 1152:1280], final[1, :, 1280:1408])
    net.send_done()


def attention_backward(args, ffn, tables):
    vmem = pltpu.VMEM
    shape = jax.ShapeDtypeStruct
    rows, width = args[0].shape
    wide = ffn.shape[-1]
    scratch = sems(24 + 14 + 3 * 19 + 1) + [
        vmem((2, 2, 4, 4, 2, 16, WIRE), BF16),
        vmem((2, 4, 4, 2, 16, WIRE), BF16),
        vmem((2048, 128), F32),
        vmem((2, 16, WIRE), F32),
        vmem((rows, WIRE), BF16),
        vmem((1024, 256), F32),
        vmem((1024, 256), F32),
        vmem((2, 4, rows, 256), BF16),
        vmem((2, 4, rows, 256), BF16),
        vmem((2, rows, 256), BF16),
        vmem((rows, 256), BF16),
        vmem((4, rows, 256), BF16),
    ]
    for own in FFN_ROWS:
        most = max(own[0][1], own[1][1])
        every = own[0][1] + own[1][1]
        scratch += [vmem((2, 3, 4, most, wide), BF16)] * 4
        scratch.append(vmem((3, 4, every, wide), BF16))
        scratch += [vmem((2, 3, most, wide), BF16)] * 4
    scratch += [vmem((2, 2, rows // 2, 256), BF16)] * 4
    scratch += [vmem((2, rows // 2, 256), BF16)] * 4
    for order in ORDERS:
        for count in range(3):
            left = lead_dims(order[count + 1 :])
            scratch += [vmem((2,) + left + (16, PIECE // 2), BF16)] * 4
            if count < 2:
                scratch.append(vmem(left + (16, PIECE), BF16))
    return call(
        backward_kernel,
        "attention_backward",
        [
            shape((rows, width), F32),
            shape((8, WIRE + 1152), F32),
            shape((EXTRA, 128), F32),
            shape((3,) + ffn.shape[3:], F32),
        ],
        [vmem] * 24,
        [vmem] * 4,
        scratch,
        2,
    )(*args, *tables)


class GatherRing:
    def __init__(self, net, axis, own, place):
        self.net, self.own, self.place = net, own, place
        self.mine = net.me[axis]
        self.left, self.right, self.far = (net.step(axis, by) for by in (3, 1, 2))
        self.to_left, self.to_right = net.neighbour(axis, 3), net.neighbour(axis, 1)

    def start(self):
        send, own, place, mine = self.net.send, self.own, self.place, self.mine
        self.r0 = send(own(0), place(mine, 0), self.to_right)
        self.l1 = send(own(1), place(mine, 1), self.to_left)
        self.r1 = send(own(1), place(mine, 1), self.to_right)
        self.l0 = send(own(0), place(mine, 0), self.to_left)

    def pass_on(self):
        send, place = self.net.send, self.place
        self.r0.wait_recv()
        self.f0 = send(place(self.left, 0), place(self.left, 0), self.to_right)
        self.l1.wait_recv()
        self.f1 = send(place(self.right, 1), place(self.right, 1), self.to_left)

    def wait_far(self):
        self.f0.wait_recv()
        self.f1.wait_recv()


class SumRing:
    def __init__(self, net, axis, part, bufs):
        self.net, self.part = net, part
        self.mine = net.me[axis]
        self.left, self.right, self.far = (net.step(axis, by) for by in (3, 1, 2))
        self.to_left, self.to_right = net.neighbour(axis, 3), net.neighbour(axis, 1)
        self.from_left, self.from_right, self.hold, self.stage = bufs

    def send_far(self):
        self.a0 = self.net.send(self.part(self.far, 0), self.hold.at[0], self.to_right)
        self.a1 = self.net.send(self.part(self.far, 1), self.hold.at[1], self.to_left)

    def send_right(self):
        self.r1 = self.net.send(self.part(self.right, 1), self.from_left.at[1], self.to_right)

    def send_left(self):
        self.l0 = self.net.send(self.part(self.left, 0), self.from_right.at[0], self.to_left)

    def pass_on(self):
        self.a0.wait_recv()
        self.stage[0] = add_up((self.part(self.right, 0), self.hold.at[0])).astype(BF16)
        self.r0 = self.net.send(self.stage.at[0], self.from_left.at[0], self.to_right)
        self.a1.wait_recv()
        self.stage[1] = add_up((self.part(self.left, 1), self.hold.at[1])).astype(BF16)
        self.l1 = self.net.send(self.stage.at[1], self.from_right.at[1], self.to_left)

    def total(self, h):
        if h == 0:
            self.l0.wait_recv()
            self.r0.wait_recv()
        else:
            self.r1.wait_recv()
            self.l1.wait_recv()
        return add_up((self.part(self.mine, h), self.from_left.at[h], self.from_right.at[h]))


def gelu_parts(u):
    root = 0.7978845608028654
    square = u * u
    th = jnp.tanh(root * u * (1.0 + 0.044715 * square))
    half = 0.5 * (1.0 + th)
    slope = half + 0.5 * u * (1.0 - th * th) * (root * (1.0 + 3 * 0.044715 * square))
    return u * half, slope


def ffn_kernel(
    own,
    weights,
    resid,
    cotangent,
    gain,
    outputs,
    back,
    gain_grad,
    weight_grads,
    send_sems,
    recv_sems,
    tokens,
    grads,
    act,
    slope,
    hidden,
    gate_g,
    up_g,
    branch,
    *bufs,
):
    net = Net(send_sems, recv_sems)
    me = net.me
    sibling = net.sibling()
    net.barrier([net.neighbour("y", 1), net.neighbour("y", 3), sibling])
    core, y = me["core"], me["y"]
    rows, width = own.shape
    half = rows // 2

    def cut(h):
        return pl.ds(h * half, half)

    def phase(source, held, run, bufs, meanwhile):
        parts, paired, ring_bufs = bufs[0], bufs[1], bufs[2:]
        gather = GatherRing(
            net, "y", lambda h: source.at[cut(h)], lambda k, h: held.at[k, core, cut(h)]
        )
        gather.start()
        swap = net.send(source, held.at[y, core], sibling)
        held[y, core] = source[...]
        left, right, far = gather.left, gather.right, gather.far

        def across(k):
            return net.send(held.at[k, core], held.at[k, core], sibling)

        def give(k):
            return net.send(parts.at[k, 1 - core], paired.at[k], sibling)

        def pair(k, copy):
            copy.wait_recv()
            paired[k] = add_up((paired.at[k], parts.at[k, core])).astype(BF16)

        sums = SumRing(net, "y", lambda k, h: paired.at[k, cut(h)], ring_bufs)
        swap.wait_recv()
        parts[y] = run(y)
        pair_own = give(y)
        gather.pass_on()
        gather.r1.wait_recv()
        swap_left = across(left)
        gather.l0.wait_recv()
        swap_right = across(right)
        swap_left.wait_recv()
        parts[left] = run(left)
        pair_left = give(left)
        gather.wait_far()
        swap_far = across(far)
        pair(y, pair_own)
        swap_right.wait_recv()
        parts[right] = run(right)
        pair_right = give(right)
        pair(left, pair_left)
        sums.send_left()
        swap_far.wait_recv()
        parts[far] = run(far)
        pair_far = give(far)
        pair(right, pair_right)
        sums.send_right()
        pair(far, pair_far)
        sums.send_far()
        meanwhile(0)
        sums.pass_on()
        meanwhile(1)
        return sums

    def dot(left, right, dims):
        return lax.dot_general(left, right, (dims, ((), ())), preferred_element_type=F32)

    def forward(k):
        rows_k = tokens[k].reshape(2 * rows, width)
        total = None
        for j in range(2):
            gate = dot(rows_k, weights[0, j], ((1,), (0,)))
            upper = dot(rows_k, weights[1, j], ((1,), (0,)))
            value, diff = gelu_parts(gate)
            act[k, j] = value.astype(BF16)
            slope[k, j] = (diff * upper).astype(BF16)
            hidden_low = (value * upper).astype(BF16)
            hidden[k, j] = hidden_low
            out = dot(hidden_low, weights[2, j], ((1,), (1,)))
            total = out if total is None else total + out
        return total.astype(BF16).reshape(2, rows, width)

    def backward(k):
        rows_k = grads[k].reshape(2 * rows, width)
        total = None
        for j in range(2):
            hidden_grad = dot(rows_k, weights[2, j], ((1,), (0,)))
            gate_low = (hidden_grad * slope[k, j].astype(F32)).astype(BF16)
            up_low = (hidden_grad * act[k, j].astype(F32)).astype(BF16)
            gate_g[k, j] = gate_low
            up_g[k, j] = up_low
            out = dot(gate_low, weights[0, j], ((1,), (1,))) + dot(
                up_low, weights[1, j], ((1,), (1,))
            )
            total = out if total is None else total + out
        return total.astype(BF16).reshape(2, rows, width)

    def weight_grad(which, held, factor):
        flat = held[...].reshape(8 * rows, width)
        for j in range(2):
            weight_grads[which, j] = dot(
                flat, factor[:, j].reshape(8 * rows, factor.shape[-1]), ((0,), (0,))
            ).astype(BF16)

    sums = phase(own, tokens, forward, bufs[:6], lambda step: None)
    gain_f = gain[...]
    gain_total = jnp.zeros_like(gain_f)
    for h in range(2):
        raw = sums.total(h)
        upstream = cotangent[cut(h)].astype(F32)
        scale = lax.rsqrt(jnp.mean(raw * raw, axis=-1, keepdims=True) + EPS)
        normed = raw * scale
        outputs[cut(h)] = resid[cut(h)] + normed * gain_f
        scaled = upstream * gain_f
        gain_total = gain_total + jnp.sum(upstream * normed, axis=0, keepdims=True)
        inner = jnp.mean(scaled * normed, axis=-1, keepdims=True)
        branch[cut(h)] = (scale * (scaled - normed * inner)).astype(BF16)
    gain_grad[...] = gain_total

    def meanwhile(step):
        if step == 0:
            weight_grad(2, grads, hidden)
        else:
            weight_grad(0, tokens, gate_g)
            weight_grad(1, tokens, up_g)

    sums = phase(branch, grads, backward, bufs[6:], meanwhile)
    for h in range(2):
        back[cut(h)] = sums.total(h)
    net.send_done()


def feed_forward(own, weights, resid, cotangent, gain):
    rows, width = own.shape
    wide = weights.shape[-1]
    vmem = pltpu.VMEM
    phase_bufs = [
        pltpu.VMEM((4, 2, rows, width), BF16),
        pltpu.VMEM((4, rows, width), BF16),
    ] + [pltpu.VMEM((2, rows // 2, width), BF16)] * 4
    return call(
        ffn_kernel,
        "feed_forward",
        [
            jax.ShapeDtypeStruct((rows, width), F32),
            jax.ShapeDtypeStruct((rows, width), F32),
            jax.ShapeDtypeStruct((1, width), F32),
            jax.ShapeDtypeStruct(weights.shape, BF16),
        ],
        [vmem] * 5,
        [vmem] * 4,
        sems(40)
        + [pltpu.VMEM((4, 2, rows, width), BF16)] * 2
        + [pltpu.VMEM((4, 2, 2 * rows, wide), BF16)] * 5
        + [pltpu.VMEM((rows, width), BF16)]
        + phase_bufs * 2,
        5,
    )(own, weights, resid, cotangent, gain)


def body(
    inputs,
    pair_order,
    attn_gain,
    query_gain,
    key_gain,
    mixer_gain,
    ffn_gain,
    branch_gain,
    query_weight,
    key_weight,
    value_weight,
    output_weight,
    gate_weight,
    up_weight,
    down_weight,
    cotangent,
):
    gains = (attn_gain, query_gain, key_gain, mixer_gain, ffn_gain, branch_gain)
    width = inputs.shape[2]
    rows = inputs.shape[1]
    head_dim = key_weight.shape[1]
    qw = query_weight.shape[1]
    gain_row = jnp.concatenate(gains)
    n_gain = gain_row.shape[0]
    own8 = jnp.concatenate(
        [query_weight[:8], key_weight[:8], value_weight[:8], output_weight], axis=1
    ).astype(F32)
    own_extra = jnp.concatenate(
        [
            query_weight[8:].reshape(8, 128),
            key_weight[8:].reshape(2, 128),
            value_weight[8:].reshape(2, 128),
            jnp.pad(gain_row, (0, 128 - n_gain))[None],
            jnp.zeros((3, 128), BF16),
        ]
    )
    ffn_own = jnp.stack([gate_weight, up_weight, down_weight.T])
    every = np.arange(width)
    last = every - 1024
    natural = np.where(
        every < 1024,
        9 * (every // 8) + every % 8,
        9 * (2 * (last % 64) + last // 64) + 8,
    )
    pairs = np.arange(256)
    tables = [
        jnp.asarray(t[None].astype(np.int32))
        for t in (natural, every % 9, every // 9, pairs % 2, pairs // 2)
    ]
    slot = lax.axis_index("ctx")
    all_positions = token_positions(pair_order[0], rows).reshape(-1)
    own_positions = lax.dynamic_slice_in_dim(all_positions, slot * rows, rows)
    angle = angles(own_positions, head_dim)
    cosines = jnp.cos(angle)
    sines = jnp.sin(angle)
    (
        all_ffn,
        weights,
        last_rows,
        gain_rows,
        attn_p,
        qkv,
        query_low,
        key_all,
        value_all,
        probs,
        mixed_low,
        attn_out,
        resid,
        ffn_input,
    ) = attention(
        own8,
        own_extra,
        ffn_own,
        inputs[0],
        own_positions[:, None],
        all_positions[None],
        cosines,
        sines,
        tables,
    )
    ff_own = gate_weight.shape[1]
    outputs, grad_ffn_input, grad_gain_branch, ffn_grads = feed_forward(
        ffn_input, all_ffn.reshape(3, 2, width, ff_own), resid, cotangent[0], gain_rows[3:4]
    )
    ffn_grads = ffn_grads.reshape(3, 4, 4, width // 8, ff_own)
    inputs_grad, main_sum, extra_sum, ffn_sum = attention_backward(
        (
            grad_ffn_input,
            cotangent[0],
            inputs[0],
            resid,
            attn_out,
            gain_rows,
            weights,
            last_rows,
            attn_p,
            qkv,
            query_low,
            key_all,
            value_all,
            probs,
            mixed_low,
            cosines,
            sines,
            ffn_grads,
            grad_gain_branch,
        ),
        ffn_grads,
        tables,
    )
    gain_sums = []
    at = 0
    for gain in gains:
        gain_sums.append(extra_sum[GAIN_ROW, at : at + gain.shape[0]])
        at += gain.shape[0]

    def nine(first, wide, extra):
        return jnp.concatenate(
            [main_sum[:, first : first + wide], extra_sum[extra : extra + wide // 128].reshape(1, wide)]
        )

    return (
        outputs[None],
        inputs_grad[None],
        *gain_sums,
        nine(0, qw, 0),
        nine(qw, head_dim, 8),
        nine(qw + head_dim, head_dim, 10),
        main_sum[:, WIRE:],
        ffn_sum[0],
        ffn_sum[1],
        ffn_sum[2].T,
    )


def solution(mesh):
    placed = (
        P("fsdp", "ctx", None),
        P("fsdp", None),
        P(("ctx", "fsdp")),
        P(("ctx", "fsdp")),
        P(("ctx", "fsdp")),
        P(("ctx", "fsdp")),
        P(("ctx", "fsdp")),
        P(("ctx", "fsdp")),
        P(("ctx", "fsdp"), None),
        P(("ctx", "fsdp"), None),
        P(("ctx", "fsdp"), None),
        P(("ctx", "fsdp"), None),
        P("ctx", "fsdp"),
        P("ctx", "fsdp"),
        P("fsdp", "ctx"),
        P("fsdp", "ctx", None),
    )
    return jax.shard_map(
        body,
        mesh=mesh,
        in_specs=placed,
        out_specs=(
            P("fsdp", "ctx", None),
            P("fsdp", "ctx", None),
            P(("ctx", "fsdp")),
            P(("ctx", "fsdp")),
            P(("ctx", "fsdp")),
            P(("ctx", "fsdp")),
            P(("ctx", "fsdp")),
            P(("ctx", "fsdp")),
            P(("ctx", "fsdp"), None),
            P(("ctx", "fsdp"), None),
            P(("ctx", "fsdp"), None),
            P(("ctx", "fsdp"), None),
            P("ctx", "fsdp"),
            P("ctx", "fsdp"),
            P("fsdp", "ctx"),
        ),
        check_vma=False,
    )
```

```python
import jax
import jax.numpy as jnp
import numpy as np
from jax import lax
from jax.experimental import pallas as pl
from jax.experimental.pallas import tpu as pltpu
from jax.sharding import PartitionSpec as P

EPS = 1e-06
SCALE = 0.0625
BASE = 1000000.0
MASKED = -1e30
BF16 = jnp.bfloat16
F32 = jnp.float32
VMEM_BYTES = 56 * 1024 * 1024


def here():
    ctx = lax.axis_index("ctx")
    fsdp = lax.axis_index("fsdp")
    return {
        "x": lax.rem(ctx, 4),
        "y": lax.div(fsdp, 4),
        "z": lax.rem(lax.div(fsdp, 2), 2) * 2 + lax.div(ctx, 4),
        "core": lax.rem(fsdp, 2),
    }


class Net:
    def __init__(self, send_sems, recv_sems):
        self.me = here()
        self.send_sems, self.recv_sems = send_sems, recv_sems
        self.used = 0
        self.sent = []

    def device(self, **moved):
        at = {**self.me, **moved}
        return (
            lax.rem(at["z"], 2) * 4 + at["x"],
            at["y"] * 4 + lax.div(at["z"], 2) * 2 + at["core"],
        )

    def step(self, axis, by):
        return lax.rem(self.me[axis] + by, 4)

    def neighbour(self, axis, by):
        return self.device(**{axis: self.step(axis, by)})

    def sibling(self):
        return self.device(core=1 - self.me["core"])

    def mirror(self):
        z = self.me["z"]
        return self.device(z=z + 1 - 2 * lax.rem(z, 2))

    def barrier(self, peers, meanwhile=None):
        sem = pltpu.get_barrier_semaphore()
        for peer in peers:
            pl.semaphore_signal(sem, inc=1, device_id=peer, device_id_type=pl.DeviceIdType.MESH)
        if meanwhile:
            meanwhile()
        pl.semaphore_wait(sem, len(peers))

    def send(self, src, dst, peer):
        n = self.used
        self.used += 1
        copy = pltpu.make_async_remote_copy(
            src_ref=src,
            dst_ref=dst,
            send_sem=self.send_sems.at[n],
            recv_sem=self.recv_sems.at[n],
            device_id=peer,
            device_id_type=pl.DeviceIdType.MESH,
        )
        copy.start()
        self.sent.append(copy)
        return copy

    def send_done(self):
        for copy in self.sent:
            copy.wait_send()


def interleave(*tasks):
    tasks = list(tasks)
    while tasks:
        for task in list(tasks):
            try:
                next(task)
            except StopIteration:
                tasks.remove(task)


def gather_ring(net, axis, own, place, arrived=None):
    mine = net.me[axis]
    left, right, far = net.step(axis, 3), net.step(axis, 1), net.step(axis, 2)
    to_left, to_right = net.neighbour(axis, 3), net.neighbour(axis, 1)
    r0 = net.send(own(0), place(mine, 0), to_right)
    l1 = net.send(own(1), place(mine, 1), to_left)
    r1 = net.send(own(1), place(mine, 1), to_right)
    l0 = net.send(own(0), place(mine, 0), to_left)
    yield
    r0.wait_recv()
    f0 = net.send(place(left, 0), place(left, 0), to_right)
    yield
    l1.wait_recv()
    f1 = net.send(place(right, 1), place(right, 1), to_left)
    yield
    r1.wait_recv()
    if arrived:
        arrived(left)
    yield
    l0.wait_recv()
    if arrived:
        arrived(right)
    yield
    f0.wait_recv()
    f1.wait_recv()
    if arrived:
        arrived(far)


def scatter_ring(net, axis, part, bufs, total):
    mine = net.me[axis]
    left, right, far = net.step(axis, 3), net.step(axis, 1), net.step(axis, 2)
    to_left, to_right = net.neighbour(axis, 3), net.neighbour(axis, 1)
    from_left, from_right, hold, stage = bufs
    a0 = net.send(part(far, 0), hold.at[0], to_right)
    a1 = net.send(part(far, 1), hold.at[1], to_left)
    r1 = net.send(part(right, 1), from_left.at[1], to_right)
    l0 = net.send(part(left, 0), from_right.at[0], to_left)
    yield
    a0.wait_recv()
    stage[0] = add_up((part(right, 0), hold.at[0])).astype(BF16)
    r0 = net.send(stage.at[0], from_left.at[0], to_right)
    yield
    a1.wait_recv()
    stage[1] = add_up((part(left, 1), hold.at[1])).astype(BF16)
    l1 = net.send(stage.at[1], from_right.at[1], to_left)
    yield
    l0.wait_recv()
    r0.wait_recv()
    total(0, (part(mine, 0), from_left.at[0], from_right.at[0]))
    yield
    r1.wait_recv()
    l1.wait_recv()
    total(1, (part(mine, 1), from_left.at[1], from_right.at[1]))


def add_up(terms):
    out = terms[0][...].astype(F32)
    for term in terms[1:]:
        out = out + term[...].astype(F32)
    return out


def sems(count):
    return [pltpu.SemaphoreType.DMA((count,)), pltpu.SemaphoreType.DMA((count,))]


def call(kernel, name, out_shape, in_spaces, out_spaces, scratch, number):
    return pl.pallas_call(
        kernel,
        name=name,
        out_shape=out_shape,
        in_specs=[pl.BlockSpec(memory_space=space) for space in in_spaces],
        out_specs=[pl.BlockSpec(memory_space=space) for space in out_spaces],
        scratch_shapes=scratch,
        compiler_params=pltpu.CompilerParams(
            collective_id=number, has_side_effects=True, vmem_limit_bytes=VMEM_BYTES
        ),
    )


ORDERS = ("xyz", "yzx", "zxy")
FFN_ROWS = (((0, 48), (48, 32)), ((80, 32), (112, 32)))
HEADS = 4
EXTRA = 16
GAIN_ROW = 12
WIRE = 1536
PIECE = WIRE // 3


def grid_at(ref, have, sel, tail):
    index = []
    every = slice(None)
    if "z" in have:
        index.append(lax.rem(sel["z"], 2) if "z" in sel else every)
    for axis in "xy":
        if axis in have:
            index.append(sel.get(axis, every))
    if "z" in have:
        index.append(lax.div(sel["z"], 2) if "z" in sel else every)
    return ref.at[tuple(index) + tail]


def lead_dims(have):
    dims = []
    if "z" in have:
        dims.append(2)
    dims += [4 for axis in "xy" if axis in have]
    if "z" in have:
        dims.append(2)
    return tuple(dims)


def dot(left, right, dims):
    return lax.dot_general(left, right, (dims, ((), ())), preferred_element_type=F32)


NN = ((1,), (0,))
NT = ((1,), (1,))
TN = ((0,), (0,))


def spread(width, offset, mod):
    lane = lax.broadcasted_iota(jnp.int32, (128, width), 0)
    return jnp.where(lane == offset + mod, 1.0, 0.0).astype(BF16)


def owned(width, div):
    row = lax.broadcasted_iota(jnp.int32, (128, width), 0)
    device = jnp.where(row < 64, 2 * row, 2 * row - 127)
    return device == div


def order_matrix(natural):
    width = natural.shape[1]
    row = lax.broadcasted_iota(jnp.int32, (width, width), 0)
    return jnp.where(row == natural, 1.0, 0.0).astype(BF16)


def unit(n):
    row = lax.broadcasted_iota(jnp.int32, (n, n), 0)
    column = lax.broadcasted_iota(jnp.int32, (n, n), 1)
    return jnp.where(row == column, 1.0, 0.0).astype(BF16)


def norm_parts(v, gain):
    scale = lax.rsqrt(jnp.mean(v * v, axis=-1, keepdims=True) + EPS)
    normed = v * scale
    return normed * gain, normed, scale


def norm_grad(v, gain, dy):
    _, normed, scale = norm_parts(v, gain)
    scaled = dy * gain
    inner = jnp.mean(scaled * normed, axis=-1, keepdims=True)
    return scale * (scaled - normed * inner), jnp.sum(dy * normed, axis=0, keepdims=True)


def turn(v, cosines, sines):
    a, b = v[:, :128], v[:, 128:]
    return jnp.concatenate([a * cosines - b * sines, b * cosines + a * sines], axis=1)


def turn_back(v, cosines, sines):
    a, b = v[:, :128], v[:, 128:]
    return jnp.concatenate([a * cosines + b * sines, b * cosines - a * sines], axis=1)


def attention_kernel(
    query_w,
    key_w,
    value_w,
    output_w,
    gate_w,
    up_w,
    down_w,
    inputs,
    gain_row,
    pairs,
    rope,
    natural,
    mod9,
    div9,
    mod2,
    div2,
    all_ffn,
    weights_out,
    cosines,
    sines,
    last_rows,
    gains,
    attn_p,
    qkv,
    query_low,
    keys_out,
    values_out,
    probs_out,
    mixed_out,
    attn_out,
    resid_out,
    ffn_in,
    send_sems,
    recv_sems,
    local_sems,
    weights,
    ffn,
    own8,
    own_extra,
    other8,
    other_extra,
    start,
    extras,
    key_own,
    value_own,
    keys,
    values,
):
    net = Net(send_sems, recv_sems)
    me = net.me
    sibling, mirror = net.sibling(), net.mirror()

    def prepare():
        at = 0
        for ref in (query_w, key_w, value_w, output_w):
            whole = ref[...].astype(F32)
            wide = whole.shape[1]
            own8[:, at : at + wide] = whole[:8]
            if whole.shape[0] > 8:
                for j in range(wide // 128):
                    row = at // 128 + j
                    own_extra[row : row + 1, :] = whole[8:, j * 128 : (j + 1) * 128]
            at += wide
        own_extra[GAIN_ROW : GAIN_ROW + 1, :] = gain_row[...]
        own_extra[GAIN_ROW + 1 :, :] = jnp.zeros((EXTRA - GAIN_ROW - 1, 128), F32)
        ffn[0] = gate_w[...]
        ffn[1] = up_w[...]
        ffn[2] = dot(unit(down_w.shape[1]), down_w[...], NT).astype(BF16)

    net.barrier(
        [net.neighbour(axis, by) for axis in "xyz" for by in (1, 3)] + [sibling], prepare
    )
    core, x_at, low = me["core"], me["x"], lax.rem(me["z"], 2)
    swap8 = net.send(own8, other8, sibling)
    swap_extra = net.send(own_extra, other_extra, sibling)
    own_ffn = pltpu.make_async_copy(ffn, all_ffn.at[:, me["z"], x_at], local_sems.at[0])
    own_ffn.start()
    forwards = []

    def piece(p, h):
        return pl.ds(p * PIECE + h * (PIECE // 2), PIECE // 2)

    every = slice(None)

    def blob_task(order, p):
        both = pl.ds(p * PIECE, PIECE)
        held = weights.at[core]
        for count, axis in enumerate(order):
            fixed = {k: me[k] for k in order[count + 1 :]}

            def place(k, h):
                return grid_at(held, "xyz", {**fixed, axis: k}, (every, piece(p, h)))

            def own(h):
                if count == 0:
                    return start.at[:, piece(p, h)]
                return place(me[axis], h)

            def forward(k):
                ref = grid_at(held, "xyz", {**fixed, axis: k}, (every, both))
                forwards.append(net.send(ref, ref, sibling))

            if count == 2:
                forward(me[axis])
            yield from gather_ring(net, axis, own, place, forward if count == 2 else None)
            yield

    def ffn_rings(axes, source):
        rings = []
        for axis, rows in zip(axes, FFN_ROWS):
            other = "z" if axis == "x" else "x"
            fixed = me[other] if source is ffn else every

            def spot(k, h, axis=axis, rows=rows, fixed=fixed):
                ix, iz = (k, fixed) if axis == "x" else (fixed, k)
                return all_ffn.at[:, iz, ix, pl.ds(*rows[h])]

            def own(h, axis=axis, rows=rows, spot=spot):
                return ffn.at[:, pl.ds(*rows[h])] if source is ffn else spot(me[axis], h)

            rings.append(GatherRing(net, axis, own, spot))
        return rings

    def ffn_task():
        first = ffn_rings("xz", ffn)
        for ring in first:
            ring.start()
        for _ in range(6):
            yield
        for ring in first:
            ring.pass_on()
        for _ in range(6):
            yield
        for ring in first:
            ring.finish()
        own_ffn.wait()
        second = ffn_rings("zx", None)
        for ring in second:
            ring.start()
        for _ in range(6):
            yield
        for ring in second:
            ring.pass_on()
        yield
        for ring in second:
            ring.finish()

    swap8.wait_recv()
    swap_extra.wait_recv()
    first = core == 0
    mine8, theirs8 = own8[...], other8[...]
    chip = jnp.concatenate(
        [jnp.where(first, mine8, theirs8), jnp.where(first, theirs8, mine8)], axis=0
    )
    mine_x, theirs_x = own_extra[...], other_extra[...]
    half1 = jnp.concatenate(
        [
            chip[:, WIRE:],
            jnp.where(first, mine_x, theirs_x),
            jnp.where(first, theirs_x, mine_x),
            jnp.zeros((16, 2 * WIRE - chip.shape[1] - 256), F32),
        ],
        axis=1,
    )
    block = jnp.where(first, chip[:, :WIRE], half1).astype(BF16)
    start[...] = block
    weights[core, low, x_at, me["y"], lax.div(me["z"], 2)] = block

    background = ffn_task()
    blob_tasks = [blob_task(order, p) for p, order in enumerate(ORDERS)]
    for turn_ in range(18):
        for task in blob_tasks:
            next(task)
        next(background)
    for task in blob_tasks:
        next(task, None)
    order = order_matrix(natural[...])
    for copy in forwards:
        copy.wait_recv()
    save = pltpu.make_async_copy(weights, weights_out, local_sems.at[1])
    save.start()
    for c in range(2):
        extras[c * 1024 : (c + 1) * 1024] = (
            weights[1, :, :, :, :, :, 1152 + c * 128 : 1280 + c * 128]
            .reshape(1024, 128)
            .astype(F32)
        )

    def extra_row(j):
        return extras[pl.ds(j, 128, stride=EXTRA), :].astype(BF16)

    for j in range(12):
        last_rows[:, j * 128 : (j + 1) * 128] = extra_row(j)
    packed = extra_row(GAIN_ROW)

    def unpack(offset, mod, div):
        wide = dot(packed, spread(mod.shape[1], offset, mod), NN)
        return jnp.sum(jnp.where(owned(mod.shape[1], div), wide, 0.0), axis=0, keepdims=True)

    gains[...] = jnp.zeros(gains.shape, F32)
    gain_in = unpack(0, mod9[...], div9[...])
    gain_query = unpack(9, mod2[...], div2[...])
    gain_key = unpack(11, mod2[...], div2[...])
    gain_mixed = unpack(13, mod9[...], div9[...])
    gain_ffn = unpack(22, mod9[...], div9[...])
    gain_branch = unpack(31, mod9[...], div9[...])
    gains[0:1, :] = gain_in
    gains[1:2, :] = gain_mixed
    gains[2:3, :] = gain_ffn
    gains[3:4, :] = gain_branch
    gains[4:5, 0:256] = gain_query
    gains[5:6, 0:256] = gain_key

    hidden_in = inputs[...].astype(F32)
    attn_in = norm_parts(hidden_in, gain_in)[0].astype(BF16)
    permuted = dot(attn_in, order, NN).astype(BF16)
    attn_p[...] = permuted
    block = pairs[0, lax.axis_index("ctx")]
    index = lax.broadcasted_iota(jnp.int32, (16, 128), 0)
    cos_, sin_ = [], []
    for b in (block, 15 - block):
        cb, sb = (
            jnp.sum(jnp.where(index == b, rope[i, 64:80, :], 0.0), axis=0, keepdims=True)
            for i in range(2)
        )
        cj, sj = rope[0, 0:64, :], rope[1, 0:64, :]
        cos_.append(cj * cb - sj * sb)
        sin_.append(sj * cb + cj * sb)
    cos_, sin_ = jnp.concatenate(cos_, axis=0), jnp.concatenate(sin_, axis=0)
    cosines[...] = cos_
    sines[...] = sin_

    def project(low_col, width):
        cols = slice(low_col, low_col + width)
        main = weights[0, :, :, :, :, :, cols].reshape(1024, width)
        out = dot(permuted[:, :1024], main, NN) + dot(permuted[:, 1024:], last_rows[:, cols], NN)
        qkv[:, cols] = out
        return out

    raw = project(1024, 512)
    key_own[...] = turn(norm_parts(raw[:, :256], gain_key)[0], cos_, sin_).astype(BF16)
    value_own[...] = raw[:, 256:].astype(BF16)
    keys[low, x_at] = key_own[...]
    values[low, x_at] = value_own[...]
    half = key_own.shape[0] // 2

    def cut(h):
        return pl.ds(h * half, half)

    def key_task():
        swap = net.send(key_own, keys.at[low, x_at], mirror)
        yield
        swap.wait_recv()
        yield from gather_ring(
            net, "x", lambda h: keys.at[:, x_at, cut(h)], lambda k, h: keys.at[:, k, cut(h)]
        )

    def value_task():
        yield from gather_ring(
            net, "x", lambda h: value_own.at[cut(h)], lambda k, h: values.at[low, k, cut(h)]
        )
        swap = net.send(values.at[low], values.at[low], mirror)
        yield
        swap.wait_recv()

    tasks = [key_task(), value_task()]
    for task in tasks:
        next(task)
    for h in range(HEADS):
        raw = project(h * 256, 256)
        query_low[:, h * 256 : (h + 1) * 256] = turn(
            norm_parts(raw, gain_query)[0], cos_, sin_
        ).astype(BF16)
    next(background)
    interleave(*tasks)
    key_all = keys[...].reshape(1024, 256)
    value_all = values[...].reshape(1024, 256)
    keys_out[...] = key_all
    values_out[...] = value_all

    def position(i, b):
        return jnp.where(i < 64, b * 64 + i, (15 - b) * 64 + i - 64)

    lane = lax.broadcasted_iota(jnp.int32, (1, 128), 1)
    all_pos = jnp.concatenate([position(lane, pairs[0, c]) for c in range(8)], axis=1)
    own_pos = position(lax.broadcasted_iota(jnp.int32, (128, 1), 0), block)
    allowed = all_pos <= own_pos
    for h in range(HEADS):
        scores = dot(query_low[:, h * 256 : (h + 1) * 256], key_all, NT) * SCALE
        scores = jnp.where(allowed, scores, MASKED)
        expo = jnp.exp(scores - jnp.max(scores, axis=-1, keepdims=True))
        probs = expo / jnp.sum(expo, axis=-1, keepdims=True)
        probs_out[h] = probs
        mixed_out[:, h * 256 : (h + 1) * 256] = dot(probs.astype(BF16), value_all, NN).astype(BF16)
    out_weight = weights[1, :, :, :, :, :, 0:1152].reshape(1024, 1152)
    mixed_by = dot(mixed_out[...], out_weight, NN)
    attn_out[...] = mixed_by
    resid = hidden_in + norm_parts(mixed_by, gain_mixed)[0]
    resid_out[...] = resid
    ffn_in[...] = norm_parts(resid, gain_ffn)[0].astype(BF16)
    next(background, None)
    save.wait()
    net.send_done()


def attention(projections, ffn, inputs, gain_row, pairs, rope, tables):
    rows, width = inputs.shape
    vmem, any_ = pltpu.VMEM, pl.ANY
    shape = jax.ShapeDtypeStruct
    wire = (2, 2, 4, 4, 2, 16, WIRE)
    return call(
        attention_kernel,
        "attention",
        [
            shape((3, 4, 4) + ffn[0].shape, BF16),
            shape(wire, BF16),
            shape((rows, 128), F32),
            shape((rows, 128), F32),
            shape((128, WIRE), BF16),
            shape((8, width), F32),
            shape((rows, width), BF16),
            shape((rows, WIRE), F32),
            shape((rows, 1024), BF16),
            shape((1024, 256), BF16),
            shape((1024, 256), BF16),
            shape((HEADS, rows, 1024), F32),
            shape((rows, 1024), BF16),
            shape((rows, width), F32),
            shape((rows, width), F32),
            shape((rows, width), BF16),
        ],
        [vmem] * 9 + [pltpu.SMEM] + [vmem] * 6,
        [any_, any_] + [vmem] * 14,
        sems(2 + 3 * 22 + 24 + 14)
        + [pltpu.SemaphoreType.DMA((2,))]
        + [
            vmem(wire, BF16),
            vmem((3,) + ffn[0].shape, BF16),
            vmem((8, WIRE + width), F32),
            vmem((EXTRA, 128), F32),
            vmem((8, WIRE + width), F32),
            vmem((EXTRA, 128), F32),
            vmem((16, WIRE), BF16),
            vmem((2048, 128), F32),
            vmem((rows, 256), BF16),
            vmem((rows, 256), BF16),
            vmem((2, 4, rows, 256), BF16),
            vmem((2, 4, rows, 256), BF16),
        ],
        1,
    )(*projections, *ffn, inputs, gain_row, pairs, rope, *tables)


class Cut:
    def __init__(self, ref, rows):
        self.ref, self.rows = ref, rows

    @property
    def at(self):
        return self

    def __getitem__(self, h):
        ref = self.ref.at[h]
        lead = (slice(None),) * (len(ref.shape) - 2)
        return ref.at[lead + (pl.ds(0, self.rows[h][1]),)]

    def __setitem__(self, h, value):
        self[h][...] = value


def backward_kernel(
    ffn_in_grad,
    cotangent,
    inputs,
    resid,
    attn_out,
    gains,
    weights,
    last_rows,
    attn_p,
    qkv,
    query_low,
    keys,
    values,
    probs,
    mixed,
    cosines,
    sines,
    ffn,
    branch_gain_grad,
    natural,
    mod9,
    div9,
    mod2,
    div2,
    inputs_grad,
    gains_out,
    query_out,
    key_out,
    value_out,
    output_out,
    gate_out,
    up_out,
    down_out,
    send_sems,
    recv_sems,
    down_sum,
    wire,
    paired,
    extras,
    final,
    glow,
    key_sum,
    value_sum,
    key_grads,
    value_grads,
    key_sent,
    key_pair,
    value_pair,
    *bufs,
):
    net = Net(send_sems, recv_sems)
    me = net.me
    sibling, mirror = net.sibling(), net.mirror()
    net.barrier(
        [net.neighbour(axis, by) for axis in "xyz" for by in (1, 3)] + [sibling]
    )
    core, low = me["core"], lax.rem(me["z"], 2)
    every = slice(None)
    bufs = list(bufs)

    def take(n):
        got = bufs[:n]
        del bufs[:n]
        return got

    def ffn_task():
        plans = []
        for axis, rows in zip("xz", FFN_ROWS):
            bufs1, result, bufs2 = take(4), take(1)[0], take(4)
            start = rows[0][0]

            def part(k, h, axis=axis, rows=rows):
                if axis == "x":
                    return ffn.at[:, :, k, pl.ds(*rows[h])]
                return ffn.at[:, k, :, pl.ds(*rows[h])]

            def part2(k, h, rows=rows, result=result, start=start):
                return result.at[:, k, pl.ds(rows[h][0] - start, rows[h][1])]

            ring = SumRing(net, axis, part, [Cut(b, rows) for b in bufs1])
            plans.append((ring, rows, result, part2, bufs2, start))
        for ring, *_ in plans:
            ring.send_all()
        yield
        for ring, *_ in plans:
            ring.pass_on()
        yield
        rings = []
        for (ring, rows, result, part2, bufs2, start), axis in zip(plans, "zx"):
            for h in range(2):
                result[:, :, pl.ds(rows[h][0] - start, rows[h][1])] = ring.total(h).astype(BF16)
            ring2 = SumRing(net, axis, part2, [Cut(b, rows) for b in bufs2])
            ring2.send_all()
            rings.append(ring2)
        for _ in range(7):
            yield
        for ring in rings:
            ring.pass_on()
        for _ in range(6):
            yield
        for ring, rows in zip(rings, FFN_ROWS):
            for h in range(2):
                sums = ring.total(h)
                for i, out in enumerate((gate_out, up_out, down_sum)):
                    out[pl.ds(*rows[h])] = sums[i]

    background = ffn_task()
    next(background)
    gain_in, gain_mixed, gain_ffn = gains[0:1, :], gains[1:2, :], gains[2:3, :]
    gain_query, gain_key = gains[4:5, 0:256], gains[5:6, 0:256]
    cos_, sin_ = cosines[...], sines[...]

    resid_dv, ffn_gain_grad = norm_grad(resid[...], gain_ffn, ffn_in_grad[...])
    resid_grad = cotangent[...].astype(F32) + resid_dv
    inputs_grad[...] = resid_grad
    attn_dv, mixed_gain_grad = norm_grad(attn_out[...], gain_mixed, resid_grad)
    attn_grad = attn_dv.astype(BF16)
    out_weight = weights[1, :, :, :, :, :, 0:1152].reshape(1024, 1152)
    mixed_grad = dot(attn_grad, out_weight, NT).astype(BF16)
    key_all, value_all = keys[...], values[...]
    query_gain_grad = jnp.zeros((1, 256), F32)
    for h in range(HEADS):
        cols = slice(h * 256, (h + 1) * 256)
        mine = mixed_grad[:, cols]
        prob = probs[h]
        prob_grad = dot(mine, value_all, NT)
        delta = jnp.sum(prob_grad * prob, axis=-1, keepdims=True)
        score_grad = (prob * (prob_grad - delta)).astype(BF16)
        value_part = dot(prob.astype(BF16), mine, TN)
        key_part = dot(score_grad, query_low[:, cols], TN)
        if h == 0:
            value_sum[...] = value_part
            key_sum[...] = key_part
        else:
            value_sum[...] += value_part
            key_sum[...] += key_part
        rot_grad = dot(score_grad, key_all, NN) * SCALE
        raw_grad, gain_part = norm_grad(qkv[:, cols], gain_query, turn_back(rot_grad, cos_, sin_))
        query_gain_grad = query_gain_grad + gain_part
        glow[:, cols] = raw_grad.astype(BF16)
    rows = glow.shape[0]
    key_grads[...] = (key_sum[...] * SCALE).astype(BF16).reshape(2, 4, rows, 256)
    value_grads[...] = value_sum[...].astype(BF16).reshape(2, 4, rows, 256)
    half = rows // 2

    def cut(h):
        return pl.ds(h * half, half)

    done = {}

    def key_task():
        ring = take(4)

        def total(h, terms):
            key_sent[:, cut(h)] = add_up(terms).astype(BF16)

        yield from scatter_ring(net, "x", lambda k, h: key_grads.at[:, k, cut(h)], ring, total)
        swap = net.send(key_sent.at[1 - low], key_pair, mirror)
        yield
        swap.wait_recv()
        done["key"] = add_up((key_sent.at[low], key_pair))

    def value_task():
        ring = take(4)
        swap = net.send(value_grads.at[1 - low], value_pair, mirror)
        yield
        swap.wait_recv()
        value_pair[...] = add_up((value_pair, value_grads.at[low])).astype(BF16)
        sums = [None, None]

        def total(h, terms):
            sums[h] = add_up(terms)

        yield from scatter_ring(net, "x", lambda k, h: value_pair.at[k, cut(h)], ring, total)
        done["value"] = jnp.concatenate(sums, axis=0)

    tasks = [key_task(), value_task()]
    for task in tasks:
        next(task)
    for c in range(3):
        cols = slice(c * 384, (c + 1) * 384)
        wire[1, :, :, :, :, :, cols] = (
            dot(mixed[...], attn_grad[:, cols], TN).astype(BF16).reshape(2, 4, 4, 2, 16, 384)
        )
    next(background)
    interleave(*tasks)

    def weight_grad(low_col, width):
        cols = slice(low_col, low_col + width)
        out = dot(attn_p[...], glow[:, cols], TN)
        wire[0, :, :, :, :, :, cols] = out[:1024].astype(BF16).reshape(2, 4, 4, 2, 16, width)
        for j in range(low_col // 128, (low_col + width) // 128):
            extras[pl.ds(j, 128, stride=EXTRA), :] = out[
                1024:, j * 128 - low_col : (j + 1) * 128 - low_col
            ]

    extras[...] = jnp.zeros(extras.shape, F32)
    weight_grad(0, 512)
    weight_grad(512, 512)
    key_raw_grad, key_gain_grad = norm_grad(
        qkv[:, 1024:1280], gain_key, turn_back(done["key"], cos_, sin_)
    )
    glow[:, 1024:1280] = key_raw_grad.astype(BF16)
    glow[:, 1280:1536] = done["value"].astype(BF16)
    weight_grad(1024, 512)
    main = weights[0].reshape(1024, WIRE)
    grad_p = jnp.concatenate(
        [dot(glow[...], main, NT), dot(glow[...], last_rows[...], NT)], axis=1
    )
    order = order_matrix(natural[...])
    high_part = grad_p.astype(BF16)
    low_part = (grad_p - high_part.astype(F32)).astype(BF16)
    attn_in_grad = dot(high_part, order, NT) + dot(low_part, order, NT)
    input_dv, in_gain_grad = norm_grad(inputs[...].astype(F32), gain_in, attn_in_grad)
    inputs_grad[...] += input_dv

    def pack(grad, offset, mod, div):
        width = mod.shape[1]
        placed = jnp.where(owned(width, div), grad, 0.0).astype(BF16)
        return dot(placed, spread(width, offset, mod), NT)

    packed = (
        pack(in_gain_grad, 0, mod9[...], div9[...])
        + pack(query_gain_grad, 9, mod2[...], div2[...])
        + pack(key_gain_grad, 11, mod2[...], div2[...])
        + pack(mixed_gain_grad, 13, mod9[...], div9[...])
        + pack(ffn_gain_grad, 22, mod9[...], div9[...])
        + pack(branch_gain_grad[...], 31, mod9[...], div9[...])
    )
    extras[pl.ds(GAIN_ROW, 128, stride=EXTRA), :] = packed
    for c in range(2):
        wire[1, :, :, :, :, :, 1152 + c * 128 : 1280 + c * 128] = (
            extras[c * 1024 : (c + 1) * 1024].astype(BF16).reshape(2, 4, 4, 2, 16, 128)
        )
    wire[1, :, :, :, :, :, 1408:1536] = jnp.zeros((2, 4, 4, 2, 16, 128), BF16)

    copies = []
    for p in range(3):
        cols = pl.ds(p * PIECE, PIECE)
        copies.append(
            net.send(
                wire.at[1 - core, :, :, :, :, :, cols], paired.at[:, :, :, :, :, cols], sibling
            )
        )

    def blob_task(order, p, copy):
        own_bufs = take(14)
        yield
        copy.wait_recv()
        cols = pl.ds(p * PIECE, PIECE)
        for a in range(2):
            for b in range(4):
                paired[a, b, :, :, :, cols] = add_up(
                    (paired.at[a, b, :, :, :, cols], wire.at[core, a, b, :, :, :, cols])
                ).astype(BF16)
        source, offset = paired, p * PIECE
        for count, axis in enumerate(order):
            have = order[count:]
            result = own_bufs[4] if count < 2 else None

            def part(k, h, source=source, offset=offset, have=have, axis=axis):
                return grid_at(
                    source, have, {axis: k}, (every, pl.ds(offset + h * (PIECE // 2), PIECE // 2))
                )

            def total(h, terms, result=result, count=count, have=have):
                if count < 2:
                    grid_at(
                        result, have[1:], {}, (every, pl.ds(h * (PIECE // 2), PIECE // 2))
                    )[...] = add_up(terms).astype(BF16)
                else:
                    final[core, :, pl.ds(p * PIECE + h * (PIECE // 2), PIECE // 2)] = add_up(terms)

            yield from scatter_ring(net, axis, part, own_bufs[:4], total)
            yield
            source, offset = result, 0
            own_bufs = own_bufs[5:]

    interleave(background, *(blob_task(order, p, copies[p]) for p, order in enumerate(ORDERS)))
    swap = net.send(final.at[core], final.at[core], sibling)
    exact = unit(down_sum.shape[1])
    high_part = down_sum[...].astype(BF16)
    low_part = (down_sum[...] - high_part.astype(F32)).astype(BF16)
    down_out[...] = dot(exact, high_part, NT) + dot(exact, low_part, NT)
    swap.wait_recv()
    mine8 = pl.ds(pl.multiple_of(core * 8, 8), 8)
    main = final[0, mine8, :]
    extra = jnp.where(core == 0, final[1, :, 1152:1280], final[1, :, 1280:1408])
    at = 0
    for out in (query_out, key_out, value_out):
        wide = out.shape[1]
        out[0:8, :] = main[:, at : at + wide]
        for j in range(wide // 128):
            row = at // 128 + j
            out[8:9, j * 128 : (j + 1) * 128] = extra[row : row + 1]
        at += wide
    output_out[...] = final[1, mine8, 0:1152]
    gains_out[...] = extra[GAIN_ROW : GAIN_ROW + 1]
    net.send_done()


def attention_backward(args, ffn, tables):
    vmem = pltpu.VMEM
    shape = jax.ShapeDtypeStruct
    rows, width = args[0].shape
    wide = ffn.shape[-1]
    scratch = sems(24 + 14 + 3 * 19 + 1) + [
        vmem(ffn.shape[3:], F32),
        vmem((2, 2, 4, 4, 2, 16, WIRE), BF16),
        vmem((2, 4, 4, 2, 16, WIRE), BF16),
        vmem((2048, 128), F32),
        vmem((2, 16, WIRE), F32),
        vmem((rows, WIRE), BF16),
        vmem((1024, 256), F32),
        vmem((1024, 256), F32),
        vmem((2, 4, rows, 256), BF16),
        vmem((2, 4, rows, 256), BF16),
        vmem((2, rows, 256), BF16),
        vmem((rows, 256), BF16),
        vmem((4, rows, 256), BF16),
    ]
    for own in FFN_ROWS:
        most = max(own[0][1], own[1][1])
        every = own[0][1] + own[1][1]
        scratch += [vmem((2, 3, 4, most, wide), BF16)] * 4
        scratch.append(vmem((3, 4, every, wide), BF16))
        scratch += [vmem((2, 3, most, wide), BF16)] * 4
    scratch += [vmem((2, 2, rows // 2, 256), BF16)] * 4
    scratch += [vmem((2, rows // 2, 256), BF16)] * 4
    for order in ORDERS:
        for count in range(3):
            left = lead_dims(order[count + 1 :])
            scratch += [vmem((2,) + left + (16, PIECE // 2), BF16)] * 4
            if count < 2:
                scratch.append(vmem(left + (16, PIECE), BF16))
    return call(
        backward_kernel,
        "attention_backward",
        [
            shape((rows, width), F32),
            shape((1, 128), F32),
            shape((9, 1024), F32),
            shape((9, 256), F32),
            shape((9, 256), F32),
            shape((8, width), F32),
            shape(ffn.shape[3:], F32),
            shape(ffn.shape[3:], F32),
            shape(ffn.shape[:2:-1], F32),
        ],
        [vmem] * 24,
        [vmem] * 9,
        scratch,
        2,
    )(*args, *tables)


class GatherRing:
    def __init__(self, net, axis, own, place):
        self.net, self.own, self.place = net, own, place
        self.mine = net.me[axis]
        self.left, self.right, self.far = (net.step(axis, by) for by in (3, 1, 2))
        self.to_left, self.to_right = net.neighbour(axis, 3), net.neighbour(axis, 1)

    def start(self):
        send, own, place, mine = self.net.send, self.own, self.place, self.mine
        self.r0 = send(own(0), place(mine, 0), self.to_right)
        self.l1 = send(own(1), place(mine, 1), self.to_left)
        self.r1 = send(own(1), place(mine, 1), self.to_right)
        self.l0 = send(own(0), place(mine, 0), self.to_left)

    def pass_on(self):
        send, place = self.net.send, self.place
        self.r0.wait_recv()
        self.f0 = send(place(self.left, 0), place(self.left, 0), self.to_right)
        self.l1.wait_recv()
        self.f1 = send(place(self.right, 1), place(self.right, 1), self.to_left)

    def finish(self):
        self.r1.wait_recv()
        self.l0.wait_recv()
        self.wait_far()

    def wait_far(self):
        self.f0.wait_recv()
        self.f1.wait_recv()


class SumRing:
    def __init__(self, net, axis, part, bufs):
        self.net, self.part = net, part
        self.mine = net.me[axis]
        self.left, self.right, self.far = (net.step(axis, by) for by in (3, 1, 2))
        self.to_left, self.to_right = net.neighbour(axis, 3), net.neighbour(axis, 1)
        self.from_left, self.from_right, self.hold, self.stage = bufs

    def send_all(self):
        self.send_far()
        self.send_right()
        self.send_left()

    def send_far(self):
        self.a0 = self.net.send(self.part(self.far, 0), self.hold.at[0], self.to_right)
        self.a1 = self.net.send(self.part(self.far, 1), self.hold.at[1], self.to_left)

    def send_right(self):
        self.r1 = self.net.send(self.part(self.right, 1), self.from_left.at[1], self.to_right)

    def send_left(self):
        self.l0 = self.net.send(self.part(self.left, 0), self.from_right.at[0], self.to_left)

    def pass_on(self):
        self.a0.wait_recv()
        self.stage[0] = add_up((self.part(self.right, 0), self.hold.at[0])).astype(BF16)
        self.r0 = self.net.send(self.stage.at[0], self.from_left.at[0], self.to_right)
        self.a1.wait_recv()
        self.stage[1] = add_up((self.part(self.left, 1), self.hold.at[1])).astype(BF16)
        self.l1 = self.net.send(self.stage.at[1], self.from_right.at[1], self.to_left)

    def total(self, h):
        if h == 0:
            self.l0.wait_recv()
            self.r0.wait_recv()
        else:
            self.r1.wait_recv()
            self.l1.wait_recv()
        return add_up((self.part(self.mine, h), self.from_left.at[h], self.from_right.at[h]))


def gelu_parts(u):
    root = 0.7978845608028654
    square = u * u
    th = jnp.tanh(root * u * (1.0 + 0.044715 * square))
    half = 0.5 * (1.0 + th)
    slope = half + 0.5 * u * (1.0 - th * th) * (root * (1.0 + 3 * 0.044715 * square))
    return u * half, slope


def ffn_kernel(
    own,
    weights,
    resid,
    cotangent,
    gain,
    outputs,
    back,
    gain_grad,
    weight_grads,
    send_sems,
    recv_sems,
    tokens,
    grads,
    act,
    slope,
    hidden,
    gate_g,
    up_g,
    branch,
    *bufs,
):
    net = Net(send_sems, recv_sems)
    me = net.me
    sibling = net.sibling()
    net.barrier([net.neighbour("y", 1), net.neighbour("y", 3), sibling])
    core, y = me["core"], me["y"]
    rows, width = own.shape
    half = rows // 2

    def cut(h):
        return pl.ds(h * half, half)

    def phase(source, held, run, bufs, meanwhile):
        parts, paired, ring_bufs = bufs[0], bufs[1], bufs[2:]
        gather = GatherRing(
            net, "y", lambda h: source.at[cut(h)], lambda k, h: held.at[k, core, cut(h)]
        )
        gather.start()
        swap = net.send(source, held.at[y, core], sibling)
        held[y, core] = source[...]
        left, right, far = gather.left, gather.right, gather.far

        def across(k):
            return net.send(held.at[k, core], held.at[k, core], sibling)

        def give(k):
            return net.send(parts.at[k, 1 - core], paired.at[k], sibling)

        def pair(k, copy):
            copy.wait_recv()
            paired[k] = add_up((paired.at[k], parts.at[k, core])).astype(BF16)

        sums = SumRing(net, "y", lambda k, h: paired.at[k, cut(h)], ring_bufs)
        swap.wait_recv()
        parts[y] = run(y)
        pair_own = give(y)
        gather.pass_on()
        gather.r1.wait_recv()
        swap_left = across(left)
        gather.l0.wait_recv()
        swap_right = across(right)
        swap_left.wait_recv()
        parts[left] = run(left)
        pair_left = give(left)
        gather.wait_far()
        swap_far = across(far)
        pair(y, pair_own)
        swap_right.wait_recv()
        parts[right] = run(right)
        pair_right = give(right)
        pair(left, pair_left)
        sums.send_left()
        swap_far.wait_recv()
        parts[far] = run(far)
        pair_far = give(far)
        pair(right, pair_right)
        sums.send_right()
        pair(far, pair_far)
        sums.send_far()
        meanwhile(0)
        sums.pass_on()
        meanwhile(1)
        return sums

    def dot(left, right, dims):
        return lax.dot_general(left, right, (dims, ((), ())), preferred_element_type=F32)

    def forward(k):
        rows_k = tokens[k].reshape(2 * rows, width)
        total = None
        for j in range(2):
            gate = dot(rows_k, weights[0, j], ((1,), (0,)))
            upper = dot(rows_k, weights[1, j], ((1,), (0,)))
            value, diff = gelu_parts(gate)
            act[k, j] = value.astype(BF16)
            slope[k, j] = (diff * upper).astype(BF16)
            hidden_low = (value * upper).astype(BF16)
            hidden[k, j] = hidden_low
            out = dot(hidden_low, weights[2, j], ((1,), (1,)))
            total = out if total is None else total + out
        return total.astype(BF16).reshape(2, rows, width)

    def backward(k):
        rows_k = grads[k].reshape(2 * rows, width)
        total = None
        for j in range(2):
            hidden_grad = dot(rows_k, weights[2, j], ((1,), (0,)))
            gate_low = (hidden_grad * slope[k, j].astype(F32)).astype(BF16)
            up_low = (hidden_grad * act[k, j].astype(F32)).astype(BF16)
            gate_g[k, j] = gate_low
            up_g[k, j] = up_low
            out = dot(gate_low, weights[0, j], ((1,), (1,))) + dot(
                up_low, weights[1, j], ((1,), (1,))
            )
            total = out if total is None else total + out
        return total.astype(BF16).reshape(2, rows, width)

    def weight_grad(which, held, factor):
        flat = held[...].reshape(8 * rows, width)
        for j in range(2):
            weight_grads[which, j] = dot(
                flat, factor[:, j].reshape(8 * rows, factor.shape[-1]), ((0,), (0,))
            ).astype(BF16)

    sums = phase(own, tokens, forward, bufs[:6], lambda step: None)
    gain_f = gain[3:4, :]
    gain_total = jnp.zeros_like(gain_f)
    for h in range(2):
        raw = sums.total(h)
        upstream = cotangent[cut(h)].astype(F32)
        scale = lax.rsqrt(jnp.mean(raw * raw, axis=-1, keepdims=True) + EPS)
        normed = raw * scale
        outputs[cut(h)] = resid[cut(h)] + normed * gain_f
        scaled = upstream * gain_f
        gain_total = gain_total + jnp.sum(upstream * normed, axis=0, keepdims=True)
        inner = jnp.mean(scaled * normed, axis=-1, keepdims=True)
        branch[cut(h)] = (scale * (scaled - normed * inner)).astype(BF16)
    gain_grad[...] = gain_total

    def meanwhile(step):
        if step == 0:
            weight_grad(2, grads, hidden)
        else:
            weight_grad(0, tokens, gate_g)
            weight_grad(1, tokens, up_g)

    sums = phase(branch, grads, backward, bufs[6:], meanwhile)
    for h in range(2):
        back[cut(h)] = sums.total(h)
    net.send_done()


def feed_forward(own, weights, resid, cotangent, gain):
    rows, width = own.shape
    wide = weights.shape[-1]
    vmem = pltpu.VMEM
    phase_bufs = [
        pltpu.VMEM((4, 2, rows, width), BF16),
        pltpu.VMEM((4, rows, width), BF16),
    ] + [pltpu.VMEM((2, rows // 2, width), BF16)] * 4
    return call(
        ffn_kernel,
        "feed_forward",
        [
            jax.ShapeDtypeStruct((rows, width), F32),
            jax.ShapeDtypeStruct((rows, width), F32),
            jax.ShapeDtypeStruct((1, width), F32),
            jax.ShapeDtypeStruct(weights.shape, BF16),
        ],
        [vmem] * 5,
        [vmem] * 4,
        sems(40)
        + [pltpu.VMEM((4, 2, rows, width), BF16)] * 2
        + [pltpu.VMEM((4, 2, 2 * rows, wide), BF16)] * 5
        + [pltpu.VMEM((rows, width), BF16)]
        + phase_bufs * 2,
        5,
    )(own, weights, resid, cotangent, gain)


def body(
    inputs,
    pair_order,
    attn_gain,
    query_gain,
    key_gain,
    mixer_gain,
    ffn_gain,
    branch_gain,
    query_weight,
    key_weight,
    value_weight,
    output_weight,
    gate_weight,
    up_weight,
    down_weight,
    cotangent,
):
    gains = (attn_gain, query_gain, key_gain, mixer_gain, ffn_gain, branch_gain)
    width = inputs.shape[2]
    gain_row = 0.0
    at = 0
    for gain in gains:
        n = gain.shape[0]
        gain_row = gain_row + jnp.pad(gain.astype(F32), (at, 128 - at - n))
        at += n
    every = np.arange(width)
    last = every - 1024
    natural = np.where(
        every < 1024,
        9 * (every // 8) + every % 8,
        9 * (2 * (last % 64) + last // 64) + 8,
    )
    twos = np.arange(256)
    tables = [
        jnp.asarray(t[None].astype(np.int32))
        for t in (natural, every % 9, every // 9, twos % 2, twos // 2)
    ]
    freqs = BASE ** (-np.arange(128) / 128)
    steps = np.concatenate([np.arange(64), 64 * np.arange(16)])
    rope = steps[:, None] * freqs[None, :]
    rope = jnp.asarray(np.stack([np.cos(rope), np.sin(rope)]).astype(np.float32))
    (
        all_ffn,
        weights,
        cosines,
        sines,
        last_rows,
        gain_rows,
        attn_p,
        qkv,
        query_low,
        key_all,
        value_all,
        probs,
        mixed_low,
        attn_out,
        resid,
        ffn_input,
    ) = attention(
        (query_weight, key_weight, value_weight, output_weight),
        (gate_weight, up_weight, down_weight),
        inputs[0],
        gain_row[None],
        pair_order,
        rope,
        tables,
    )
    ff_own = gate_weight.shape[1]
    outputs, grad_ffn_input, grad_gain_branch, ffn_grads = feed_forward(
        ffn_input, all_ffn.reshape(3, 2, width, ff_own), resid, cotangent[0], gain_rows
    )
    ffn_grads = ffn_grads.reshape(3, 4, 4, width // 8, ff_own)
    inputs_grad, gain_sum, *weight_sums = attention_backward(
        (
            grad_ffn_input,
            cotangent[0],
            inputs[0],
            resid,
            attn_out,
            gain_rows,
            weights,
            last_rows,
            attn_p,
            qkv,
            query_low,
            key_all,
            value_all,
            probs,
            mixed_low,
            cosines,
            sines,
            ffn_grads,
            grad_gain_branch,
        ),
        ffn_grads,
        tables,
    )
    gain_sums = []
    at = 0
    for gain in gains:
        gain_sums.append(gain_sum[0, at : at + gain.shape[0]])
        at += gain.shape[0]
    return (outputs[None], inputs_grad[None], *gain_sums, *weight_sums)


def solution(mesh):
    placed = (
        P("fsdp", "ctx", None),
        P("fsdp", None),
        P(("ctx", "fsdp")),
        P(("ctx", "fsdp")),
        P(("ctx", "fsdp")),
        P(("ctx", "fsdp")),
        P(("ctx", "fsdp")),
        P(("ctx", "fsdp")),
        P(("ctx", "fsdp"), None),
        P(("ctx", "fsdp"), None),
        P(("ctx", "fsdp"), None),
        P(("ctx", "fsdp"), None),
        P("ctx", "fsdp"),
        P("ctx", "fsdp"),
        P("fsdp", "ctx"),
        P("fsdp", "ctx", None),
    )
    return jax.shard_map(
        body,
        mesh=mesh,
        in_specs=placed,
        out_specs=(
            P("fsdp", "ctx", None),
            P("fsdp", "ctx", None),
            P(("ctx", "fsdp")),
            P(("ctx", "fsdp")),
            P(("ctx", "fsdp")),
            P(("ctx", "fsdp")),
            P(("ctx", "fsdp")),
            P(("ctx", "fsdp")),
            P(("ctx", "fsdp"), None),
            P(("ctx", "fsdp"), None),
            P(("ctx", "fsdp"), None),
            P(("ctx", "fsdp"), None),
            P("ctx", "fsdp"),
            P("ctx", "fsdp"),
            P("fsdp", "ctx"),
        ),
        check_vma=False,
    )
```

```python
import jax
import jax.numpy as jnp
import numpy as np
from jax import lax
from jax.experimental import pallas as pl
from jax.experimental.pallas import tpu as pltpu
from jax.sharding import PartitionSpec as P

EPS = 1e-06
SCALE = 0.0625
BASE = 1000000.0
MASKED = -1e30
BF16 = jnp.bfloat16
F32 = jnp.float32
VMEM_BYTES = 56 * 1024 * 1024


def here():
    ctx = lax.axis_index("ctx")
    fsdp = lax.axis_index("fsdp")
    return {
        "x": lax.rem(ctx, 4),
        "y": lax.div(fsdp, 4),
        "z": lax.rem(lax.div(fsdp, 2), 2) * 2 + lax.div(ctx, 4),
        "core": lax.rem(fsdp, 2),
    }


class Net:
    def __init__(self, send_sems, recv_sems):
        self.me = here()
        self.send_sems, self.recv_sems = send_sems, recv_sems
        self.used = 0
        self.sent = []

    def device(self, **moved):
        at = {**self.me, **moved}
        return (
            lax.rem(at["z"], 2) * 4 + at["x"],
            at["y"] * 4 + lax.div(at["z"], 2) * 2 + at["core"],
        )

    def step(self, axis, by):
        return lax.rem(self.me[axis] + by, 4)

    def neighbour(self, axis, by):
        return self.device(**{axis: self.step(axis, by)})

    def sibling(self):
        return self.device(core=1 - self.me["core"])

    def mirror(self):
        z = self.me["z"]
        return self.device(z=z + 1 - 2 * lax.rem(z, 2))

    def barrier(self, peers, meanwhile=None):
        sem = pltpu.get_barrier_semaphore()
        for peer in peers:
            pl.semaphore_signal(sem, inc=1, device_id=peer, device_id_type=pl.DeviceIdType.MESH)
        if meanwhile:
            meanwhile()
        pl.semaphore_wait(sem, len(peers))

    def send(self, src, dst, peer):
        n = self.used
        self.used += 1
        copy = pltpu.make_async_remote_copy(
            src_ref=src,
            dst_ref=dst,
            send_sem=self.send_sems.at[n],
            recv_sem=self.recv_sems.at[n],
            device_id=peer,
            device_id_type=pl.DeviceIdType.MESH,
        )
        copy.start()
        self.sent.append(copy)
        return copy

    def send_done(self):
        for copy in self.sent:
            copy.wait_send()


def interleave(*tasks):
    tasks = list(tasks)
    while tasks:
        for task in list(tasks):
            try:
                next(task)
            except StopIteration:
                tasks.remove(task)


def gather_ring(net, axis, own, place, arrived=None):
    mine = net.me[axis]
    left, right, far = net.step(axis, 3), net.step(axis, 1), net.step(axis, 2)
    to_left, to_right = net.neighbour(axis, 3), net.neighbour(axis, 1)
    r0 = net.send(own(0), place(mine, 0), to_right)
    l1 = net.send(own(1), place(mine, 1), to_left)
    r1 = net.send(own(1), place(mine, 1), to_right)
    l0 = net.send(own(0), place(mine, 0), to_left)
    yield
    r0.wait_recv()
    f0 = net.send(place(left, 0), place(left, 0), to_right)
    yield
    l1.wait_recv()
    f1 = net.send(place(right, 1), place(right, 1), to_left)
    yield
    r1.wait_recv()
    if arrived:
        arrived(left)
    yield
    l0.wait_recv()
    if arrived:
        arrived(right)
    yield
    f0.wait_recv()
    f1.wait_recv()
    if arrived:
        arrived(far)


def scatter_ring(net, axis, part, bufs, total):
    mine = net.me[axis]
    left, right, far = net.step(axis, 3), net.step(axis, 1), net.step(axis, 2)
    to_left, to_right = net.neighbour(axis, 3), net.neighbour(axis, 1)
    from_left, from_right, hold, stage = bufs
    a0 = net.send(part(far, 0), hold.at[0], to_right)
    a1 = net.send(part(far, 1), hold.at[1], to_left)
    r1 = net.send(part(right, 1), from_left.at[1], to_right)
    l0 = net.send(part(left, 0), from_right.at[0], to_left)
    yield
    a0.wait_recv()
    stage[0] = add_up((part(right, 0), hold.at[0])).astype(BF16)
    r0 = net.send(stage.at[0], from_left.at[0], to_right)
    yield
    a1.wait_recv()
    stage[1] = add_up((part(left, 1), hold.at[1])).astype(BF16)
    l1 = net.send(stage.at[1], from_right.at[1], to_left)
    yield
    l0.wait_recv()
    r0.wait_recv()
    total(0, (part(mine, 0), from_left.at[0], from_right.at[0]))
    yield
    r1.wait_recv()
    l1.wait_recv()
    total(1, (part(mine, 1), from_left.at[1], from_right.at[1]))


def add_up(terms):
    out = terms[0][...].astype(F32)
    for term in terms[1:]:
        out = out + term[...].astype(F32)
    return out


def sems(count):
    return [pltpu.SemaphoreType.DMA((count,)), pltpu.SemaphoreType.DMA((count,))]


def call(kernel, name, out_shape, in_spaces, out_spaces, scratch, number):
    return pl.pallas_call(
        kernel,
        name=name,
        out_shape=out_shape,
        in_specs=[pl.BlockSpec(memory_space=space) for space in in_spaces],
        out_specs=[pl.BlockSpec(memory_space=space) for space in out_spaces],
        scratch_shapes=scratch,
        compiler_params=pltpu.CompilerParams(
            collective_id=number, has_side_effects=True, vmem_limit_bytes=VMEM_BYTES
        ),
    )


GATHER_ORDERS = ("xyz", "yzx", "zxy")
SUM_ORDERS = ("xyz", "yzx", "zxy")
FFN_ROWS = (((0, 112), (112, 112)), ((224, 112), (336, 96)))
TURNS = (3, 5, 10)
HEADS = 4
EXTRA = 16
GAIN_ROW = 12
WIRE = 1536
PIECE = WIRE // 3


def grid_at(ref, have, sel, tail):
    index = []
    every = slice(None)
    if "z" in have:
        index.append(lax.rem(sel["z"], 2) if "z" in sel else every)
    for axis in "xy":
        if axis in have:
            index.append(sel.get(axis, every))
    if "z" in have:
        index.append(lax.div(sel["z"], 2) if "z" in sel else every)
    return ref.at[tuple(index) + tail]


def lead_dims(have):
    dims = []
    if "z" in have:
        dims.append(2)
    dims += [4 for axis in "xy" if axis in have]
    if "z" in have:
        dims.append(2)
    return tuple(dims)


def dot(left, right, dims):
    return lax.dot_general(left, right, (dims, ((), ())), preferred_element_type=F32)


NN = ((1,), (0,))
NT = ((1,), (1,))
TN = ((0,), (0,))


def spread(width, offset, mod):
    lane = lax.broadcasted_iota(jnp.int32, (128, width), 0)
    return jnp.where(lane == offset + mod, 1.0, 0.0).astype(BF16)


def owned(width, div):
    row = lax.broadcasted_iota(jnp.int32, (128, width), 0)
    device = jnp.where(row < 64, 2 * row, 2 * row - 127)
    return device == div


def order_matrix(natural):
    width = natural.shape[1]
    row = lax.broadcasted_iota(jnp.int32, (width, width), 0)
    return jnp.where(row == natural, 1.0, 0.0).astype(BF16)


def unit(n):
    row = lax.broadcasted_iota(jnp.int32, (n, n), 0)
    column = lax.broadcasted_iota(jnp.int32, (n, n), 1)
    return jnp.where(row == column, 1.0, 0.0).astype(BF16)


def norm_parts(v, gain):
    scale = lax.rsqrt(jnp.mean(v * v, axis=-1, keepdims=True) + EPS)
    normed = v * scale
    return normed * gain, normed, scale


def norm_grad(v, gain, dy):
    _, normed, scale = norm_parts(v, gain)
    scaled = dy * gain
    inner = jnp.mean(scaled * normed, axis=-1, keepdims=True)
    return scale * (scaled - normed * inner), jnp.sum(dy * normed, axis=0, keepdims=True)


def turn(v, cosines, sines):
    a, b = v[:, :128], v[:, 128:]
    return jnp.concatenate([a * cosines - b * sines, b * cosines + a * sines], axis=1)


def turn_back(v, cosines, sines):
    a, b = v[:, :128], v[:, 128:]
    return jnp.concatenate([a * cosines + b * sines, b * cosines - a * sines], axis=1)


def attention_kernel(
    query_w,
    key_w,
    value_w,
    output_w,
    gate_w,
    up_w,
    down_w,
    inputs,
    gain_row,
    pairs,
    rope,
    natural,
    mod9,
    div9,
    mod2,
    div2,
    all_ffn,
    weights_out,
    cosines,
    sines,
    last_rows,
    gains,
    attn_p,
    qkv,
    query_low,
    keys_out,
    values_out,
    probs_out,
    mixed_out,
    attn_out,
    resid_out,
    ffn_in,
    send_sems,
    recv_sems,
    local_sems,
    weights,
    ffn,
    own8,
    own_extra,
    other8,
    other_extra,
    start,
    extras,
    key_own,
    value_own,
    keys,
    values,
):
    net = Net(send_sems, recv_sems)
    me = net.me
    sibling, mirror = net.sibling(), net.mirror()

    def prepare():
        at = 0
        for ref in (query_w, key_w, value_w, output_w):
            whole = ref[...].astype(F32)
            wide = whole.shape[1]
            own8[:, at : at + wide] = whole[:8]
            if whole.shape[0] > 8:
                for j in range(wide // 128):
                    row = at // 128 + j
                    own_extra[row : row + 1, :] = whole[8:, j * 128 : (j + 1) * 128]
            at += wide
        own_extra[GAIN_ROW : GAIN_ROW + 1, :] = gain_row[...]
        own_extra[GAIN_ROW + 1 :, :] = jnp.zeros((EXTRA - GAIN_ROW - 1, 128), F32)
        share = gate_w.shape[0]
        ffn[0:share] = gate_w[...]
        ffn[share : 2 * share] = up_w[...]
        ffn[2 * share :] = dot(unit(down_w.shape[1]), down_w[...], NT).astype(BF16)

    net.barrier(
        [net.neighbour(axis, by) for axis in "xyz" for by in (1, 3)] + [sibling], prepare
    )
    core, x_at, low = me["core"], me["x"], lax.rem(me["z"], 2)
    swap8 = net.send(own8, other8, sibling)
    swap_extra = net.send(own_extra, other_extra, sibling)
    own_ffn = pltpu.make_async_copy(ffn, all_ffn.at[me["z"], x_at], local_sems.at[0])
    own_ffn.start()
    forwards = []

    def piece(p, h):
        return pl.ds(p * PIECE + h * (PIECE // 2), PIECE // 2)

    every = slice(None)

    def blob_task(order, p):
        both = pl.ds(p * PIECE, PIECE)
        held = weights.at[core]
        for count, axis in enumerate(order):
            fixed = {k: me[k] for k in order[count + 1 :]}

            def place(k, h):
                return grid_at(held, "xyz", {**fixed, axis: k}, (every, piece(p, h)))

            def own(h):
                if count == 0:
                    return start.at[:, piece(p, h)]
                return place(me[axis], h)

            def forward(k):
                ref = grid_at(held, "xyz", {**fixed, axis: k}, (every, both))
                forwards.append(net.send(ref, ref, sibling))

            if count == 2:
                forward(me[axis])
            yield from gather_ring(net, axis, own, place, forward if count == 2 else None)
            yield

    def ffn_rings(axes, source):
        rings = []
        for axis, rows in zip(axes, FFN_ROWS):
            other = "z" if axis == "x" else "x"
            fixed = me[other] if source is ffn else every

            def spot(k, h, axis=axis, rows=rows, fixed=fixed):
                ix, iz = (k, fixed) if axis == "x" else (fixed, k)
                return all_ffn.at[iz, ix, pl.ds(*rows[h])]

            def own(h, axis=axis, rows=rows, spot=spot):
                return ffn.at[pl.ds(*rows[h])] if source is ffn else spot(me[axis], h)

            rings.append(GatherRing(net, axis, own, spot))
        return rings

    def ffn_task():
        first = ffn_rings("xz", ffn)
        for ring in first:
            ring.start()
        for _ in range(TURNS[0]):
            yield
        for ring in first:
            ring.pass_on()
        for _ in range(TURNS[1]):
            yield
        for ring in first:
            ring.finish()
        own_ffn.wait()
        second = ffn_rings("zx", None)
        for ring in second:
            ring.start()
        for _ in range(TURNS[2]):
            yield
        for ring in second:
            ring.pass_on()
        yield
        for ring in second:
            ring.finish()

    swap8.wait_recv()
    swap_extra.wait_recv()
    first = core == 0
    mine8, theirs8 = own8[...], other8[...]
    chip = jnp.concatenate(
        [jnp.where(first, mine8, theirs8), jnp.where(first, theirs8, mine8)], axis=0
    )
    mine_x, theirs_x = own_extra[...], other_extra[...]
    half1 = jnp.concatenate(
        [
            chip[:, WIRE:],
            jnp.where(first, mine_x, theirs_x),
            jnp.where(first, theirs_x, mine_x),
            jnp.zeros((16, 2 * WIRE - chip.shape[1] - 256), F32),
        ],
        axis=1,
    )
    block = jnp.where(first, chip[:, :WIRE], half1).astype(BF16)
    start[...] = block
    weights[core, low, x_at, me["y"], lax.div(me["z"], 2)] = block

    background = ffn_task()
    blob_tasks = [blob_task(order, p) for p, order in enumerate(GATHER_ORDERS)]
    for turn_ in range(18):
        for task in blob_tasks:
            next(task)
        next(background)
    for task in blob_tasks:
        next(task, None)
    order = order_matrix(natural[...])
    for copy in forwards:
        copy.wait_recv()
    save = pltpu.make_async_copy(weights, weights_out, local_sems.at[1])
    save.start()
    for c in range(2):
        extras[c * 1024 : (c + 1) * 1024] = (
            weights[1, :, :, :, :, :, 1152 + c * 128 : 1280 + c * 128]
            .reshape(1024, 128)
            .astype(F32)
        )

    def extra_row(j):
        return extras[pl.ds(j, 128, stride=EXTRA), :].astype(BF16)

    for j in range(12):
        last_rows[:, j * 128 : (j + 1) * 128] = extra_row(j)
    packed = extra_row(GAIN_ROW)

    def unpack(offset, mod, div):
        wide = dot(packed, spread(mod.shape[1], offset, mod), NN)
        return jnp.sum(jnp.where(owned(mod.shape[1], div), wide, 0.0), axis=0, keepdims=True)

    gains[...] = jnp.zeros(gains.shape, F32)
    gain_in = unpack(0, mod9[...], div9[...])
    gain_query = unpack(9, mod2[...], div2[...])
    gain_key = unpack(11, mod2[...], div2[...])
    gain_mixed = unpack(13, mod9[...], div9[...])
    gain_ffn = unpack(22, mod9[...], div9[...])
    gain_branch = unpack(31, mod9[...], div9[...])
    gains[0:1, :] = gain_in
    gains[1:2, :] = gain_mixed
    gains[2:3, :] = gain_ffn
    gains[3:4, :] = gain_branch
    gains[4:5, 0:256] = gain_query
    gains[5:6, 0:256] = gain_key

    hidden_in = inputs[...].astype(F32)
    attn_in = norm_parts(hidden_in, gain_in)[0].astype(BF16)
    permuted = dot(attn_in, order, NN).astype(BF16)
    attn_p[...] = permuted
    block = pairs[0, lax.axis_index("ctx")]
    index = lax.broadcasted_iota(jnp.int32, (16, 128), 0)
    cos_, sin_ = [], []
    for b in (block, 15 - block):
        cb, sb = (
            jnp.sum(jnp.where(index == b, rope[i, 64:80, :], 0.0), axis=0, keepdims=True)
            for i in range(2)
        )
        cj, sj = rope[0, 0:64, :], rope[1, 0:64, :]
        cos_.append(cj * cb - sj * sb)
        sin_.append(sj * cb + cj * sb)
    cos_, sin_ = jnp.concatenate(cos_, axis=0), jnp.concatenate(sin_, axis=0)
    cosines[...] = cos_
    sines[...] = sin_

    def project(low_col, width):
        cols = slice(low_col, low_col + width)
        main = weights[0, :, :, :, :, :, cols].reshape(1024, width)
        out = dot(permuted[:, :1024], main, NN) + dot(permuted[:, 1024:], last_rows[:, cols], NN)
        qkv[:, cols] = out
        return out

    raw = project(1024, 512)
    key_own[...] = turn(norm_parts(raw[:, :256], gain_key)[0], cos_, sin_).astype(BF16)
    value_own[...] = raw[:, 256:].astype(BF16)
    keys[low, x_at] = key_own[...]
    values[low, x_at] = value_own[...]
    half = key_own.shape[0] // 2

    def cut(h):
        return pl.ds(h * half, half)

    def key_task():
        swap = net.send(key_own, keys.at[low, x_at], mirror)
        yield
        swap.wait_recv()
        yield from gather_ring(
            net, "x", lambda h: keys.at[:, x_at, cut(h)], lambda k, h: keys.at[:, k, cut(h)]
        )

    def value_task():
        yield from gather_ring(
            net, "x", lambda h: value_own.at[cut(h)], lambda k, h: values.at[low, k, cut(h)]
        )
        swap = net.send(values.at[low], values.at[low], mirror)
        yield
        swap.wait_recv()

    tasks = [key_task(), value_task()]
    for task in tasks:
        next(task)
    for h in range(HEADS):
        raw = project(h * 256, 256)
        query_low[:, h * 256 : (h + 1) * 256] = turn(
            norm_parts(raw, gain_query)[0], cos_, sin_
        ).astype(BF16)
    next(background)
    interleave(*tasks)
    key_all = keys[...].reshape(1024, 256)
    value_all = values[...].reshape(1024, 256)
    keys_out[...] = key_all
    values_out[...] = value_all

    def position(i, b):
        return jnp.where(i < 64, b * 64 + i, (15 - b) * 64 + i - 64)

    lane = lax.broadcasted_iota(jnp.int32, (1, 128), 1)
    all_pos = jnp.concatenate([position(lane, pairs[0, c]) for c in range(8)], axis=1)
    own_pos = position(lax.broadcasted_iota(jnp.int32, (128, 1), 0), block)
    allowed = all_pos <= own_pos
    for h in range(HEADS):
        scores = dot(query_low[:, h * 256 : (h + 1) * 256], key_all, NT) * SCALE
        scores = jnp.where(allowed, scores, MASKED)
        expo = jnp.exp(scores - jnp.max(scores, axis=-1, keepdims=True))
        probs = expo / jnp.sum(expo, axis=-1, keepdims=True)
        probs_out[h] = probs
        mixed_out[:, h * 256 : (h + 1) * 256] = dot(probs.astype(BF16), value_all, NN).astype(BF16)
    out_weight = weights[1, :, :, :, :, :, 0:1152].reshape(1024, 1152)
    mixed_by = dot(mixed_out[...], out_weight, NN)
    attn_out[...] = mixed_by
    resid = hidden_in + norm_parts(mixed_by, gain_mixed)[0]
    resid_out[...] = resid
    ffn_in[...] = norm_parts(resid, gain_ffn)[0].astype(BF16)
    next(background, None)
    save.wait()
    net.send_done()


def attention(projections, ffn, inputs, gain_row, pairs, rope, tables):
    rows, width = inputs.shape
    vmem, any_ = pltpu.VMEM, pl.ANY
    shape = jax.ShapeDtypeStruct
    wire = (2, 2, 4, 4, 2, 16, WIRE)
    return call(
        attention_kernel,
        "attention",
        [
            shape((4, 4, 3 * ffn[0].shape[0], ffn[0].shape[1]), BF16),
            shape(wire, BF16),
            shape((rows, 128), F32),
            shape((rows, 128), F32),
            shape((128, WIRE), BF16),
            shape((8, width), F32),
            shape((rows, width), BF16),
            shape((rows, WIRE), F32),
            shape((rows, 1024), BF16),
            shape((1024, 256), BF16),
            shape((1024, 256), BF16),
            shape((HEADS, rows, 1024), F32),
            shape((rows, 1024), BF16),
            shape((rows, width), F32),
            shape((rows, width), F32),
            shape((rows, width), BF16),
        ],
        [vmem] * 9 + [pltpu.SMEM] + [vmem] * 6,
        [any_, any_] + [vmem] * 14,
        sems(2 + 3 * 22 + 24 + 14)
        + [pltpu.SemaphoreType.DMA((2,))]
        + [
            vmem(wire, BF16),
            vmem((3 * ffn[0].shape[0], ffn[0].shape[1]), BF16),
            vmem((8, WIRE + width), F32),
            vmem((EXTRA, 128), F32),
            vmem((8, WIRE + width), F32),
            vmem((EXTRA, 128), F32),
            vmem((16, WIRE), BF16),
            vmem((2048, 128), F32),
            vmem((rows, 256), BF16),
            vmem((rows, 256), BF16),
            vmem((2, 4, rows, 256), BF16),
            vmem((2, 4, rows, 256), BF16),
        ],
        1,
    )(*projections, *ffn, inputs, gain_row, pairs, rope, *tables)


class Cut:
    def __init__(self, ref, rows):
        self.ref, self.rows = ref, rows

    @property
    def at(self):
        return self

    def __getitem__(self, h):
        ref = self.ref.at[h]
        lead = (slice(None),) * (len(ref.shape) - 2)
        return ref.at[lead + (pl.ds(0, self.rows[h][1]),)]

    def __setitem__(self, h, value):
        self[h][...] = value


def backward_kernel(
    ffn_in_grad,
    cotangent,
    inputs,
    resid,
    attn_out,
    gains,
    weights,
    last_rows,
    attn_p,
    qkv,
    query_low,
    keys,
    values,
    probs,
    mixed,
    cosines,
    sines,
    ffn,
    branch_gain_grad,
    natural,
    mod9,
    div9,
    mod2,
    div2,
    inputs_grad,
    main_out,
    extra_out,
    ffn_out,
    send_sems,
    recv_sems,
    wire,
    paired,
    extras,
    final,
    glow,
    key_sum,
    value_sum,
    key_grads,
    value_grads,
    key_sent,
    key_pair,
    value_pair,
    *bufs,
):
    net = Net(send_sems, recv_sems)
    me = net.me
    sibling, mirror = net.sibling(), net.mirror()
    net.barrier(
        [net.neighbour(axis, by) for axis in "xyz" for by in (1, 3)] + [sibling]
    )
    core, low = me["core"], lax.rem(me["z"], 2)
    every = slice(None)
    bufs = list(bufs)

    def take(n):
        got = bufs[:n]
        del bufs[:n]
        return got

    def ffn_task():
        plans = []
        for axis, rows in zip("xz", FFN_ROWS):
            bufs1, result, bufs2 = take(4), take(1)[0], take(4)
            start = rows[0][0]

            def part(k, h, axis=axis, rows=rows):
                if axis == "x":
                    return ffn.at[:, k, pl.ds(*rows[h])]
                return ffn.at[k, :, pl.ds(*rows[h])]

            def part2(k, h, rows=rows, result=result, start=start):
                return result.at[k, pl.ds(rows[h][0] - start, rows[h][1])]

            ring = SumRing(net, axis, part, [Cut(b, rows) for b in bufs1])
            plans.append((ring, rows, result, part2, bufs2, start))
        for ring, *_ in plans:
            ring.send_all()
        yield
        for ring, *_ in plans:
            ring.pass_on()
        yield
        rings = []
        for (ring, rows, result, part2, bufs2, start), axis in zip(plans, "zx"):
            for h in range(2):
                result[:, pl.ds(rows[h][0] - start, rows[h][1])] = ring.total(h).astype(BF16)
            ring2 = SumRing(net, axis, part2, [Cut(b, rows) for b in bufs2])
            ring2.send_all()
            rings.append(ring2)
        for _ in range(7):
            yield
        for ring in rings:
            ring.pass_on()
        for _ in range(6):
            yield
        for ring, rows in zip(rings, FFN_ROWS):
            for h in range(2):
                ffn_out[pl.ds(*rows[h])] = ring.total(h)

    background = ffn_task()
    next(background)
    gain_in, gain_mixed, gain_ffn = gains[0:1, :], gains[1:2, :], gains[2:3, :]
    gain_query, gain_key = gains[4:5, 0:256], gains[5:6, 0:256]
    cos_, sin_ = cosines[...], sines[...]

    resid_dv, ffn_gain_grad = norm_grad(resid[...], gain_ffn, ffn_in_grad[...])
    resid_grad = cotangent[...].astype(F32) + resid_dv
    inputs_grad[...] = resid_grad
    attn_dv, mixed_gain_grad = norm_grad(attn_out[...], gain_mixed, resid_grad)
    attn_grad = attn_dv.astype(BF16)
    out_weight = weights[1, :, :, :, :, :, 0:1152].reshape(1024, 1152)
    mixed_grad = dot(attn_grad, out_weight, NT).astype(BF16)
    key_all, value_all = keys[...], values[...]
    query_gain_grad = jnp.zeros((1, 256), F32)
    for h in range(HEADS):
        cols = slice(h * 256, (h + 1) * 256)
        mine = mixed_grad[:, cols]
        prob = probs[h]
        prob_grad = dot(mine, value_all, NT)
        delta = jnp.sum(prob_grad * prob, axis=-1, keepdims=True)
        score_grad = (prob * (prob_grad - delta)).astype(BF16)
        value_part = dot(prob.astype(BF16), mine, TN)
        key_part = dot(score_grad, query_low[:, cols], TN)
        if h == 0:
            value_sum[...] = value_part
            key_sum[...] = key_part
        else:
            value_sum[...] += value_part
            key_sum[...] += key_part
        rot_grad = dot(score_grad, key_all, NN) * SCALE
        raw_grad, gain_part = norm_grad(qkv[:, cols], gain_query, turn_back(rot_grad, cos_, sin_))
        query_gain_grad = query_gain_grad + gain_part
        glow[:, cols] = raw_grad.astype(BF16)
    rows = glow.shape[0]
    key_grads[...] = (key_sum[...] * SCALE).astype(BF16).reshape(2, 4, rows, 256)
    value_grads[...] = value_sum[...].astype(BF16).reshape(2, 4, rows, 256)
    half = rows // 2

    def cut(h):
        return pl.ds(h * half, half)

    done = {}

    def key_task():
        ring = take(4)

        def total(h, terms):
            key_sent[:, cut(h)] = add_up(terms).astype(BF16)

        yield from scatter_ring(net, "x", lambda k, h: key_grads.at[:, k, cut(h)], ring, total)
        swap = net.send(key_sent.at[1 - low], key_pair, mirror)
        yield
        swap.wait_recv()
        done["key"] = add_up((key_sent.at[low], key_pair))

    def value_task():
        ring = take(4)
        swap = net.send(value_grads.at[1 - low], value_pair, mirror)
        yield
        swap.wait_recv()
        value_pair[...] = add_up((value_pair, value_grads.at[low])).astype(BF16)
        sums = [None, None]

        def total(h, terms):
            sums[h] = add_up(terms)

        yield from scatter_ring(net, "x", lambda k, h: value_pair.at[k, cut(h)], ring, total)
        done["value"] = jnp.concatenate(sums, axis=0)

    tasks = [key_task(), value_task()]
    for task in tasks:
        next(task)
    for c in range(3):
        cols = slice(c * 384, (c + 1) * 384)
        wire[1, :, :, :, :, :, cols] = (
            dot(mixed[...], attn_grad[:, cols], TN).astype(BF16).reshape(2, 4, 4, 2, 16, 384)
        )
    interleave(*tasks)
    next(background)

    def weight_grad(low_col, width):
        cols = slice(low_col, low_col + width)
        out = dot(attn_p[...], glow[:, cols], TN)
        wire[0, :, :, :, :, :, cols] = out[:1024].astype(BF16).reshape(2, 4, 4, 2, 16, width)
        for j in range(low_col // 128, (low_col + width) // 128):
            extras[pl.ds(j, 128, stride=EXTRA), :] = out[
                1024:, j * 128 - low_col : (j + 1) * 128 - low_col
            ]

    extras[...] = jnp.zeros(extras.shape, F32)
    weight_grad(0, 512)
    weight_grad(512, 512)
    key_raw_grad, key_gain_grad = norm_grad(
        qkv[:, 1024:1280], gain_key, turn_back(done["key"], cos_, sin_)
    )
    glow[:, 1024:1280] = key_raw_grad.astype(BF16)
    glow[:, 1280:1536] = done["value"].astype(BF16)
    weight_grad(1024, 512)
    main = weights[0].reshape(1024, WIRE)
    grad_p = jnp.concatenate(
        [dot(glow[...], main, NT), dot(glow[...], last_rows[...], NT)], axis=1
    )
    order = order_matrix(natural[...])
    high_part = grad_p.astype(BF16)
    low_part = (grad_p - high_part.astype(F32)).astype(BF16)
    attn_in_grad = dot(high_part, order, NT) + dot(low_part, order, NT)
    input_dv, in_gain_grad = norm_grad(inputs[...].astype(F32), gain_in, attn_in_grad)
    inputs_grad[...] += input_dv

    def pack(grad, offset, mod, div):
        width = mod.shape[1]
        placed = jnp.where(owned(width, div), grad, 0.0).astype(BF16)
        return dot(placed, spread(width, offset, mod), NT)

    packed = (
        pack(in_gain_grad, 0, mod9[...], div9[...])
        + pack(query_gain_grad, 9, mod2[...], div2[...])
        + pack(key_gain_grad, 11, mod2[...], div2[...])
        + pack(mixed_gain_grad, 13, mod9[...], div9[...])
        + pack(ffn_gain_grad, 22, mod9[...], div9[...])
        + pack(branch_gain_grad[...], 31, mod9[...], div9[...])
    )
    extras[pl.ds(GAIN_ROW, 128, stride=EXTRA), :] = packed
    for c in range(2):
        wire[1, :, :, :, :, :, 1152 + c * 128 : 1280 + c * 128] = (
            extras[c * 1024 : (c + 1) * 1024].astype(BF16).reshape(2, 4, 4, 2, 16, 128)
        )
    wire[1, :, :, :, :, :, 1408:1536] = jnp.zeros((2, 4, 4, 2, 16, 128), BF16)

    copies = []
    for p in range(3):
        cols = pl.ds(p * PIECE, PIECE)
        copies.append(
            net.send(
                wire.at[1 - core, :, :, :, :, :, cols], paired.at[:, :, :, :, :, cols], sibling
            )
        )

    def blob_task(order, p, copy):
        own_bufs = take(14)
        yield
        copy.wait_recv()
        cols = pl.ds(p * PIECE, PIECE)
        for a in range(2):
            for b in range(4):
                paired[a, b, :, :, :, cols] = add_up(
                    (paired.at[a, b, :, :, :, cols], wire.at[core, a, b, :, :, :, cols])
                ).astype(BF16)
        source, offset = paired, p * PIECE
        for count, axis in enumerate(order):
            have = order[count:]
            result = own_bufs[4] if count < 2 else None

            def part(k, h, source=source, offset=offset, have=have, axis=axis):
                return grid_at(
                    source, have, {axis: k}, (every, pl.ds(offset + h * (PIECE // 2), PIECE // 2))
                )

            def total(h, terms, result=result, count=count, have=have):
                if count < 2:
                    grid_at(
                        result, have[1:], {}, (every, pl.ds(h * (PIECE // 2), PIECE // 2))
                    )[...] = add_up(terms).astype(BF16)
                else:
                    final[core, :, pl.ds(p * PIECE + h * (PIECE // 2), PIECE // 2)] = add_up(terms)

            yield from scatter_ring(net, axis, part, own_bufs[:4], total)
            yield
            source, offset = result, 0
            own_bufs = own_bufs[5:]

    interleave(background, *(blob_task(order, p, copies[p]) for p, order in enumerate(SUM_ORDERS)))
    swap = net.send(final.at[core], final.at[core], sibling)
    swap.wait_recv()
    mine8 = pl.ds(pl.multiple_of(core * 8, 8), 8)
    main_out[:, 0:WIRE] = final[0, mine8, :]
    main_out[:, WIRE:] = final[1, mine8, 0:1152]
    extra_out[...] = jnp.where(core == 0, final[1, :, 1152:1280], final[1, :, 1280:1408])
    net.send_done()


def results_kernel(
    out_in,
    inputs_grad_in,
    main,
    extra,
    ffn,
    out,
    inputs_grad,
    gains_out,
    query_out,
    key_out,
    value_out,
    output_out,
    gate_out,
    up_out,
    down_out,
):
    out[...] = out_in[...]
    inputs_grad[...] = inputs_grad_in[...]
    at = 0
    for ref in (query_out, key_out, value_out):
        wide = ref.shape[1]
        ref[0:8, :] = main[:, at : at + wide]
        for j in range(wide // 128):
            row = at // 128 + j
            ref[8:9, j * 128 : (j + 1) * 128] = extra[row : row + 1]
        at += wide
    output_out[...] = main[:, WIRE:]
    gains_out[...] = extra[GAIN_ROW : GAIN_ROW + 1]
    share = gate_out.shape[0]
    gate_out[...] = ffn[0:share]
    up_out[...] = ffn[share : 2 * share]
    down = ffn[2 * share :]
    exact = unit(down.shape[1])
    high_part = down.astype(BF16)
    low_part = (down - high_part.astype(F32)).astype(BF16)
    down_out[...] = dot(exact, high_part, NT) + dot(exact, low_part, NT)


def results(out, inputs_grad, main, extra, ffn):
    shape = jax.ShapeDtypeStruct
    width = out.shape[1]
    share, wide = ffn.shape[0] // 3, ffn.shape[1]
    shapes = (
        [out.shape, out.shape, (1, 128), (9, 1024), (9, 256), (9, 256), (8, width)]
        + [(share, wide)] * 2
        + [(wide, share)]
    )
    vmem = pltpu.VMEM
    return pl.pallas_call(
        results_kernel,
        name="results",
        out_shape=[shape(s, F32) for s in shapes],
        in_specs=[pl.BlockSpec(memory_space=vmem)] * 5,
        out_specs=[pl.BlockSpec(memory_space=vmem)] * 10,
        compiler_params=pltpu.CompilerParams(vmem_limit_bytes=VMEM_BYTES),
    )(out, inputs_grad, main, extra, ffn)


def attention_backward(args, ffn, tables):
    vmem = pltpu.VMEM
    shape = jax.ShapeDtypeStruct
    rows, width = args[0].shape
    wide = ffn.shape[-1]
    scratch = sems(24 + 14 + 3 * 19 + 1) + [
        vmem((2, 2, 4, 4, 2, 16, WIRE), BF16),
        vmem((2, 4, 4, 2, 16, WIRE), BF16),
        vmem((2048, 128), F32),
        vmem((2, 16, WIRE), F32),
        vmem((rows, WIRE), BF16),
        vmem((1024, 256), F32),
        vmem((1024, 256), F32),
        vmem((2, 4, rows, 256), BF16),
        vmem((2, 4, rows, 256), BF16),
        vmem((2, rows, 256), BF16),
        vmem((rows, 256), BF16),
        vmem((4, rows, 256), BF16),
    ]
    for own in FFN_ROWS:
        most = max(own[0][1], own[1][1])
        every = own[0][1] + own[1][1]
        scratch += [vmem((2, 4, most, wide), BF16)] * 4
        scratch.append(vmem((4, every, wide), BF16))
        scratch += [vmem((2, most, wide), BF16)] * 4
    scratch += [vmem((2, 2, rows // 2, 256), BF16)] * 4
    scratch += [vmem((2, rows // 2, 256), BF16)] * 4
    for order in SUM_ORDERS:
        for count in range(3):
            left = lead_dims(order[count + 1 :])
            scratch += [vmem((2,) + left + (16, PIECE // 2), BF16)] * 4
            if count < 2:
                scratch.append(vmem(left + (16, PIECE), BF16))
    return call(
        backward_kernel,
        "attention_backward",
        [
            shape((rows, width), F32),
            shape((8, WIRE + width), F32),
            shape((EXTRA, 128), F32),
            shape(ffn.shape[2:], F32),
        ],
        [vmem] * 24,
        [vmem] * 4,
        scratch,
        2,
    )(*args, *tables)


class GatherRing:
    def __init__(self, net, axis, own, place):
        self.net, self.own, self.place = net, own, place
        self.mine = net.me[axis]
        self.left, self.right, self.far = (net.step(axis, by) for by in (3, 1, 2))
        self.to_left, self.to_right = net.neighbour(axis, 3), net.neighbour(axis, 1)

    def start(self):
        send, own, place, mine = self.net.send, self.own, self.place, self.mine
        self.r0 = send(own(0), place(mine, 0), self.to_right)
        self.l1 = send(own(1), place(mine, 1), self.to_left)
        self.r1 = send(own(1), place(mine, 1), self.to_right)
        self.l0 = send(own(0), place(mine, 0), self.to_left)

    def pass_on(self):
        send, place = self.net.send, self.place
        self.r0.wait_recv()
        self.f0 = send(place(self.left, 0), place(self.left, 0), self.to_right)
        self.l1.wait_recv()
        self.f1 = send(place(self.right, 1), place(self.right, 1), self.to_left)

    def finish(self):
        self.r1.wait_recv()
        self.l0.wait_recv()
        self.wait_far()

    def wait_far(self):
        self.f0.wait_recv()
        self.f1.wait_recv()


class SumRing:
    def __init__(self, net, axis, part, bufs):
        self.net, self.part = net, part
        self.mine = net.me[axis]
        self.left, self.right, self.far = (net.step(axis, by) for by in (3, 1, 2))
        self.to_left, self.to_right = net.neighbour(axis, 3), net.neighbour(axis, 1)
        self.from_left, self.from_right, self.hold, self.stage = bufs

    def send_all(self):
        self.send_far()
        self.send_right()
        self.send_left()

    def send_far(self):
        self.a0 = self.net.send(self.part(self.far, 0), self.hold.at[0], self.to_right)
        self.a1 = self.net.send(self.part(self.far, 1), self.hold.at[1], self.to_left)

    def send_right(self):
        self.r1 = self.net.send(self.part(self.right, 1), self.from_left.at[1], self.to_right)

    def send_left(self):
        self.l0 = self.net.send(self.part(self.left, 0), self.from_right.at[0], self.to_left)

    def pass_on(self):
        self.a0.wait_recv()
        self.stage[0] = add_up((self.part(self.right, 0), self.hold.at[0])).astype(BF16)
        self.r0 = self.net.send(self.stage.at[0], self.from_left.at[0], self.to_right)
        self.a1.wait_recv()
        self.stage[1] = add_up((self.part(self.left, 1), self.hold.at[1])).astype(BF16)
        self.l1 = self.net.send(self.stage.at[1], self.from_right.at[1], self.to_left)

    def total(self, h):
        if h == 0:
            self.l0.wait_recv()
            self.r0.wait_recv()
        else:
            self.r1.wait_recv()
            self.l1.wait_recv()
        return add_up((self.part(self.mine, h), self.from_left.at[h], self.from_right.at[h]))


def gelu_parts(u):
    root = 0.7978845608028654
    square = u * u
    th = jnp.tanh(root * u * (1.0 + 0.044715 * square))
    half = 0.5 * (1.0 + th)
    slope = half + 0.5 * u * (1.0 - th * th) * (root * (1.0 + 3 * 0.044715 * square))
    return u * half, slope


def ffn_kernel(
    own,
    all_ffn,
    resid,
    cotangent,
    gain,
    outputs,
    back,
    gain_grad,
    weight_grads,
    send_sems,
    recv_sems,
    local_sems,
    weights,
    tokens,
    grads,
    act,
    slope,
    hidden,
    gate_g,
    up_g,
    branch,
    *bufs,
):
    net = Net(send_sems, recv_sems)
    me = net.me
    sibling = net.sibling()
    share = all_ffn.shape[2] // 3
    loads = [
        pltpu.make_async_copy(
            all_ffn.at[:, :, pl.ds(m * share, share)], weights.at[m], local_sems.at[m]
        )
        for m in range(3)
    ]
    for load in loads:
        load.start()
    net.barrier([net.neighbour("y", 1), net.neighbour("y", 3), sibling])
    core, y = me["core"], me["y"]
    rows, width = own.shape

    def weight(m, j):
        return weights[m, 2 * j : 2 * j + 2].reshape(width, weights.shape[-1])
    half = rows // 2

    def cut(h):
        return pl.ds(h * half, half)

    def phase(source, held, run, bufs, meanwhile):
        parts, paired, ring_bufs = bufs[0], bufs[1], bufs[2:]
        gather = GatherRing(
            net, "y", lambda h: source.at[cut(h)], lambda k, h: held.at[k, core, cut(h)]
        )
        gather.start()
        swap = net.send(source, held.at[y, core], sibling)
        held[y, core] = source[...]
        left, right, far = gather.left, gather.right, gather.far

        def across(k):
            return net.send(held.at[k, core], held.at[k, core], sibling)

        def give(k):
            return net.send(parts.at[k, 1 - core], paired.at[k], sibling)

        def pair(k, copy):
            copy.wait_recv()
            paired[k] = add_up((paired.at[k], parts.at[k, core])).astype(BF16)

        sums = SumRing(net, "y", lambda k, h: paired.at[k, cut(h)], ring_bufs)
        swap.wait_recv()
        while loads:
            loads.pop().wait()
        parts[y] = run(y)
        pair_own = give(y)
        gather.pass_on()
        gather.r1.wait_recv()
        swap_left = across(left)
        gather.l0.wait_recv()
        swap_right = across(right)
        swap_left.wait_recv()
        parts[left] = run(left)
        pair_left = give(left)
        gather.wait_far()
        swap_far = across(far)
        pair(y, pair_own)
        swap_right.wait_recv()
        parts[right] = run(right)
        pair_right = give(right)
        pair(left, pair_left)
        sums.send_left()
        swap_far.wait_recv()
        parts[far] = run(far)
        pair_far = give(far)
        pair(right, pair_right)
        sums.send_right()
        pair(far, pair_far)
        sums.send_far()
        meanwhile(0)
        sums.pass_on()
        meanwhile(1)
        return sums

    def dot(left, right, dims):
        return lax.dot_general(left, right, (dims, ((), ())), preferred_element_type=F32)

    def forward(k):
        rows_k = tokens[k].reshape(2 * rows, width)
        total = None
        for j in range(2):
            gate = dot(rows_k, weight(0, j), ((1,), (0,)))
            upper = dot(rows_k, weight(1, j), ((1,), (0,)))
            value, diff = gelu_parts(gate)
            act[k, j] = value.astype(BF16)
            slope[k, j] = (diff * upper).astype(BF16)
            hidden_low = (value * upper).astype(BF16)
            hidden[k, j] = hidden_low
            out = dot(hidden_low, weight(2, j), ((1,), (1,)))
            total = out if total is None else total + out
        return total.astype(BF16).reshape(2, rows, width)

    def backward(k):
        rows_k = grads[k].reshape(2 * rows, width)
        total = None
        for j in range(2):
            hidden_grad = dot(rows_k, weight(2, j), ((1,), (0,)))
            gate_low = (hidden_grad * slope[k, j].astype(F32)).astype(BF16)
            up_low = (hidden_grad * act[k, j].astype(F32)).astype(BF16)
            gate_g[k, j] = gate_low
            up_g[k, j] = up_low
            out = dot(gate_low, weight(0, j), ((1,), (1,))) + dot(
                up_low, weight(1, j), ((1,), (1,))
            )
            total = out if total is None else total + out
        return total.astype(BF16).reshape(2, rows, width)

    def weight_grad(which, held, factor):
        flat = held[...].reshape(8 * rows, width)
        for j in range(2):
            out = dot(flat, factor[:, j].reshape(8 * rows, factor.shape[-1]), ((0,), (0,)))
            weight_grads[2 * j : 2 * j + 2, :, which * share : (which + 1) * share] = out.astype(
                BF16
            ).reshape(2, 4, share, out.shape[-1])

    sums = phase(own, tokens, forward, bufs[:6], lambda step: None)
    gain_f = gain[3:4, :]
    gain_total = jnp.zeros_like(gain_f)
    for h in range(2):
        raw = sums.total(h)
        upstream = cotangent[cut(h)].astype(F32)
        scale = lax.rsqrt(jnp.mean(raw * raw, axis=-1, keepdims=True) + EPS)
        normed = raw * scale
        outputs[cut(h)] = resid[cut(h)] + normed * gain_f
        scaled = upstream * gain_f
        gain_total = gain_total + jnp.sum(upstream * normed, axis=0, keepdims=True)
        inner = jnp.mean(scaled * normed, axis=-1, keepdims=True)
        branch[cut(h)] = (scale * (scaled - normed * inner)).astype(BF16)
    gain_grad[...] = gain_total

    def meanwhile(step):
        if step == 0:
            weight_grad(2, grads, hidden)
        else:
            weight_grad(0, tokens, gate_g)
            weight_grad(1, tokens, up_g)

    sums = phase(branch, grads, backward, bufs[6:], meanwhile)
    for h in range(2):
        back[cut(h)] = sums.total(h)
    net.send_done()


def feed_forward(own, weights, resid, cotangent, gain):
    rows, width = own.shape
    wide = weights.shape[-1]
    vmem = pltpu.VMEM
    phase_bufs = [
        pltpu.VMEM((4, 2, rows, width), BF16),
        pltpu.VMEM((4, rows, width), BF16),
    ] + [pltpu.VMEM((2, rows // 2, width), BF16)] * 4
    return call(
        ffn_kernel,
        "feed_forward",
        [
            jax.ShapeDtypeStruct((rows, width), F32),
            jax.ShapeDtypeStruct((rows, width), F32),
            jax.ShapeDtypeStruct((1, width), F32),
            jax.ShapeDtypeStruct(weights.shape, BF16),
        ],
        [vmem, pl.ANY] + [vmem] * 3,
        [vmem] * 4,
        sems(40)
        + [pltpu.SemaphoreType.DMA((3,)), vmem((3, 4, 4, weights.shape[2] // 3, wide), BF16)]
        + [pltpu.VMEM((4, 2, rows, width), BF16)] * 2
        + [pltpu.VMEM((4, 2, 2 * rows, wide), BF16)] * 5
        + [pltpu.VMEM((rows, width), BF16)]
        + phase_bufs * 2,
        5,
    )(own, weights, resid, cotangent, gain)


def body(
    inputs,
    pair_order,
    attn_gain,
    query_gain,
    key_gain,
    mixer_gain,
    ffn_gain,
    branch_gain,
    query_weight,
    key_weight,
    value_weight,
    output_weight,
    gate_weight,
    up_weight,
    down_weight,
    cotangent,
):
    gains = (attn_gain, query_gain, key_gain, mixer_gain, ffn_gain, branch_gain)
    width = inputs.shape[2]
    gain_row = 0.0
    at = 0
    for gain in gains:
        n = gain.shape[0]
        gain_row = gain_row + jnp.pad(gain.astype(F32), (at, 128 - at - n))
        at += n
    every = np.arange(width)
    last = every - 1024
    natural = np.where(
        every < 1024,
        9 * (every // 8) + every % 8,
        9 * (2 * (last % 64) + last // 64) + 8,
    )
    twos = np.arange(256)
    tables = [
        jnp.asarray(t[None].astype(np.int32))
        for t in (natural, every % 9, every // 9, twos % 2, twos // 2)
    ]
    freqs = BASE ** (-np.arange(128) / 128)
    steps = np.concatenate([np.arange(64), 64 * np.arange(16)])
    rope = steps[:, None] * freqs[None, :]
    rope = jnp.asarray(np.stack([np.cos(rope), np.sin(rope)]).astype(np.float32))
    (
        all_ffn,
        weights,
        cosines,
        sines,
        last_rows,
        gain_rows,
        attn_p,
        qkv,
        query_low,
        key_all,
        value_all,
        probs,
        mixed_low,
        attn_out,
        resid,
        ffn_input,
    ) = attention(
        (query_weight, key_weight, value_weight, output_weight),
        (gate_weight, up_weight, down_weight),
        inputs[0],
        gain_row[None],
        pair_order,
        rope,
        tables,
    )
    outputs, grad_ffn_input, grad_gain_branch, ffn_grads = feed_forward(
        ffn_input, all_ffn, resid, cotangent[0], gain_rows
    )
    sums = attention_backward(
        (
            grad_ffn_input,
            cotangent[0],
            inputs[0],
            resid,
            attn_out,
            gain_rows,
            weights,
            last_rows,
            attn_p,
            qkv,
            query_low,
            key_all,
            value_all,
            probs,
            mixed_low,
            cosines,
            sines,
            ffn_grads,
            grad_gain_branch,
        ),
        ffn_grads,
        tables,
    )
    outputs, inputs_grad, gain_sum, *weight_sums = results(outputs, *sums)
    gain_sums = []
    at = 0
    for gain in gains:
        gain_sums.append(gain_sum[0, at : at + gain.shape[0]])
        at += gain.shape[0]
    return (outputs[None], inputs_grad[None], *gain_sums, *weight_sums)


def solution(mesh):
    placed = (
        P("fsdp", "ctx", None),
        P("fsdp", None),
        P(("ctx", "fsdp")),
        P(("ctx", "fsdp")),
        P(("ctx", "fsdp")),
        P(("ctx", "fsdp")),
        P(("ctx", "fsdp")),
        P(("ctx", "fsdp")),
        P(("ctx", "fsdp"), None),
        P(("ctx", "fsdp"), None),
        P(("ctx", "fsdp"), None),
        P(("ctx", "fsdp"), None),
        P("ctx", "fsdp"),
        P("ctx", "fsdp"),
        P("fsdp", "ctx"),
        P("fsdp", "ctx", None),
    )
    return jax.shard_map(
        body,
        mesh=mesh,
        in_specs=placed,
        out_specs=(
            P("fsdp", "ctx", None),
            P("fsdp", "ctx", None),
            P(("ctx", "fsdp")),
            P(("ctx", "fsdp")),
            P(("ctx", "fsdp")),
            P(("ctx", "fsdp")),
            P(("ctx", "fsdp")),
            P(("ctx", "fsdp")),
            P(("ctx", "fsdp"), None),
            P(("ctx", "fsdp"), None),
            P(("ctx", "fsdp"), None),
            P(("ctx", "fsdp"), None),
            P("ctx", "fsdp"),
            P("ctx", "fsdp"),
            P("fsdp", "ctx"),
        ),
        check_vma=False,
    )
```

```python
import jax
import jax.numpy as jnp
import numpy as np
from jax import lax
from jax.experimental import pallas as pl
from jax.experimental.pallas import tpu as pltpu
from jax.sharding import PartitionSpec as P

EPS = 1e-06
SCALE = 0.0625
BASE = 1000000.0
MASKED = -1e30
BF16 = jnp.bfloat16
F32 = jnp.float32
VMEM_BYTES = 56 * 1024 * 1024


def here():
    ctx = lax.axis_index("ctx")
    fsdp = lax.axis_index("fsdp")
    return {
        "x": lax.rem(ctx, 4),
        "y": lax.div(fsdp, 4),
        "z": lax.rem(lax.div(fsdp, 2), 2) * 2 + lax.div(ctx, 4),
        "core": lax.rem(fsdp, 2),
    }


class Net:
    def __init__(self, send_sems, recv_sems):
        self.me = here()
        self.send_sems, self.recv_sems = send_sems, recv_sems
        self.used = 0
        self.sent = []

    def device(self, **moved):
        at = {**self.me, **moved}
        return (
            lax.rem(at["z"], 2) * 4 + at["x"],
            at["y"] * 4 + lax.div(at["z"], 2) * 2 + at["core"],
        )

    def step(self, axis, by):
        return lax.rem(self.me[axis] + by, 4)

    def neighbour(self, axis, by):
        return self.device(**{axis: self.step(axis, by)})

    def sibling(self):
        return self.device(core=1 - self.me["core"])

    def mirror(self):
        z = self.me["z"]
        return self.device(z=z + 1 - 2 * lax.rem(z, 2))

    def barrier(self, peers, meanwhile=None):
        sem = pltpu.get_barrier_semaphore()
        for peer in peers:
            pl.semaphore_signal(sem, inc=1, device_id=peer, device_id_type=pl.DeviceIdType.MESH)
        if meanwhile:
            meanwhile()
        pl.semaphore_wait(sem, len(peers))

    def send(self, src, dst, peer):
        n = self.used
        self.used += 1
        copy = pltpu.make_async_remote_copy(
            src_ref=src,
            dst_ref=dst,
            send_sem=self.send_sems.at[n],
            recv_sem=self.recv_sems.at[n],
            device_id=peer,
            device_id_type=pl.DeviceIdType.MESH,
        )
        copy.start()
        self.sent.append(copy)
        return copy

    def send_done(self):
        for copy in self.sent:
            copy.wait_send()


def interleave(*tasks):
    tasks = list(tasks)
    while tasks:
        for task in list(tasks):
            try:
                next(task)
            except StopIteration:
                tasks.remove(task)


def gather_ring(net, axis, own, place, arrived=None):
    mine = net.me[axis]
    left, right, far = net.step(axis, 3), net.step(axis, 1), net.step(axis, 2)
    to_left, to_right = net.neighbour(axis, 3), net.neighbour(axis, 1)
    r0 = net.send(own(0), place(mine, 0), to_right)
    l1 = net.send(own(1), place(mine, 1), to_left)
    r1 = net.send(own(1), place(mine, 1), to_right)
    l0 = net.send(own(0), place(mine, 0), to_left)
    yield
    r0.wait_recv()
    f0 = net.send(place(left, 0), place(left, 0), to_right)
    yield
    l1.wait_recv()
    f1 = net.send(place(right, 1), place(right, 1), to_left)
    yield
    r1.wait_recv()
    if arrived:
        arrived(left)
    yield
    l0.wait_recv()
    if arrived:
        arrived(right)
    yield
    f0.wait_recv()
    f1.wait_recv()
    if arrived:
        arrived(far)


def scatter_ring(net, axis, part, bufs, total):
    mine = net.me[axis]
    left, right, far = net.step(axis, 3), net.step(axis, 1), net.step(axis, 2)
    to_left, to_right = net.neighbour(axis, 3), net.neighbour(axis, 1)
    from_left, from_right, hold, stage = bufs
    a0 = net.send(part(far, 0), hold.at[0], to_right)
    a1 = net.send(part(far, 1), hold.at[1], to_left)
    r1 = net.send(part(right, 1), from_left.at[1], to_right)
    l0 = net.send(part(left, 0), from_right.at[0], to_left)
    yield
    a0.wait_recv()
    stage[0] = add_up((part(right, 0), hold.at[0])).astype(BF16)
    r0 = net.send(stage.at[0], from_left.at[0], to_right)
    yield
    a1.wait_recv()
    stage[1] = add_up((part(left, 1), hold.at[1])).astype(BF16)
    l1 = net.send(stage.at[1], from_right.at[1], to_left)
    yield
    l0.wait_recv()
    r0.wait_recv()
    total(0, (part(mine, 0), from_left.at[0], from_right.at[0]))
    yield
    r1.wait_recv()
    l1.wait_recv()
    total(1, (part(mine, 1), from_left.at[1], from_right.at[1]))


def add_up(terms):
    out = terms[0][...].astype(F32)
    for term in terms[1:]:
        out = out + term[...].astype(F32)
    return out


def sems(count):
    return [pltpu.SemaphoreType.DMA((count,)), pltpu.SemaphoreType.DMA((count,))]


def call(kernel, name, out_shape, in_spaces, out_spaces, scratch, number):
    return pl.pallas_call(
        kernel,
        name=name,
        out_shape=out_shape,
        in_specs=[pl.BlockSpec(memory_space=space) for space in in_spaces],
        out_specs=[pl.BlockSpec(memory_space=space) for space in out_spaces],
        scratch_shapes=scratch,
        compiler_params=pltpu.CompilerParams(
            collective_id=number, has_side_effects=True, vmem_limit_bytes=VMEM_BYTES
        ),
    )


GATHER_ORDERS = ("xyz", "yzx", "zxy")
SUM_ORDERS = ("xyz", "yzx", "zxy")
GATHER_ROWS = (((0, 80), (80, 64)), ((144, 80), (224, 64)))
DOWN_ROWS = (((0, 48), (48, 32)), ((80, 32), (112, 32)))
FFN_ROWS = (((0, 112), (112, 112)), ((224, 112), (336, 96)))
TURNS = (3, 5, 10)
HEADS = 4
EXTRA = 16
GAIN_ROW = 12
WIRE = 1536
PIECE = WIRE // 3


def grid_at(ref, have, sel, tail):
    index = []
    every = slice(None)
    if "z" in have:
        index.append(lax.rem(sel["z"], 2) if "z" in sel else every)
    for axis in "xy":
        if axis in have:
            index.append(sel.get(axis, every))
    if "z" in have:
        index.append(lax.div(sel["z"], 2) if "z" in sel else every)
    return ref.at[tuple(index) + tail]


def lead_dims(have):
    dims = []
    if "z" in have:
        dims.append(2)
    dims += [4 for axis in "xy" if axis in have]
    if "z" in have:
        dims.append(2)
    return tuple(dims)


def dot(left, right, dims):
    return lax.dot_general(left, right, (dims, ((), ())), preferred_element_type=F32)


NN = ((1,), (0,))
NT = ((1,), (1,))
TN = ((0,), (0,))


def spread(width, offset, mod):
    lane = lax.broadcasted_iota(jnp.int32, (128, width), 0)
    return jnp.where(lane == offset + mod, 1.0, 0.0).astype(BF16)


def owned(width, div):
    row = lax.broadcasted_iota(jnp.int32, (128, width), 0)
    device = jnp.where(row < 64, 2 * row, 2 * row - 127)
    return device == div


def order_matrix(natural):
    width = natural.shape[1]
    row = lax.broadcasted_iota(jnp.int32, (width, width), 0)
    return jnp.where(row == natural, 1.0, 0.0).astype(BF16)


def unit(n):
    row = lax.broadcasted_iota(jnp.int32, (n, n), 0)
    column = lax.broadcasted_iota(jnp.int32, (n, n), 1)
    return jnp.where(row == column, 1.0, 0.0).astype(BF16)


def norm_parts(v, gain):
    scale = lax.rsqrt(jnp.mean(v * v, axis=-1, keepdims=True) + EPS)
    normed = v * scale
    return normed * gain, normed, scale


def norm_grad(v, gain, dy):
    _, normed, scale = norm_parts(v, gain)
    scaled = dy * gain
    inner = jnp.mean(scaled * normed, axis=-1, keepdims=True)
    return scale * (scaled - normed * inner), jnp.sum(dy * normed, axis=0, keepdims=True)


def turn(v, cosines, sines):
    a, b = v[:, :128], v[:, 128:]
    return jnp.concatenate([a * cosines - b * sines, b * cosines + a * sines], axis=1)


def turn_back(v, cosines, sines):
    a, b = v[:, :128], v[:, 128:]
    return jnp.concatenate([a * cosines + b * sines, b * cosines - a * sines], axis=1)


def attention_kernel(
    query_w,
    key_w,
    value_w,
    output_w,
    gate_w,
    up_w,
    down_w,
    inputs,
    gain_row,
    pairs,
    rope,
    natural,
    mod9,
    div9,
    mod2,
    div2,
    all_ffn,
    down_t,
    weights_out,
    cosines,
    sines,
    last_rows,
    gains,
    attn_p,
    qkv,
    query_low,
    keys_out,
    values_out,
    probs_out,
    mixed_out,
    attn_out,
    resid_out,
    ffn_in,
    send_sems,
    recv_sems,
    local_sems,
    weights,
    ffn,
    own8,
    own_extra,
    other8,
    other_extra,
    start,
    extras,
    key_own,
    value_own,
    keys,
    values,
):
    net = Net(send_sems, recv_sems)
    me = net.me
    sibling, mirror = net.sibling(), net.mirror()

    def prepare():
        at = 0
        for ref in (query_w, key_w, value_w, output_w):
            whole = ref[...].astype(F32)
            wide = whole.shape[1]
            own8[:, at : at + wide] = whole[:8]
            if whole.shape[0] > 8:
                for j in range(wide // 128):
                    row = at // 128 + j
                    own_extra[row : row + 1, :] = whole[8:, j * 128 : (j + 1) * 128]
            at += wide
        own_extra[GAIN_ROW : GAIN_ROW + 1, :] = gain_row[...]
        own_extra[GAIN_ROW + 1 :, :] = jnp.zeros((EXTRA - GAIN_ROW - 1, 128), F32)
        share = gate_w.shape[0]
        ffn[0:share] = gate_w[...]
        ffn[share : 2 * share] = up_w[...]
        down_t[...] = dot(unit(down_w.shape[1]), down_w[...], NT).astype(BF16)

    net.barrier(
        [net.neighbour(axis, by) for axis in "xyz" for by in (1, 3)] + [sibling], prepare
    )
    core, x_at, low = me["core"], me["x"], lax.rem(me["z"], 2)
    swap8 = net.send(own8, other8, sibling)
    swap_extra = net.send(own_extra, other_extra, sibling)
    own_ffn = pltpu.make_async_copy(ffn, all_ffn.at[me["z"], x_at], local_sems.at[0])
    own_ffn.start()
    forwards = []

    def piece(p, h):
        return pl.ds(p * PIECE + h * (PIECE // 2), PIECE // 2)

    every = slice(None)

    def blob_task(order, p):
        both = pl.ds(p * PIECE, PIECE)
        held = weights.at[core]
        for count, axis in enumerate(order):
            fixed = {k: me[k] for k in order[count + 1 :]}

            def place(k, h):
                return grid_at(held, "xyz", {**fixed, axis: k}, (every, piece(p, h)))

            def own(h):
                if count == 0:
                    return start.at[:, piece(p, h)]
                return place(me[axis], h)

            def forward(k):
                ref = grid_at(held, "xyz", {**fixed, axis: k}, (every, both))
                forwards.append(net.send(ref, ref, sibling))

            if count == 2:
                forward(me[axis])
            yield from gather_ring(net, axis, own, place, forward if count == 2 else None)
            yield

    def ffn_rings(axes, source):
        rings = []
        for axis, rows in zip(axes, GATHER_ROWS):
            other = "z" if axis == "x" else "x"
            fixed = me[other] if source is ffn else every

            def spot(k, h, axis=axis, rows=rows, fixed=fixed):
                ix, iz = (k, fixed) if axis == "x" else (fixed, k)
                return all_ffn.at[iz, ix, pl.ds(*rows[h])]

            def own(h, axis=axis, rows=rows, spot=spot):
                return ffn.at[pl.ds(*rows[h])] if source is ffn else spot(me[axis], h)

            rings.append(GatherRing(net, axis, own, spot))
        return rings

    def ffn_task():
        first = ffn_rings("xz", ffn)
        for ring in first:
            ring.start()
        for _ in range(TURNS[0]):
            yield
        for ring in first:
            ring.pass_on()
        for _ in range(TURNS[1]):
            yield
        for ring in first:
            ring.finish()
        own_ffn.wait()
        second = ffn_rings("zx", None)
        for ring in second:
            ring.start()
        for _ in range(TURNS[2]):
            yield
        for ring in second:
            ring.pass_on()
        yield
        for ring in second:
            ring.finish()

    swap8.wait_recv()
    swap_extra.wait_recv()
    first = core == 0
    mine8, theirs8 = own8[...], other8[...]
    chip = jnp.concatenate(
        [jnp.where(first, mine8, theirs8), jnp.where(first, theirs8, mine8)], axis=0
    )
    mine_x, theirs_x = own_extra[...], other_extra[...]
    half1 = jnp.concatenate(
        [
            chip[:, WIRE:],
            jnp.where(first, mine_x, theirs_x),
            jnp.where(first, theirs_x, mine_x),
            jnp.zeros((16, 2 * WIRE - chip.shape[1] - 256), F32),
        ],
        axis=1,
    )
    block = jnp.where(first, chip[:, :WIRE], half1).astype(BF16)
    start[...] = block
    weights[core, low, x_at, me["y"], lax.div(me["z"], 2)] = block

    background = ffn_task()
    blob_tasks = [blob_task(order, p) for p, order in enumerate(GATHER_ORDERS)]
    for turn_ in range(18):
        for task in blob_tasks:
            next(task)
        next(background)
    for task in blob_tasks:
        next(task, None)
    order = order_matrix(natural[...])
    for copy in forwards:
        copy.wait_recv()
    save = pltpu.make_async_copy(weights, weights_out, local_sems.at[1])
    save.start()
    for c in range(2):
        extras[c * 1024 : (c + 1) * 1024] = (
            weights[1, :, :, :, :, :, 1152 + c * 128 : 1280 + c * 128]
            .reshape(1024, 128)
            .astype(F32)
        )

    def extra_row(j):
        return extras[pl.ds(j, 128, stride=EXTRA), :].astype(BF16)

    for j in range(12):
        last_rows[:, j * 128 : (j + 1) * 128] = extra_row(j)
    packed = extra_row(GAIN_ROW)

    def unpack(offset, mod, div):
        wide = dot(packed, spread(mod.shape[1], offset, mod), NN)
        return jnp.sum(jnp.where(owned(mod.shape[1], div), wide, 0.0), axis=0, keepdims=True)

    gains[...] = jnp.zeros(gains.shape, F32)
    gain_in = unpack(0, mod9[...], div9[...])
    gain_query = unpack(9, mod2[...], div2[...])
    gain_key = unpack(11, mod2[...], div2[...])
    gain_mixed = unpack(13, mod9[...], div9[...])
    gain_ffn = unpack(22, mod9[...], div9[...])
    gain_branch = unpack(31, mod9[...], div9[...])
    gains[0:1, :] = gain_in
    gains[1:2, :] = gain_mixed
    gains[2:3, :] = gain_ffn
    gains[3:4, :] = gain_branch
    gains[4:5, 0:256] = gain_query
    gains[5:6, 0:256] = gain_key

    hidden_in = inputs[...].astype(F32)
    attn_in = norm_parts(hidden_in, gain_in)[0].astype(BF16)
    permuted = dot(attn_in, order, NN).astype(BF16)
    attn_p[...] = permuted
    block = pairs[0, lax.axis_index("ctx")]
    index = lax.broadcasted_iota(jnp.int32, (16, 128), 0)
    cos_, sin_ = [], []
    for b in (block, 15 - block):
        cb, sb = (
            jnp.sum(jnp.where(index == b, rope[i, 64:80, :], 0.0), axis=0, keepdims=True)
            for i in range(2)
        )
        cj, sj = rope[0, 0:64, :], rope[1, 0:64, :]
        cos_.append(cj * cb - sj * sb)
        sin_.append(sj * cb + cj * sb)
    cos_, sin_ = jnp.concatenate(cos_, axis=0), jnp.concatenate(sin_, axis=0)
    cosines[...] = cos_
    sines[...] = sin_

    def project(low_col, width):
        cols = slice(low_col, low_col + width)
        main = weights[0, :, :, :, :, :, cols].reshape(1024, width)
        out = dot(permuted[:, :1024], main, NN) + dot(permuted[:, 1024:], last_rows[:, cols], NN)
        qkv[:, cols] = out
        return out

    raw = project(1024, 512)
    key_own[...] = turn(norm_parts(raw[:, :256], gain_key)[0], cos_, sin_).astype(BF16)
    value_own[...] = raw[:, 256:].astype(BF16)
    keys[low, x_at] = key_own[...]
    values[low, x_at] = value_own[...]
    half = key_own.shape[0] // 2

    def cut(h):
        return pl.ds(h * half, half)

    def key_task():
        swap = net.send(key_own, keys.at[low, x_at], mirror)
        yield
        swap.wait_recv()
        yield from gather_ring(
            net, "x", lambda h: keys.at[:, x_at, cut(h)], lambda k, h: keys.at[:, k, cut(h)]
        )

    def value_task():
        yield from gather_ring(
            net, "x", lambda h: value_own.at[cut(h)], lambda k, h: values.at[low, k, cut(h)]
        )
        swap = net.send(values.at[low], values.at[low], mirror)
        yield
        swap.wait_recv()

    tasks = [key_task(), value_task()]
    for task in tasks:
        next(task)
    for h in range(HEADS):
        raw = project(h * 256, 256)
        query_low[:, h * 256 : (h + 1) * 256] = turn(
            norm_parts(raw, gain_query)[0], cos_, sin_
        ).astype(BF16)
    next(background)
    interleave(*tasks)
    key_all = keys[...].reshape(1024, 256)
    value_all = values[...].reshape(1024, 256)
    keys_out[...] = key_all
    values_out[...] = value_all

    def position(i, b):
        return jnp.where(i < 64, b * 64 + i, (15 - b) * 64 + i - 64)

    lane = lax.broadcasted_iota(jnp.int32, (1, 128), 1)
    all_pos = jnp.concatenate([position(lane, pairs[0, c]) for c in range(8)], axis=1)
    own_pos = position(lax.broadcasted_iota(jnp.int32, (128, 1), 0), block)
    allowed = all_pos <= own_pos
    for h in range(HEADS):
        scores = dot(query_low[:, h * 256 : (h + 1) * 256], key_all, NT) * SCALE
        scores = jnp.where(allowed, scores, MASKED)
        expo = jnp.exp(scores - jnp.max(scores, axis=-1, keepdims=True))
        probs = expo / jnp.sum(expo, axis=-1, keepdims=True)
        probs_out[h] = probs
        mixed_out[:, h * 256 : (h + 1) * 256] = dot(probs.astype(BF16), value_all, NN).astype(BF16)
    out_weight = weights[1, :, :, :, :, :, 0:1152].reshape(1024, 1152)
    mixed_by = dot(mixed_out[...], out_weight, NN)
    attn_out[...] = mixed_by
    resid = hidden_in + norm_parts(mixed_by, gain_mixed)[0]
    resid_out[...] = resid
    ffn_in[...] = norm_parts(resid, gain_ffn)[0].astype(BF16)
    next(background, None)
    save.wait()
    net.send_done()


def attention(projections, ffn, inputs, gain_row, pairs, rope, tables):
    rows, width = inputs.shape
    vmem, any_ = pltpu.VMEM, pl.ANY
    shape = jax.ShapeDtypeStruct
    wire = (2, 2, 4, 4, 2, 16, WIRE)
    return call(
        attention_kernel,
        "attention",
        [
            shape((4, 4, 2 * ffn[0].shape[0], ffn[0].shape[1]), BF16),
            shape(ffn[0].shape, BF16),
            shape(wire, BF16),
            shape((rows, 128), F32),
            shape((rows, 128), F32),
            shape((128, WIRE), BF16),
            shape((8, width), F32),
            shape((rows, width), BF16),
            shape((rows, WIRE), F32),
            shape((rows, 1024), BF16),
            shape((1024, 256), BF16),
            shape((1024, 256), BF16),
            shape((HEADS, rows, 1024), F32),
            shape((rows, 1024), BF16),
            shape((rows, width), F32),
            shape((rows, width), F32),
            shape((rows, width), BF16),
        ],
        [vmem] * 9 + [pltpu.SMEM] + [vmem] * 6,
        [any_, vmem, any_] + [vmem] * 14,
        sems(2 + 3 * 22 + 24 + 14)
        + [pltpu.SemaphoreType.DMA((2,))]
        + [
            vmem(wire, BF16),
            vmem((2 * ffn[0].shape[0], ffn[0].shape[1]), BF16),
            vmem((8, WIRE + width), F32),
            vmem((EXTRA, 128), F32),
            vmem((8, WIRE + width), F32),
            vmem((EXTRA, 128), F32),
            vmem((16, WIRE), BF16),
            vmem((2048, 128), F32),
            vmem((rows, 256), BF16),
            vmem((rows, 256), BF16),
            vmem((2, 4, rows, 256), BF16),
            vmem((2, 4, rows, 256), BF16),
        ],
        1,
    )(*projections, *ffn, inputs, gain_row, pairs, rope, *tables)


class Cut:
    def __init__(self, ref, rows):
        self.ref, self.rows = ref, rows

    @property
    def at(self):
        return self

    def __getitem__(self, h):
        ref = self.ref.at[h]
        lead = (slice(None),) * (len(ref.shape) - 2)
        return ref.at[lead + (pl.ds(0, self.rows[h][1]),)]

    def __setitem__(self, h, value):
        self[h][...] = value


def backward_kernel(
    ffn_in_grad,
    cotangent,
    inputs,
    resid,
    attn_out,
    gains,
    weights,
    last_rows,
    attn_p,
    qkv,
    query_low,
    keys,
    values,
    probs,
    mixed,
    cosines,
    sines,
    ffn,
    branch_gain_grad,
    natural,
    mod9,
    div9,
    mod2,
    div2,
    inputs_grad,
    main_out,
    extra_out,
    ffn_out,
    send_sems,
    recv_sems,
    wire,
    paired,
    extras,
    final,
    glow,
    key_sum,
    value_sum,
    key_grads,
    value_grads,
    key_sent,
    key_pair,
    value_pair,
    *bufs,
):
    net = Net(send_sems, recv_sems)
    me = net.me
    sibling, mirror = net.sibling(), net.mirror()
    net.barrier(
        [net.neighbour(axis, by) for axis in "xyz" for by in (1, 3)] + [sibling]
    )
    core, low = me["core"], lax.rem(me["z"], 2)
    every = slice(None)
    bufs = list(bufs)

    def take(n):
        got = bufs[:n]
        del bufs[:n]
        return got

    def ffn_task():
        plans = []
        for axis, rows in zip("xz", FFN_ROWS):
            bufs1, result, bufs2 = take(4), take(1)[0], take(4)
            start = rows[0][0]

            def part(k, h, axis=axis, rows=rows):
                if axis == "x":
                    return ffn.at[:, k, pl.ds(*rows[h])]
                return ffn.at[k, :, pl.ds(*rows[h])]

            def part2(k, h, rows=rows, result=result, start=start):
                return result.at[k, pl.ds(rows[h][0] - start, rows[h][1])]

            ring = SumRing(net, axis, part, [Cut(b, rows) for b in bufs1])
            plans.append((ring, rows, result, part2, bufs2, start))
        for ring, *_ in plans:
            ring.send_all()
        yield
        for ring, *_ in plans:
            ring.pass_on()
        yield
        rings = []
        for (ring, rows, result, part2, bufs2, start), axis in zip(plans, "zx"):
            for h in range(2):
                result[:, pl.ds(rows[h][0] - start, rows[h][1])] = ring.total(h).astype(BF16)
            ring2 = SumRing(net, axis, part2, [Cut(b, rows) for b in bufs2])
            ring2.send_all()
            rings.append(ring2)
        for _ in range(7):
            yield
        for ring in rings:
            ring.pass_on()
        for _ in range(6):
            yield
        for ring, rows in zip(rings, FFN_ROWS):
            for h in range(2):
                ffn_out[pl.ds(*rows[h])] = ring.total(h)

    background = ffn_task()
    next(background)
    gain_in, gain_mixed, gain_ffn = gains[0:1, :], gains[1:2, :], gains[2:3, :]
    gain_query, gain_key = gains[4:5, 0:256], gains[5:6, 0:256]
    cos_, sin_ = cosines[...], sines[...]

    resid_dv, ffn_gain_grad = norm_grad(resid[...], gain_ffn, ffn_in_grad[...])
    resid_grad = cotangent[...].astype(F32) + resid_dv
    inputs_grad[...] = resid_grad
    attn_dv, mixed_gain_grad = norm_grad(attn_out[...], gain_mixed, resid_grad)
    attn_grad = attn_dv.astype(BF16)
    out_weight = weights[1, :, :, :, :, :, 0:1152].reshape(1024, 1152)
    mixed_grad = dot(attn_grad, out_weight, NT).astype(BF16)
    key_all, value_all = keys[...], values[...]
    query_gain_grad = jnp.zeros((1, 256), F32)
    for h in range(HEADS):
        cols = slice(h * 256, (h + 1) * 256)
        mine = mixed_grad[:, cols]
        prob = probs[h]
        prob_grad = dot(mine, value_all, NT)
        delta = jnp.sum(prob_grad * prob, axis=-1, keepdims=True)
        score_grad = (prob * (prob_grad - delta)).astype(BF16)
        value_part = dot(prob.astype(BF16), mine, TN)
        key_part = dot(score_grad, query_low[:, cols], TN)
        if h == 0:
            value_sum[...] = value_part
            key_sum[...] = key_part
        else:
            value_sum[...] += value_part
            key_sum[...] += key_part
        rot_grad = dot(score_grad, key_all, NN) * SCALE
        raw_grad, gain_part = norm_grad(qkv[:, cols], gain_query, turn_back(rot_grad, cos_, sin_))
        query_gain_grad = query_gain_grad + gain_part
        glow[:, cols] = raw_grad.astype(BF16)
    rows = glow.shape[0]
    key_grads[...] = (key_sum[...] * SCALE).astype(BF16).reshape(2, 4, rows, 256)
    value_grads[...] = value_sum[...].astype(BF16).reshape(2, 4, rows, 256)
    half = rows // 2

    def cut(h):
        return pl.ds(h * half, half)

    done = {}

    def key_task():
        ring = take(4)

        def total(h, terms):
            key_sent[:, cut(h)] = add_up(terms).astype(BF16)

        yield from scatter_ring(net, "x", lambda k, h: key_grads.at[:, k, cut(h)], ring, total)
        swap = net.send(key_sent.at[1 - low], key_pair, mirror)
        yield
        swap.wait_recv()
        done["key"] = add_up((key_sent.at[low], key_pair))

    def value_task():
        ring = take(4)
        swap = net.send(value_grads.at[1 - low], value_pair, mirror)
        yield
        swap.wait_recv()
        value_pair[...] = add_up((value_pair, value_grads.at[low])).astype(BF16)
        sums = [None, None]

        def total(h, terms):
            sums[h] = add_up(terms)

        yield from scatter_ring(net, "x", lambda k, h: value_pair.at[k, cut(h)], ring, total)
        done["value"] = jnp.concatenate(sums, axis=0)

    tasks = [key_task(), value_task()]
    for task in tasks:
        next(task)
    for c in range(3):
        cols = slice(c * 384, (c + 1) * 384)
        wire[1, :, :, :, :, :, cols] = (
            dot(mixed[...], attn_grad[:, cols], TN).astype(BF16).reshape(2, 4, 4, 2, 16, 384)
        )
    interleave(*tasks)
    next(background)

    def weight_grad(low_col, width):
        cols = slice(low_col, low_col + width)
        out = dot(attn_p[...], glow[:, cols], TN)
        wire[0, :, :, :, :, :, cols] = out[:1024].astype(BF16).reshape(2, 4, 4, 2, 16, width)
        for j in range(low_col // 128, (low_col + width) // 128):
            extras[pl.ds(j, 128, stride=EXTRA), :] = out[
                1024:, j * 128 - low_col : (j + 1) * 128 - low_col
            ]

    extras[...] = jnp.zeros(extras.shape, F32)
    weight_grad(0, 512)
    weight_grad(512, 512)
    key_raw_grad, key_gain_grad = norm_grad(
        qkv[:, 1024:1280], gain_key, turn_back(done["key"], cos_, sin_)
    )
    glow[:, 1024:1280] = key_raw_grad.astype(BF16)
    glow[:, 1280:1536] = done["value"].astype(BF16)
    weight_grad(1024, 512)
    main = weights[0].reshape(1024, WIRE)
    grad_p = jnp.concatenate(
        [dot(glow[...], main, NT), dot(glow[...], last_rows[...], NT)], axis=1
    )
    order = order_matrix(natural[...])
    high_part = grad_p.astype(BF16)
    low_part = (grad_p - high_part.astype(F32)).astype(BF16)
    attn_in_grad = dot(high_part, order, NT) + dot(low_part, order, NT)
    input_dv, in_gain_grad = norm_grad(inputs[...].astype(F32), gain_in, attn_in_grad)
    inputs_grad[...] += input_dv

    def pack(grad, offset, mod, div):
        width = mod.shape[1]
        placed = jnp.where(owned(width, div), grad, 0.0).astype(BF16)
        return dot(placed, spread(width, offset, mod), NT)

    packed = (
        pack(in_gain_grad, 0, mod9[...], div9[...])
        + pack(query_gain_grad, 9, mod2[...], div2[...])
        + pack(key_gain_grad, 11, mod2[...], div2[...])
        + pack(mixed_gain_grad, 13, mod9[...], div9[...])
        + pack(ffn_gain_grad, 22, mod9[...], div9[...])
        + pack(branch_gain_grad[...], 31, mod9[...], div9[...])
    )
    extras[pl.ds(GAIN_ROW, 128, stride=EXTRA), :] = packed
    for c in range(2):
        wire[1, :, :, :, :, :, 1152 + c * 128 : 1280 + c * 128] = (
            extras[c * 1024 : (c + 1) * 1024].astype(BF16).reshape(2, 4, 4, 2, 16, 128)
        )
    wire[1, :, :, :, :, :, 1408:1536] = jnp.zeros((2, 4, 4, 2, 16, 128), BF16)

    copies = []
    for p in range(3):
        cols = pl.ds(p * PIECE, PIECE)
        copies.append(
            net.send(
                wire.at[1 - core, :, :, :, :, :, cols], paired.at[:, :, :, :, :, cols], sibling
            )
        )

    def blob_task(order, p, copy):
        own_bufs = take(14)
        yield
        copy.wait_recv()
        cols = pl.ds(p * PIECE, PIECE)
        for a in range(2):
            for b in range(4):
                paired[a, b, :, :, :, cols] = add_up(
                    (paired.at[a, b, :, :, :, cols], wire.at[core, a, b, :, :, :, cols])
                ).astype(BF16)
        source, offset = paired, p * PIECE
        for count, axis in enumerate(order):
            have = order[count:]
            result = own_bufs[4] if count < 2 else None

            def part(k, h, source=source, offset=offset, have=have, axis=axis):
                return grid_at(
                    source, have, {axis: k}, (every, pl.ds(offset + h * (PIECE // 2), PIECE // 2))
                )

            def total(h, terms, result=result, count=count, have=have):
                if count < 2:
                    grid_at(
                        result, have[1:], {}, (every, pl.ds(h * (PIECE // 2), PIECE // 2))
                    )[...] = add_up(terms).astype(BF16)
                else:
                    final[core, :, pl.ds(p * PIECE + h * (PIECE // 2), PIECE // 2)] = add_up(terms)

            yield from scatter_ring(net, axis, part, own_bufs[:4], total)
            yield
            source, offset = result, 0
            own_bufs = own_bufs[5:]

    interleave(background, *(blob_task(order, p, copies[p]) for p, order in enumerate(SUM_ORDERS)))
    swap = net.send(final.at[core], final.at[core], sibling)
    swap.wait_recv()
    mine8 = pl.ds(pl.multiple_of(core * 8, 8), 8)
    main_out[:, 0:WIRE] = final[0, mine8, :]
    main_out[:, WIRE:] = final[1, mine8, 0:1152]
    extra_out[...] = jnp.where(core == 0, final[1, :, 1152:1280], final[1, :, 1280:1408])
    net.send_done()


def results_kernel(
    out_in,
    inputs_grad_in,
    main,
    extra,
    ffn,
    out,
    inputs_grad,
    gains_out,
    query_out,
    key_out,
    value_out,
    output_out,
    gate_out,
    up_out,
    down_out,
):
    out[...] = out_in[...]
    inputs_grad[...] = inputs_grad_in[...]
    at = 0
    for ref in (query_out, key_out, value_out):
        wide = ref.shape[1]
        ref[0:8, :] = main[:, at : at + wide]
        for j in range(wide // 128):
            row = at // 128 + j
            ref[8:9, j * 128 : (j + 1) * 128] = extra[row : row + 1]
        at += wide
    output_out[...] = main[:, WIRE:]
    gains_out[...] = extra[GAIN_ROW : GAIN_ROW + 1]
    share = gate_out.shape[0]
    gate_out[...] = ffn[0:share]
    up_out[...] = ffn[share : 2 * share]
    down = ffn[2 * share :]
    exact = unit(down.shape[1])
    high_part = down.astype(BF16)
    low_part = (down - high_part.astype(F32)).astype(BF16)
    down_out[...] = dot(exact, high_part, NT) + dot(exact, low_part, NT)


def results(out, inputs_grad, main, extra, ffn):
    shape = jax.ShapeDtypeStruct
    width = out.shape[1]
    share, wide = ffn.shape[0] // 3, ffn.shape[1]
    shapes = (
        [out.shape, out.shape, (1, 128), (9, 1024), (9, 256), (9, 256), (8, width)]
        + [(share, wide)] * 2
        + [(wide, share)]
    )
    vmem = pltpu.VMEM
    return pl.pallas_call(
        results_kernel,
        name="results",
        out_shape=[shape(s, F32) for s in shapes],
        in_specs=[pl.BlockSpec(memory_space=vmem)] * 5,
        out_specs=[pl.BlockSpec(memory_space=vmem)] * 10,
        compiler_params=pltpu.CompilerParams(vmem_limit_bytes=VMEM_BYTES),
    )(out, inputs_grad, main, extra, ffn)


def attention_backward(args, ffn, tables):
    vmem = pltpu.VMEM
    shape = jax.ShapeDtypeStruct
    rows, width = args[0].shape
    wide = ffn.shape[-1]
    scratch = sems(24 + 14 + 3 * 19 + 1) + [
        vmem((2, 2, 4, 4, 2, 16, WIRE), BF16),
        vmem((2, 4, 4, 2, 16, WIRE), BF16),
        vmem((2048, 128), F32),
        vmem((2, 16, WIRE), F32),
        vmem((rows, WIRE), BF16),
        vmem((1024, 256), F32),
        vmem((1024, 256), F32),
        vmem((2, 4, rows, 256), BF16),
        vmem((2, 4, rows, 256), BF16),
        vmem((2, rows, 256), BF16),
        vmem((rows, 256), BF16),
        vmem((4, rows, 256), BF16),
    ]
    for own in FFN_ROWS:
        most = max(own[0][1], own[1][1])
        every = own[0][1] + own[1][1]
        scratch += [vmem((2, 4, most, wide), BF16)] * 4
        scratch.append(vmem((4, every, wide), BF16))
        scratch += [vmem((2, most, wide), BF16)] * 4
    scratch += [vmem((2, 2, rows // 2, 256), BF16)] * 4
    scratch += [vmem((2, rows // 2, 256), BF16)] * 4
    for order in SUM_ORDERS:
        for count in range(3):
            left = lead_dims(order[count + 1 :])
            scratch += [vmem((2,) + left + (16, PIECE // 2), BF16)] * 4
            if count < 2:
                scratch.append(vmem(left + (16, PIECE), BF16))
    return call(
        backward_kernel,
        "attention_backward",
        [
            shape((rows, width), F32),
            shape((8, WIRE + width), F32),
            shape((EXTRA, 128), F32),
            shape(ffn.shape[2:], F32),
        ],
        [vmem] * 24,
        [vmem] * 4,
        scratch,
        2,
    )(*args, *tables)


class GatherRing:
    def __init__(self, net, axis, own, place):
        self.net, self.own, self.place = net, own, place
        self.mine = net.me[axis]
        self.left, self.right, self.far = (net.step(axis, by) for by in (3, 1, 2))
        self.to_left, self.to_right = net.neighbour(axis, 3), net.neighbour(axis, 1)

    def start(self):
        send, own, place, mine = self.net.send, self.own, self.place, self.mine
        self.r0 = send(own(0), place(mine, 0), self.to_right)
        self.l1 = send(own(1), place(mine, 1), self.to_left)
        self.r1 = send(own(1), place(mine, 1), self.to_right)
        self.l0 = send(own(0), place(mine, 0), self.to_left)

    def pass_on(self):
        send, place = self.net.send, self.place
        self.r0.wait_recv()
        self.f0 = send(place(self.left, 0), place(self.left, 0), self.to_right)
        self.l1.wait_recv()
        self.f1 = send(place(self.right, 1), place(self.right, 1), self.to_left)

    def finish(self):
        self.r1.wait_recv()
        self.l0.wait_recv()
        self.wait_far()

    def wait_far(self):
        self.f0.wait_recv()
        self.f1.wait_recv()


class SumRing:
    def __init__(self, net, axis, part, bufs):
        self.net, self.part = net, part
        self.mine = net.me[axis]
        self.left, self.right, self.far = (net.step(axis, by) for by in (3, 1, 2))
        self.to_left, self.to_right = net.neighbour(axis, 3), net.neighbour(axis, 1)
        self.from_left, self.from_right, self.hold, self.stage = bufs

    def send_all(self):
        self.send_far()
        self.send_right()
        self.send_left()

    def send_far(self):
        self.a0 = self.net.send(self.part(self.far, 0), self.hold.at[0], self.to_right)
        self.a1 = self.net.send(self.part(self.far, 1), self.hold.at[1], self.to_left)

    def send_right(self):
        self.r1 = self.net.send(self.part(self.right, 1), self.from_left.at[1], self.to_right)

    def send_left(self):
        self.l0 = self.net.send(self.part(self.left, 0), self.from_right.at[0], self.to_left)

    def pass_on(self):
        self.a0.wait_recv()
        self.stage[0] = add_up((self.part(self.right, 0), self.hold.at[0])).astype(BF16)
        self.r0 = self.net.send(self.stage.at[0], self.from_left.at[0], self.to_right)
        self.a1.wait_recv()
        self.stage[1] = add_up((self.part(self.left, 1), self.hold.at[1])).astype(BF16)
        self.l1 = self.net.send(self.stage.at[1], self.from_right.at[1], self.to_left)

    def total(self, h):
        if h == 0:
            self.l0.wait_recv()
            self.r0.wait_recv()
        else:
            self.r1.wait_recv()
            self.l1.wait_recv()
        return add_up((self.part(self.mine, h), self.from_left.at[h], self.from_right.at[h]))


def gelu_parts(u):
    root = 0.7978845608028654
    square = u * u
    th = jnp.tanh(root * u * (1.0 + 0.044715 * square))
    half = 0.5 * (1.0 + th)
    slope = half + 0.5 * u * (1.0 - th * th) * (root * (1.0 + 3 * 0.044715 * square))
    return u * half, slope


def ffn_kernel(
    own,
    all_ffn,
    down_t,
    resid,
    cotangent,
    gain,
    outputs,
    back,
    gain_grad,
    weight_grads,
    send_sems,
    recv_sems,
    local_sems,
    weights,
    tokens,
    grads,
    act,
    slope,
    hidden,
    gate_g,
    up_g,
    branch,
    *bufs,
):
    net = Net(send_sems, recv_sems)
    me = net.me
    sibling = net.sibling()
    share = down_t.shape[0]
    loads = [
        pltpu.make_async_copy(
            all_ffn.at[:, :, pl.ds(m * share, share)], weights.at[m], local_sems.at[m]
        )
        for m in range(2)
    ]
    for load in loads:
        load.start()
    net.barrier([net.neighbour(axis, by) for axis in "xyz" for by in (1, 3)] + [sibling])
    core, y = me["core"], me["y"]
    rows, width = own.shape

    def down_rings(axes, first):
        rings = []
        for axis, cuts in zip(axes, DOWN_ROWS):
            fixed = me["z" if axis == "x" else "x"] if first else slice(None)

            def spot(k, h, axis=axis, cuts=cuts, fixed=fixed):
                ix, iz = (k, fixed) if axis == "x" else (fixed, k)
                return weights.at[2, iz, ix, pl.ds(*cuts[h])]

            def give(h, axis=axis, cuts=cuts, spot=spot):
                return down_t.at[pl.ds(*cuts[h])] if first else spot(me[axis], h)

            rings.append(GatherRing(net, axis, give, spot))
        return rings

    def weight(m, j):
        return weights[m, 2 * j : 2 * j + 2].reshape(width, weights.shape[-1])
    half = rows // 2

    def cut(h):
        return pl.ds(h * half, half)

    def phase(source, held, run, bufs, meanwhile):
        parts, paired, ring_bufs = bufs[0], bufs[1], bufs[2:]
        gather = GatherRing(
            net, "y", lambda h: source.at[cut(h)], lambda k, h: held.at[k, core, cut(h)]
        )
        gather.start()
        swap = net.send(source, held.at[y, core], sibling)
        held[y, core] = source[...]
        left, right, far = gather.left, gather.right, gather.far

        def across(k):
            return net.send(held.at[k, core], held.at[k, core], sibling)

        def give(k):
            return net.send(parts.at[k, 1 - core], paired.at[k], sibling)

        def pair(k, copy):
            copy.wait_recv()
            paired[k] = add_up((paired.at[k], parts.at[k, core])).astype(BF16)

        sums = SumRing(net, "y", lambda k, h: paired.at[k, cut(h)], ring_bufs)
        swap.wait_recv()
        parts[y] = run(y)
        pair_own = give(y)
        gather.pass_on()
        gather.r1.wait_recv()
        swap_left = across(left)
        gather.l0.wait_recv()
        swap_right = across(right)
        swap_left.wait_recv()
        parts[left] = run(left)
        pair_left = give(left)
        gather.wait_far()
        swap_far = across(far)
        pair(y, pair_own)
        swap_right.wait_recv()
        parts[right] = run(right)
        pair_right = give(right)
        pair(left, pair_left)
        sums.send_left()
        swap_far.wait_recv()
        parts[far] = run(far)
        pair_far = give(far)
        pair(right, pair_right)
        sums.send_right()
        pair(far, pair_far)
        sums.send_far()
        meanwhile(0)
        sums.pass_on()
        meanwhile(1)
        return sums

    def dot(left, right, dims):
        return lax.dot_general(left, right, (dims, ((), ())), preferred_element_type=F32)

    def front(k):
        rows_k = tokens[k].reshape(2 * rows, width)
        for j in range(2):
            gate = dot(rows_k, weight(0, j), ((1,), (0,)))
            upper = dot(rows_k, weight(1, j), ((1,), (0,)))
            value, diff = gelu_parts(gate)
            act[k, j] = value.astype(BF16)
            slope[k, j] = (diff * upper).astype(BF16)
            hidden[k, j] = (value * upper).astype(BF16)

    def rear(k):
        total = dot(hidden[k, 0], weight(2, 0), ((1,), (1,))) + dot(
            hidden[k, 1], weight(2, 1), ((1,), (1,))
        )
        return total.astype(BF16).reshape(2, rows, width)

    def forward_phase(source, held, bufs):
        parts, paired, ring_bufs = bufs[0], bufs[1], bufs[2:]
        gather = GatherRing(
            net, "y", lambda h: source.at[cut(h)], lambda k, h: held.at[k, core, cut(h)]
        )
        gather.start()
        swap = net.send(source, held.at[y, core], sibling)
        first = down_rings("xz", True)
        for ring in first:
            ring.start()
        held[y, core] = source[...]
        weights[2, me["z"], me["x"]] = down_t[...]
        left, right, far = gather.left, gather.right, gather.far

        def across(k):
            return net.send(held.at[k, core], held.at[k, core], sibling)

        def give(k):
            return net.send(parts.at[k, 1 - core], paired.at[k], sibling)

        def pair(k, copy):
            copy.wait_recv()
            paired[k] = add_up((paired.at[k], parts.at[k, core])).astype(BF16)

        sums = SumRing(net, "y", lambda k, h: paired.at[k, cut(h)], ring_bufs)
        swap.wait_recv()
        for load in loads:
            load.wait()
        front(y)
        gather.pass_on()
        for ring in first:
            ring.pass_on()
        gather.r1.wait_recv()
        swap_left = across(left)
        gather.l0.wait_recv()
        swap_right = across(right)
        swap_left.wait_recv()
        front(left)
        gather.wait_far()
        swap_far = across(far)
        for ring in first:
            ring.finish()
        second = down_rings("zx", False)
        for ring in second:
            ring.start()
        swap_right.wait_recv()
        front(right)
        swap_far.wait_recv()
        for ring in second:
            ring.pass_on()
        front(far)
        for ring in second:
            ring.finish()
        parts[far] = rear(far)
        pair_far = give(far)
        parts[right] = rear(right)
        pair_right = give(right)
        pair(far, pair_far)
        sums.send_far()
        parts[left] = rear(left)
        pair_left = give(left)
        pair(right, pair_right)
        sums.send_right()
        parts[y] = rear(y)
        pair_own = give(y)
        pair(left, pair_left)
        sums.send_left()
        sums.pass_on()
        pair(y, pair_own)
        return sums

    def backward(k):
        rows_k = grads[k].reshape(2 * rows, width)
        total = None
        for j in range(2):
            hidden_grad = dot(rows_k, weight(2, j), ((1,), (0,)))
            gate_low = (hidden_grad * slope[k, j].astype(F32)).astype(BF16)
            up_low = (hidden_grad * act[k, j].astype(F32)).astype(BF16)
            gate_g[k, j] = gate_low
            up_g[k, j] = up_low
            out = dot(gate_low, weight(0, j), ((1,), (1,))) + dot(
                up_low, weight(1, j), ((1,), (1,))
            )
            total = out if total is None else total + out
        return total.astype(BF16).reshape(2, rows, width)

    def weight_grad(which, held, factor):
        flat = held[...].reshape(8 * rows, width)
        for j in range(2):
            out = dot(flat, factor[:, j].reshape(8 * rows, factor.shape[-1]), ((0,), (0,)))
            weight_grads[2 * j : 2 * j + 2, :, which * share : (which + 1) * share] = out.astype(
                BF16
            ).reshape(2, 4, share, out.shape[-1])

    sums = forward_phase(own, tokens, bufs[:6])
    gain_f = gain[3:4, :]
    gain_total = jnp.zeros_like(gain_f)
    for h in range(2):
        raw = sums.total(h)
        upstream = cotangent[cut(h)].astype(F32)
        scale = lax.rsqrt(jnp.mean(raw * raw, axis=-1, keepdims=True) + EPS)
        normed = raw * scale
        outputs[cut(h)] = resid[cut(h)] + normed * gain_f
        scaled = upstream * gain_f
        gain_total = gain_total + jnp.sum(upstream * normed, axis=0, keepdims=True)
        inner = jnp.mean(scaled * normed, axis=-1, keepdims=True)
        branch[cut(h)] = (scale * (scaled - normed * inner)).astype(BF16)
    gain_grad[...] = gain_total

    def meanwhile(step):
        if step == 0:
            weight_grad(2, grads, hidden)
        else:
            weight_grad(0, tokens, gate_g)
            weight_grad(1, tokens, up_g)

    sums = phase(branch, grads, backward, bufs[6:], meanwhile)
    for h in range(2):
        back[cut(h)] = sums.total(h)
    net.send_done()


def feed_forward(own, weights, down_t, resid, cotangent, gain):
    rows, width = own.shape
    wide = weights.shape[-1]
    vmem = pltpu.VMEM
    phase_bufs = [
        pltpu.VMEM((4, 2, rows, width), BF16),
        pltpu.VMEM((4, rows, width), BF16),
    ] + [pltpu.VMEM((2, rows // 2, width), BF16)] * 4
    return call(
        ffn_kernel,
        "feed_forward",
        [
            jax.ShapeDtypeStruct((rows, width), F32),
            jax.ShapeDtypeStruct((rows, width), F32),
            jax.ShapeDtypeStruct((1, width), F32),
            jax.ShapeDtypeStruct((4, 4, 3 * down_t.shape[0], wide), BF16),
        ],
        [vmem, pl.ANY] + [vmem] * 4,
        [vmem] * 4,
        sems(64) + [pltpu.SemaphoreType.DMA((2,)), vmem((3, 4, 4) + down_t.shape, BF16)]
        + [pltpu.VMEM((4, 2, rows, width), BF16)] * 2
        + [pltpu.VMEM((4, 2, 2 * rows, wide), BF16)] * 5
        + [pltpu.VMEM((rows, width), BF16)]
        + phase_bufs * 2,
        5,
    )(own, weights, down_t, resid, cotangent, gain)


def body(
    inputs,
    pair_order,
    attn_gain,
    query_gain,
    key_gain,
    mixer_gain,
    ffn_gain,
    branch_gain,
    query_weight,
    key_weight,
    value_weight,
    output_weight,
    gate_weight,
    up_weight,
    down_weight,
    cotangent,
):
    gains = (attn_gain, query_gain, key_gain, mixer_gain, ffn_gain, branch_gain)
    width = inputs.shape[2]
    gain_row = 0.0
    at = 0
    for gain in gains:
        n = gain.shape[0]
        gain_row = gain_row + jnp.pad(gain.astype(F32), (at, 128 - at - n))
        at += n
    every = np.arange(width)
    last = every - 1024
    natural = np.where(
        every < 1024,
        9 * (every // 8) + every % 8,
        9 * (2 * (last % 64) + last // 64) + 8,
    )
    twos = np.arange(256)
    tables = [
        jnp.asarray(t[None].astype(np.int32))
        for t in (natural, every % 9, every // 9, twos % 2, twos // 2)
    ]
    freqs = BASE ** (-np.arange(128) / 128)
    steps = np.concatenate([np.arange(64), 64 * np.arange(16)])
    rope = steps[:, None] * freqs[None, :]
    rope = jnp.asarray(np.stack([np.cos(rope), np.sin(rope)]).astype(np.float32))
    (
        all_ffn,
        down_t,
        weights,
        cosines,
        sines,
        last_rows,
        gain_rows,
        attn_p,
        qkv,
        query_low,
        key_all,
        value_all,
        probs,
        mixed_low,
        attn_out,
        resid,
        ffn_input,
    ) = attention(
        (query_weight, key_weight, value_weight, output_weight),
        (gate_weight, up_weight, down_weight),
        inputs[0],
        gain_row[None],
        pair_order,
        rope,
        tables,
    )
    outputs, grad_ffn_input, grad_gain_branch, ffn_grads = feed_forward(
        ffn_input, all_ffn, down_t, resid, cotangent[0], gain_rows
    )
    sums = attention_backward(
        (
            grad_ffn_input,
            cotangent[0],
            inputs[0],
            resid,
            attn_out,
            gain_rows,
            weights,
            last_rows,
            attn_p,
            qkv,
            query_low,
            key_all,
            value_all,
            probs,
            mixed_low,
            cosines,
            sines,
            ffn_grads,
            grad_gain_branch,
        ),
        ffn_grads,
        tables,
    )
    outputs, inputs_grad, gain_sum, *weight_sums = results(outputs, *sums)
    gain_sums = []
    at = 0
    for gain in gains:
        gain_sums.append(gain_sum[0, at : at + gain.shape[0]])
        at += gain.shape[0]
    return (outputs[None], inputs_grad[None], *gain_sums, *weight_sums)


def solution(mesh):
    placed = (
        P("fsdp", "ctx", None),
        P("fsdp", None),
        P(("ctx", "fsdp")),
        P(("ctx", "fsdp")),
        P(("ctx", "fsdp")),
        P(("ctx", "fsdp")),
        P(("ctx", "fsdp")),
        P(("ctx", "fsdp")),
        P(("ctx", "fsdp"), None),
        P(("ctx", "fsdp"), None),
        P(("ctx", "fsdp"), None),
        P(("ctx", "fsdp"), None),
        P("ctx", "fsdp"),
        P("ctx", "fsdp"),
        P("fsdp", "ctx"),
        P("fsdp", "ctx", None),
    )
    return jax.shard_map(
        body,
        mesh=mesh,
        in_specs=placed,
        out_specs=(
            P("fsdp", "ctx", None),
            P("fsdp", "ctx", None),
            P(("ctx", "fsdp")),
            P(("ctx", "fsdp")),
            P(("ctx", "fsdp")),
            P(("ctx", "fsdp")),
            P(("ctx", "fsdp")),
            P(("ctx", "fsdp")),
            P(("ctx", "fsdp"), None),
            P(("ctx", "fsdp"), None),
            P(("ctx", "fsdp"), None),
            P(("ctx", "fsdp"), None),
            P("ctx", "fsdp"),
            P("ctx", "fsdp"),
            P("fsdp", "ctx"),
        ),
        check_vma=False,
    )
```
